512 devices in a mesh: circ: 16 (over y_hi, x), sect: 32 (over z, y_lo, core).
Axes of the slice: x: 4, y: 8 (y_hi: 4, y_lo: 2; y = y_hi * 2 + y_lo), z: 8, core: 2. Of those that a mesh axis runs over, the one named last changes fastest.
Arguments:
- strain: bfloat16 [2048, 2, 36, 4096], P('circ', None, None, 'sect'), may hold values from -6 to 6
- region: int32 [36, 4096], P(None, 'sect'), may hold values from 0 to 7
- prior_peak: float32 [36, 4096], P(None, 'sect'), may hold values from 5 to 25
- temp_prev: float32 [36, 4096], P(None, 'sect'), may hold values from 0.5 to 1.5
- conductivity: float32 [36, 4096], P(None, 'sect'), may hold values from 0.5 to 2
- loss_moduli: float32 [8, 8], replicated, may hold values from 0.02 to 0.25
- mullins_loss: float32 [8], replicated, may hold values from 0.1 to 1
- stiffness: float32 [8], replicated, may hold values from 0.5 to 4
Outputs:
- temperature: float32 [36, 4096], P(None, 'sect')
- peak: float32 [36, 4096], P(None, 'sect')
- modulus: bfloat16 [2048, 36, 4096], P('circ', None, 'sect')
The draws below stay inside these ranges and needn't reach their ends.
All inputs are finite; a program needn't handle non-finite values.
Results may differ from the reference program's by a relative error of at most 0.0023.
Values sent between devices are 32-bit elements; how exact they have to be, the bound alone decides.
No kernel may reach another device: no remote copies, remote signals or barrier semaphores. Data moves between devices by JAX's collectives and lax.ppermute only.
A program may use at most 64 MiB of HBM per device.

```python
import math
import jax
import jax.numpy as jnp
from jax import lax

SEC_DEV = 128
LAY = 36
COMP = 2
HARM = 8
NREG = 8
SWEEPS = 4
NSEC = 2048
PATH = 4096
N_CIRC = 16


def touch_ends(result, rng, smallest, top_value):
    spot = [jax.random.randint(jax.random.fold_in(rng, axis), (), 0, length) for axis, length in enumerate(result.shape)]
    longest = result.shape.index(max(result.shape))
    next_to = spot[:longest] + [(spot[longest] + 1) % result.shape[longest]] + spot[longest + 1:]
    return result.at[tuple(spot)].set(smallest).at[tuple(next_to)].set(top_value)


def block_scale(key, dims, split, smallest, top_value):
    loudness, own = 1.0, jax.random.fold_in(key, 6)
    for axis_at, blocks in split:
        draws = jnp.exp(jax.random.uniform(jax.random.fold_in(own, axis_at), (blocks,), jnp.float32, smallest / len(split), top_value / len(split)))
        loudness = loudness * jnp.repeat(draws, dims[axis_at] // blocks).reshape([-1 if axis == axis_at else 1 for axis in range(len(dims))])
    return loudness


def centred(own_key, extent, scale, bound, pieces=(), kind=jnp.bfloat16):
    values = scale * jax.random.normal(own_key, extent, jnp.float32)
    if pieces:
        values = values * block_scale(own_key, extent, pieces, -0.22, 0.18)
    return jnp.clip(values, -bound, bound).astype(kind)


def setup_inputs(seed: int = 0) -> dict:
    streams_of = jax.random.split(jax.random.key(seed), 9)
    return {
        "strain": centred(streams_of[0], (NSEC, COMP, LAY, PATH), 1.0, 6.0, ((0, 16), (3, 32))),
        "region": touch_ends(jax.random.randint(streams_of[1], (LAY, PATH), 0, NREG), jax.random.fold_in(streams_of[1], 1), 0, NREG - 1).astype(jnp.int32),
        "prior_peak": jnp.clip(5.0 + 20.0 * jax.random.uniform(streams_of[2], (LAY, PATH), jnp.float32) ** block_scale(streams_of[2], (LAY, PATH), ((1, 32),), -0.2, 0.2), 5.0, 25.0),
        "temp_prev": jnp.clip(0.5 + 1.0 * jax.random.uniform(streams_of[3], (LAY, PATH), jnp.float32) ** block_scale(streams_of[3], (LAY, PATH), ((1, 32),), -0.2, 0.2), 0.5, 1.5),
        "conductivity": jnp.clip(jnp.exp(math.log(2.0) - 1.3862944 * jax.random.uniform(streams_of[4], (LAY, PATH), jnp.float32) ** block_scale(streams_of[4], (LAY, PATH), ((1, 32),), -0.2, 0.2)), 0.5, 2.0),
        "loss_moduli": jnp.clip(jnp.exp(jax.random.uniform(streams_of[5], (NREG, HARM), jnp.float32, math.log(0.02), math.log(0.25))), 0.02, 0.25),
        "mullins_loss": jnp.clip(jnp.exp(jax.random.uniform(streams_of[6], (NREG,), jnp.float32, math.log(0.1), math.log(1.0))), 0.1, 1.0),
        "stiffness": jnp.clip(jnp.exp(jax.random.uniform(streams_of[7], (NREG,), jnp.float32, math.log(0.5), math.log(4.0))), 0.5, 4.0),
    }


sink_rate = 0.1

def harmonic_table():
    sections = jnp.arange(NSEC, dtype=jnp.int32)
    orders = jnp.arange(1, HARM + 1, dtype=jnp.int32)
    phase = orders[:, None] * sections[None, :] % NSEC
    angle = phase.astype(jnp.float32) * (2.0 * math.pi / NSEC)
    return jnp.concatenate([jnp.cos(angle), jnp.sin(angle)], 0).astype(jnp.bfloat16)

def reference(strain, region, prior_peak, temp_prev, conductivity, loss_moduli, mullins_loss, stiffness):
    blocks = strain.reshape(N_CIRC, SEC_DEV, COMP, LAY, PATH)
    table = harmonic_table().reshape(2 * HARM, N_CIRC, SEC_DEV).transpose(1, 0, 2)

    def accumulate(carry, item):
        tab, block = item
        total, top = carry
        total = total + jnp.dot(tab, block.reshape(SEC_DEV, -1), preferred_element_type=jnp.float32)
        energy = lax.optimization_barrier(jnp.sum(jnp.square(block.astype(jnp.float32)), axis=1))
        top = jnp.maximum(top, lax.optimization_barrier(jnp.max(energy, axis=0)))
        return ((total, top), None)
    init = (jnp.zeros((2 * HARM, COMP * LAY * PATH), jnp.float32), jnp.zeros((LAY, PATH), jnp.float32))
    (total, top), _ = lax.scan(accumulate, init, (table, blocks))
    coeffs = (total / jnp.sqrt(jnp.float32(NSEC))).reshape(2 * HARM, COMP, LAY, PATH)
    power = lax.optimization_barrier(jnp.sum(jnp.square(coeffs[:HARM]) + jnp.square(coeffs[HARM:]), axis=1))
    loss_map = jnp.transpose(loss_moduli[region], (2, 0, 1))
    hysteresis = jnp.exp(-0.5 * temp_prev) * lax.optimization_barrier(jnp.sum(loss_map * power, axis=0))
    peak = jnp.maximum(prior_peak, top)
    heat = hysteresis + mullins_loss[region] * (peak - prior_peak)
    field = temp_prev
    for sweep_index in range(SWEEPS):
        padded = jnp.pad(field, 1)
        beside = padded[2:, 1:-1] + padded[:-2, 1:-1] + padded[1:-1, 2:] + padded[1:-1, :-2]
        field = (heat + conductivity * beside) / (4.0 * conductivity + sink_rate)
    factor = stiffness[region] * jnp.exp(-0.5 * field)

    def soften(block):
        energy = lax.optimization_barrier(jnp.sum(jnp.square(block.astype(jnp.float32)), axis=1))
        return (factor[None] * (1.0 - 0.5 * jnp.tanh((peak[None] - energy) / 4.0))).astype(jnp.bfloat16)
    modulus = lax.map(soften, blocks).reshape(NSEC, LAY, PATH)
    return (field, peak, modulus)
```

```python
import functools
import math

import jax
import jax.numpy as jnp
import ml_dtypes
import numpy as np
from jax import lax
from jax.experimental import pallas as pl
from jax.experimental.pallas import tpu as pltpu
from jax.sharding import PartitionSpec as P

COMP = 2
HARM = 8
SWEEPS = 4
SINK = 0.1
SEC = 128
LAY = 36
LANES = 128
NREG = 8
CIRC = 16
NSEC = SEC * CIRC
RANK = 10
ROWS = 48
EDGE = 4
FIELD_ROWS = 40


def split3(values):
    parts = []
    rest = values.astype(np.float64)
    for _ in range(3):
        part = rest.astype(ml_dtypes.bfloat16)
        parts.append(part)
        rest = rest - part.astype(np.float64)
    return parts


def window_basis():
    t = (np.arange(SEC) - 0.5 * (SEC - 1)) / (0.5 * (SEC - 1))
    rows = [np.ones_like(t), t]
    for _ in range(RANK - 2):
        rows.append(2.0 * t * rows[-1] - rows[-2])
    return np.stack(rows)


def project_matrix():
    basis = window_basis()
    full = np.zeros((COMP * RANK, SEC, COMP))
    for comp in range(COMP):
        full[comp * RANK : (comp + 1) * RANK, :, comp] = basis
    full = full.reshape(COMP * RANK, SEC * COMP)
    out = []
    for kind in range(3):
        rows = np.zeros((32 if kind == 2 else 24, SEC * COMP))
        if kind == 0:
            rows[:20] = full
        elif kind == 1:
            rows[4:] = full
        else:
            for b in range(4):
                rows[8 * b : 8 * b + 5] = full[5 * b : 5 * b + 5]
        out.append(np.concatenate(split3(rows)))
    return np.concatenate(out)


def combine_matrix():
    half = 0.5 * (SEC - 1) * 2.0 * math.pi / NSEC
    nodes = 64
    n = (np.arange(nodes) + 0.5) * math.pi / nodes
    even = np.zeros((HARM, RANK))
    odd = np.zeros((HARM, RANK))
    for k in range(1, HARM + 1):
        for m in range(RANK):
            weight = (1.0 if m == 0 else 2.0) / nodes
            f = np.cos(k * half * np.cos(n)) if m % 2 == 0 else np.sin(k * half * np.cos(n))
            (even if m % 2 == 0 else odd)[k - 1, m] = weight * np.sum(f * np.cos(m * n))
    u = np.zeros((2 * HARM, CIRC, RANK))
    for d in range(CIRC):
        centre = 2.0 * math.pi * (SEC * d + 0.5 * (SEC - 1)) / NSEC
        for k in range(1, HARM + 1):
            c, s = math.cos(k * centre), math.sin(k * centre)
            u[k - 1, d] = c * even[k - 1] - s * odd[k - 1]
            u[HARM + k - 1, d] = s * even[k - 1] + c * odd[k - 1]
    u = u / math.sqrt(NSEC)
    w = np.zeros((128, CIRC, ROWS))
    for a in range(2):
        for comp in range(COMP):
            at = 20 * a + RANK * comp
            w[32 * a + 16 * comp : 32 * a + 16 * comp + 16, :, at : at + RANK] = u
    for b in range(4):
        first = 5 * (b % 2)
        w[64 + 16 * b : 64 + 16 * b + 16, :, 40:45] = u[:, :, first : first + 5]
    w = w.reshape(128, CIRC * ROWS)
    hi = w.astype(ml_dtypes.bfloat16)
    lo = (w - hi.astype(np.float64)).astype(ml_dtypes.bfloat16)
    return np.concatenate([hi, lo])


def lane_of(shape):
    return lax.broadcasted_iota(jnp.int32, shape, len(shape) - 1)


def row_of(shape):
    return lax.broadcasted_iota(jnp.int32, shape, 0)


def halves(first, second):
    low = lane_of(first.shape) < 64
    return (
        jnp.where(low, first, pltpu.roll(second, 64, 1)),
        jnp.where(low, pltpu.roll(first, 64, 1), second),
    )


def quarter_of(u, h):
    return 3 * h if u % 2 == 0 else 1 + h


CHUNK = 12


def project_kernel(strain_hbm, a_ref, send_ref, energy_ref, buf, squares, sem):
    copies = [
        pltpu.make_async_copy(strain_hbm.at[:, l], buf.at[l], sem.at[l]) for l in range(LAY)
    ]
    for copy in copies:
        copy.start()
    rows = buf.reshape(LAY, SEC * COMP, LANES)
    tops = {}
    sums = {}
    sub = row_of((8, LANES))
    block = lane_of((8, LANES)) // 32

    def pair(t):
        kind = 2 if t >= 16 else t % 2
        size = 32 if kind == 2 else 24
        base = 72 * kind
        x = jnp.concatenate([rows[2 * t], rows[2 * t + 1]], axis=1)
        d = jnp.dot(a_ref[base : base + 3 * size], x, preferred_element_type=jnp.float32)
        d = d[:size] + d[size : 2 * size] + d[2 * size :]
        for i in range(2):
            l = 2 * t + i
            slot = l % CHUNK
            wide = rows[l].astype(jnp.float32)
            squares[slot] = wide * wide
            e = squares[slot, pl.ds(0, SEC, stride=2), :] + squares[slot, pl.ds(1, SEC, stride=2), :]
            energy_ref[l] = e
            tops[l] = jnp.max(e, axis=0, keepdims=True)
            sums[l] = d[:, LANES * i : LANES * (i + 1)]

    for l in range(LAY):
        if l % CHUNK == 0:
            for other in range(l, min(l + CHUNK, LAY)):
                copies[other].wait()
        if l % 2 == 0:
            pair(l // 2)

    tails = {}
    for v in range(4):
        x = sums[32 + v]
        shifted = []
        for delta in range(4):
            w = jnp.zeros((8, LANES), jnp.float32)
            for b in range(4):
                w = jnp.where(block == (b - delta) % 4, x[8 * b : 8 * b + 8], w)
            shifted.append(pltpu.roll(w, 32 * delta, 1) if delta else w)
        for g in range(4):
            y = shifted[0]
            for b in range(4):
                y = jnp.where(block == b, shifted[(b - g) % 4], y)
            tails[v, g] = y

    for u in range(8):
        first = halves(sums[4 * u], sums[4 * u + 1])
        second = halves(sums[4 * u + 2], sums[4 * u + 3])
        top0 = halves(tops[4 * u], tops[4 * u + 1])
        top1 = halves(tops[4 * u + 2], tops[4 * u + 3])
        for h in range(2):
            c = 2 * u + h
            v, g = u // 2, quarter_of(u, h)
            send_ref[c, 0:16] = first[h][0:16]
            send_ref[c, 16:24] = first[h][16:24] + second[h][0:8]
            send_ref[c, 24:40] = second[h][8:24]
            top2 = tops[32 + v]
            if g:
                top2 = pltpu.roll(top2, LANES - 32 * g, 1)
            tile = jnp.where(sub == 5, top0[h], tails[v, g])
            tile = jnp.where(sub == 6, top1[h], tile)
            send_ref[c, 40:48] = jnp.where(sub == 7, top2, tile)


def project(strain, a):
    return pl.pallas_call(
        project_kernel,
        name="project",
        out_shape=[
            jax.ShapeDtypeStruct((CIRC, ROWS, LANES), jnp.float32),
            jax.ShapeDtypeStruct((LAY, SEC, LANES), jnp.float32),
        ],
        in_specs=[pl.BlockSpec(memory_space=pl.ANY), pl.BlockSpec(memory_space=pltpu.VMEM)],
        out_specs=[pl.BlockSpec(memory_space=pltpu.VMEM)] * 2,
        scratch_shapes=[
            pltpu.VMEM((LAY, SEC, COMP, LANES), jnp.bfloat16),
            pltpu.VMEM((CHUNK, SEC * COMP, LANES), jnp.float32),
            pltpu.SemaphoreType.DMA((LAY,)),
        ],
        compiler_params=pltpu.CompilerParams(vmem_limit_bytes=32 * 2**20),
    )(strain, a)


def owner_kernel(
    recv_ref, w_ref, region_ref, prior_ref, temp_ref, cond_ref, loss_ref, mullins_ref, own_ref, msg_ref
):
    c = lax.axis_index("circ")
    u = c // 2
    h = c % 2
    is_left = h == 0
    lane = lane_of((1, LANES))
    sub = row_of((8, LANES))
    p = recv_ref[...]
    hi = p.astype(jnp.bfloat16)
    lo = (p - hi.astype(jnp.float32)).astype(jnp.bfloat16)
    o = jnp.dot(
        w_ref[...], jnp.concatenate([hi, lo], axis=1), preferred_element_type=jnp.float32
    )
    coeffs = o[:128, :LANES] + o[128:, :LANES] + o[:128, LANES:]
    squared = coeffs[:64] * coeffs[:64]
    powers = [
        squared[32 * a : 32 * a + 8]
        + squared[32 * a + 8 : 32 * a + 16]
        + squared[32 * a + 16 : 32 * a + 24]
        + squared[32 * a + 24 : 32 * a + 32]
        for a in range(2)
    ]
    last = [coeffs[64 + 16 * b : 80 + 16 * b] for b in range(4)]
    comp0 = last[0] + pltpu.roll(last[1], 96, 1)
    comp1 = pltpu.roll(last[2], 64, 1) + pltpu.roll(last[3], 32, 1)
    comp0, comp1 = comp0 * comp0, comp1 * comp1
    powers.append(comp0[:8] + comp0[8:] + comp1[:8] + comp1[8:])

    quarter = jnp.where(u % 2 == 0, 3 * h, 1 + h)
    back = (LANES - 32 * quarter) % LANES

    def natural(ref):
        rows = [ref[pl.ds(4 * u + j, 1), :] for j in range(4)]
        rows.append(ref[pl.ds(32 + u // 2, 1), :])
        return rows

    def packed(rows):
        out = []
        for a in range(2):
            left, right = halves(rows[2 * a], rows[2 * a + 1])
            out.append(jnp.where(is_left, left, right))
        out.append(pltpu.roll(rows[4], back, 1))
        return out

    region = packed(natural(region_ref))
    prior = packed(natural(prior_ref))
    temp_rows = natural(temp_ref)
    temp = packed(temp_rows)
    cond_rows = natural(cond_ref)
    heats, peaks = [], []
    for i in range(3):
        q = loss_ref[:, 0:1] * powers[i][0:1]
        for k in range(1, HARM):
            q = q + loss_ref[:, k : k + 1] * powers[i][k : k + 1]
        picked = jnp.sum(jnp.where(region[i] == sub, q, 0.0), axis=0, keepdims=True)
        share = jnp.zeros((1, LANES), jnp.float32)
        for r in range(NREG):
            share = jnp.where(region[i] == r, mullins_ref[0:1, r : r + 1], share)
        top = jnp.max(recv_ref[pl.ds(45 + i, CIRC, stride=ROWS), :], axis=0, keepdims=True)
        peak = jnp.maximum(prior[i], top)
        heats.append(jnp.exp(-0.5 * temp[i]) * picked + share * (peak - prior[i]))
        peaks.append(peak)

    third = (lane >= 32) & (lane < 64)
    own = jnp.where(sub == 0, heats[0], 0.0)
    own = jnp.where(sub == 1, heats[1], own)
    own = jnp.where(sub == 2, peaks[0], own)
    own = jnp.where(sub == 3, peaks[1], own)
    own = jnp.where((sub == 4) & third, pltpu.roll(heats[2], 32, 1), own)
    own_ref[...] = jnp.where((sub == 5) & third, pltpu.roll(peaks[2], 32, 1), own)

    edge_heat = []
    for a in range(2):
        turned = pltpu.roll(heats[a], 64, 1)
        edge_heat.append(jnp.where(is_left, heats[a], turned))
        edge_heat.append(jnp.where(is_left, turned, heats[a]))
    edge_heat.append(jnp.where(is_left, heats[2], pltpu.roll(heats[2], 96, 1)))
    edge = jnp.where(is_left, lane, LANES - 1 - lane) < EDGE
    step = jnp.where(is_left, EDGE, LANES - EDGE)
    msg = jnp.zeros((8, LANES), jnp.float32)
    for j in range(5):
        row = jnp.where(edge, edge_heat[j], 0.0)
        row = row + pltpu.roll(jnp.where(edge, cond_rows[j], 0.0), step, 1)
        row = row + pltpu.roll(jnp.where(edge, temp_rows[j], 0.0), (2 * step) % LANES, 1)
        if j < 4:
            msg = msg + jnp.where(sub == 4 + j, row, 0.0)
        else:
            row = pltpu.roll(row, jnp.where(is_left, 32, 96), 1)
            msg = msg + jnp.where(sub == 6, row, 0.0)
    msg_ref[...] = msg


def owner(recv, w, region, prior, temp, cond, loss, mullins):
    vmem = pl.BlockSpec(memory_space=pltpu.VMEM)
    return pl.pallas_call(
        owner_kernel,
        name="owner",
        out_shape=[jax.ShapeDtypeStruct((8, LANES), jnp.float32)] * 2,
        in_specs=[vmem] * 8,
        out_specs=[vmem] * 2,
        compiler_params=pltpu.CompilerParams(vmem_limit_bytes=32 * 2**20),
    )(recv, w, region, prior, temp, cond, loss, mullins)


GROUPS = 6


def modulus_kernel(
    all_ref, energy_ref, region_ref, temp_ref, cond_ref, stiff_ref,
    field_hbm, peak_hbm, out_hbm,
    heat_s, peak_s, halo_s, cond_s, temp_s, region_s, field_s, out_s, sem,
):
    low = lane_of((8, LANES)) < 64
    lane = lane_of((FIELD_ROWS, LANES))
    for scratch in (heat_s, peak_s, halo_s, cond_s, temp_s):
        scratch[32:FIELD_ROWS] = jnp.zeros((8, LANES), jnp.float32)
    region_s[32:FIELD_ROWS] = jnp.zeros((8, LANES), jnp.int32)
    cond_s[0:LAY] = cond_ref[...]
    temp_s[0:LAY] = temp_ref[...]
    region_s[0:LAY] = region_ref[...]
    for a in range(2):
        for base, target in ((0, heat_s), (2, peak_s)):
            left = all_ref[pl.ds(base + a, 8, stride=16), :]
            right = all_ref[pl.ds(8 + base + a, 8, stride=16), :]
            target[pl.ds(2 * a, 8, stride=4), :] = jnp.where(low, left, pltpu.roll(right, 64, 1))
            target[pl.ds(2 * a + 1, 8, stride=4), :] = jnp.where(low, pltpu.roll(left, 64, 1), right)
    small = lane_of((4, LANES))
    for base, target in ((4, heat_s), (5, peak_s)):
        row = jnp.zeros((4, LANES), jnp.float32)
        for odd, h, g in ((0, 0, 0), (1, 0, 1), (1, 1, 2), (0, 1, 3)):
            part = all_ref[pl.ds(16 * odd + 8 * h + base, 4, stride=32), :]
            if g != 1:
                part = pltpu.roll(part, (32 * g - 32) % LANES, 1)
            row = jnp.where(small // 32 == g, part, row)
        target[32:LAY] = row
    wide = lane_of((8, LANES))
    outer = (wide < 3 * EDGE) | (wide >= LANES - 3 * EDGE)
    for j in range(4):
        both = all_ref[pl.ds(4 + j, 8, stride=16), :] + all_ref[pl.ds(12 + j, 8, stride=16), :]
        halo_s[pl.ds(j, 8, stride=4), :] = jnp.where(outer, both, 0.0)
    from_left = pltpu.roll(all_ref[pl.ds(6, 4, stride=32), :], 32, 1)
    from_right = pltpu.roll(all_ref[pl.ds(14, 4, stride=32), :], 96, 1)
    halo_s[32:LAY] = jnp.where(
        small >= LANES - 3 * EDGE, from_left, jnp.where(small < 3 * EDGE, from_right, 0.0)
    )

    halo = halo_s[...]

    def unpack(n):
        low_part = pltpu.roll(halo, (LANES - EDGE * n) % LANES, 1) if n else halo
        high_part = pltpu.roll(halo, EDGE * n, 1) if n else halo
        return jnp.where(
            lane < EDGE, low_part, jnp.where(lane >= LANES - EDGE, high_part, 0.0)
        )

    peak = peak_s[...]
    heat = (heat_s[...], unpack(0))
    cond = (cond_s[...], unpack(1))
    field = (temp_s[...], unpack(2))
    scale = [1.0 / (4.0 * k + SINK) for k in cond]
    heat = [x * y for x, y in zip(heat, scale)]
    cond = [x * y for x, y in zip(cond, scale)]
    rows = row_of((FIELD_ROWS, LANES))
    valid = rows < LAY
    first, final = lane == 0, lane == LANES - 1
    for _ in range(SWEEPS):
        right = [pltpu.roll(x, 1, 1) for x in field]
        left = [pltpu.roll(x, LANES - 1, 1) for x in field]
        new = []
        for i in range(2):
            beside = jnp.where(first, right[1 - i], right[i]) + jnp.where(final, left[1 - i], left[i])
            beside = beside + pltpu.roll(field[i], 1, 0) + pltpu.roll(field[i], FIELD_ROWS - 1, 0)
            new.append(jnp.where(valid, heat[i] + cond[i] * beside, 0.0))
        field = new
    field_s[...] = field[0]
    copies = [
        pltpu.make_async_copy(field_s.at[0:LAY], field_hbm, sem.at[0]),
        pltpu.make_async_copy(peak_s.at[0:LAY], peak_hbm, sem.at[1]),
    ]
    for copy in copies:
        copy.start()
    region = region_s[...]
    stiff = jnp.zeros((FIELD_ROWS, LANES), jnp.float32)
    for r in range(NREG):
        stiff = jnp.where(region == r, stiff_ref[0:1, r : r + 1], stiff)
    factor = stiff * jnp.exp(-0.5 * field[0])
    size = LAY // GROUPS
    for group in range(GROUPS):
        for l in range(group * size, (group + 1) * size):
            soft = jnp.tanh((peak[l : l + 1] - energy_ref[l]) * 0.25)
            out_s[l] = (factor[l : l + 1] * (1.0 - 0.5 * soft)).astype(jnp.bfloat16)
        where = pl.ds(group * size, size)
        copy = pltpu.make_async_copy(out_s.at[where], out_hbm.at[where], sem.at[2 + group])
        copy.start()
        copies.append(copy)
    for copy in copies:
        copy.wait()


def soften(everything, energy, region, temp, cond, stiff):
    vmem = pl.BlockSpec(memory_space=pltpu.VMEM)
    plane = pltpu.VMEM((FIELD_ROWS, LANES), jnp.float32)
    return pl.pallas_call(
        modulus_kernel,
        name="modulus",
        out_shape=[
            jax.ShapeDtypeStruct((LAY, LANES), jnp.float32),
            jax.ShapeDtypeStruct((LAY, LANES), jnp.float32),
            jax.ShapeDtypeStruct((LAY, SEC, LANES), jnp.bfloat16),
        ],
        in_specs=[vmem] * 6,
        out_specs=[pl.BlockSpec(memory_space=pl.ANY)] * 3,
        scratch_shapes=[
            plane, plane, plane, plane, plane,
            pltpu.VMEM((FIELD_ROWS, LANES), jnp.int32),
            plane,
            pltpu.VMEM((LAY, SEC, LANES), jnp.bfloat16),
            pltpu.SemaphoreType.DMA((2 + GROUPS,)),
        ],
        compiler_params=pltpu.CompilerParams(vmem_limit_bytes=32 * 2**20),
    )(everything, energy, region, temp, cond, stiff)


def per_device(sects, a, w, strain, region, prior, temp, cond, loss, mullins, stiff):
    send, energy = project(strain.transpose(0, 2, 1, 3), a)
    recv = lax.all_to_all(send, "circ", 0, 0, tiled=True)
    own, msg = owner(
        recv.reshape(CIRC * ROWS, LANES), w, region, prior, temp, cond, loss, mullins.reshape(1, NREG)
    )
    pairs = []
    for s in range(1, sects):
        for u in range(CIRC // 2):
            left, right = 2 * u * sects + s, (2 * u + 1) * sects + s - 1
            pairs += [(left, right), (right, left)]
    halo = lax.ppermute(msg, ("circ", "sect"), pairs)
    block = jnp.broadcast_to((own + halo)[None], (CIRC, 8, LANES))
    everything = lax.all_to_all(block, "circ", 0, 0, tiled=True)
    field, peak, modulus = soften(
        everything.reshape(CIRC * 8, LANES), energy, region, temp, cond, stiff.reshape(1, NREG)
    )
    return field, peak, modulus.transpose(1, 0, 2)


def solution(mesh):
    a = project_matrix()
    w = combine_matrix()
    maps = P(None, "sect")

    def whole(*args):
        return jax.shard_map(
            functools.partial(per_device, mesh.shape["sect"], jnp.asarray(a), jnp.asarray(w)),
            mesh=mesh,
            in_specs=(P("circ", None, None, "sect"), maps, maps, maps, maps, P(), P(), P()),
            out_specs=(maps, maps, P("circ", None, "sect")),
            check_vma=False,
        )(*args)

    return whole
```

```python
import functools
import math

import jax
import jax.numpy as jnp
import ml_dtypes
import numpy as np
from jax import lax
from jax.experimental import pallas as pl
from jax.experimental.pallas import tpu as pltpu
from jax.sharding import PartitionSpec as P

COMP = 2
HARM = 8
SWEEPS = 4
SINK = 0.1
SEC = 128
LAY = 36
LANES = 128
NREG = 8
CIRC = 16
NSEC = SEC * CIRC
RANK = 10
ROWS = 48
EDGE = 4
FIELD_ROWS = 40


def combine_matrix():
    half = 0.5 * (SEC - 1) * 2.0 * math.pi / NSEC
    nodes = 64
    n = (np.arange(nodes) + 0.5) * math.pi / nodes
    even = np.zeros((HARM, RANK))
    odd = np.zeros((HARM, RANK))
    for k in range(1, HARM + 1):
        for m in range(RANK):
            weight = (1.0 if m == 0 else 2.0) / nodes
            f = np.cos(k * half * np.cos(n)) if m % 2 == 0 else np.sin(k * half * np.cos(n))
            (even if m % 2 == 0 else odd)[k - 1, m] = weight * np.sum(f * np.cos(m * n))
    u = np.zeros((2 * HARM, CIRC, RANK))
    for d in range(CIRC):
        centre = 2.0 * math.pi * (SEC * d + 0.5 * (SEC - 1)) / NSEC
        for k in range(1, HARM + 1):
            c, s = math.cos(k * centre), math.sin(k * centre)
            u[k - 1, d] = c * even[k - 1] - s * odd[k - 1]
            u[HARM + k - 1, d] = s * even[k - 1] + c * odd[k - 1]
    u = u / math.sqrt(NSEC)
    w = np.zeros((128, CIRC, ROWS))
    for a in range(2):
        for comp in range(COMP):
            at = 20 * a + RANK * comp
            w[32 * a + 16 * comp : 32 * a + 16 * comp + 16, :, at : at + RANK] = u
    for b in range(4):
        first = 5 * (b % 2)
        w[64 + 16 * b : 64 + 16 * b + 16, :, 40:45] = u[:, :, first : first + 5]
    w = w.reshape(128, CIRC * ROWS)
    hi = w.astype(ml_dtypes.bfloat16)
    lo = (w - hi.astype(np.float64)).astype(ml_dtypes.bfloat16)
    return np.concatenate([hi, lo])


def lane_of(shape):
    return lax.broadcasted_iota(jnp.int32, shape, len(shape) - 1)


def row_of(shape):
    return lax.broadcasted_iota(jnp.int32, shape, 0)


def halves(first, second):
    low = lane_of(first.shape) < 64
    return (
        jnp.where(low, first, pltpu.roll(second, 64, 1)),
        jnp.where(low, pltpu.roll(first, 64, 1), second),
    )


def quarter_of(u, h):
    return 3 * h if u % 2 == 0 else 1 + h


def window_matrix():
    wide = (1, SEC * COMP)
    lane = lane_of(wide)
    t = ((lane // 2).astype(jnp.float32) - 0.5 * (SEC - 1)) * (2.0 / (SEC - 1))
    basis = [jnp.ones(wide, jnp.float32), t]
    for _ in range(RANK - 2):
        basis.append(2.0 * t * basis[-1] - basis[-2])
    rows = [
        jnp.where(lane % 2 == comp, values, 0.0) for comp in range(COMP) for values in basis
    ]
    sub = row_of((8, SEC * COMP))
    parts = []
    for places in (
        range(20),
        range(4, 24),
        [8 * b + i for b in range(4) for i in range(5)],
    ):
        tiles = {}
        for place, row in zip(places, rows):
            tile = tiles.get(place // 8, jnp.zeros((8, SEC * COMP), jnp.float32))
            tiles[place // 8] = jnp.where(sub == place % 8, row, tile)
        rest = jnp.concatenate([tiles[i] for i in sorted(tiles)])
        for _ in range(3):
            part = rest.astype(jnp.bfloat16).astype(jnp.float32)
            parts.append(part)
            rest = rest - part
    return jnp.concatenate(parts).astype(jnp.bfloat16)


TAIL = 8
ORDER = ((TAIL, 0, 1, 2, 3, 4, 5, 6, 7),)


def project_kernel(strain_hbm, send_ref, energy_ref, buf, a_ref, sem):
    copies = {}
    for group in ORDER:
        for u in group:
            for l in range(4 * u, 4 * u + 4):
                copies[l] = pltpu.make_async_copy(strain_hbm.at[:, l], buf.at[l], sem.at[l])
                copies[l].start()
    rows = buf.reshape(LAY, SEC * COMP, LANES)
    tops = {}
    sums = {}
    tails = {}
    sub = row_of((8, LANES))
    block = lane_of((8, LANES)) // 32

    def pair(t):
        kind = 2 if t >= 16 else t % 2
        size = 32 if kind == 2 else 24
        base = 72 * kind
        x = jnp.concatenate([rows[2 * t], rows[2 * t + 1]], axis=1)
        d = jnp.dot(a_ref[base : base + 3 * size], x, preferred_element_type=jnp.float32)
        d = d[:size] + d[size : 2 * size] + d[2 * size :]
        for i in range(2):
            l = 2 * t + i
            c0 = rows[l, pl.ds(0, SEC, stride=2), :].astype(jnp.float32)
            c1 = rows[l, pl.ds(1, SEC, stride=2), :].astype(jnp.float32)
            e = c0 * c0 + c1 * c1
            energy_ref[l] = e
            tops[l] = jnp.max(e, axis=0, keepdims=True)
            sums[l] = d[:, LANES * i : LANES * (i + 1)]

    def pack_tail():
        for v in range(4):
            x = sums[32 + v]
            shifted = []
            for delta in range(4):
                w = jnp.zeros((8, LANES), jnp.float32)
                for b in range(4):
                    w = jnp.where(block == (b - delta) % 4, x[8 * b : 8 * b + 8], w)
                shifted.append(pltpu.roll(w, 32 * delta, 1) if delta else w)
            for g in range(4):
                y = shifted[0]
                for b in range(4):
                    y = jnp.where(block == b, shifted[(b - g) % 4], y)
                top = tops[32 + v]
                if g:
                    top = pltpu.roll(top, LANES - 32 * g, 1)
                tails[v, g] = jnp.where(sub == 7, top, y)

    def pack(u):
        first = halves(sums[4 * u], sums[4 * u + 1])
        second = halves(sums[4 * u + 2], sums[4 * u + 3])
        top0 = halves(tops[4 * u], tops[4 * u + 1])
        top1 = halves(tops[4 * u + 2], tops[4 * u + 3])
        for h in range(2):
            c = 2 * u + h
            send_ref[c, 0:16] = first[h][0:16]
            send_ref[c, 16:24] = first[h][16:24] + second[h][0:8]
            send_ref[c, 24:40] = second[h][8:24]
            tile = jnp.where(sub == 5, top0[h], tails[u // 2, quarter_of(u, h)])
            send_ref[c, 40:48] = jnp.where(sub == 6, top1[h], tile)

    a_ref[...] = window_matrix()
    waiting = []
    for group in ORDER:
        for u in group:
            for l in range(4 * u, 4 * u + 4):
                copies[l].wait()
        for u in group:
            pair(2 * u)
            pair(2 * u + 1)
        for u in waiting:
            pack_tail() if u == TAIL else pack(u)
        waiting = group
    for u in waiting:
        pack_tail() if u == TAIL else pack(u)


def project(strain):
    return pl.pallas_call(
        project_kernel,
        name="project",
        out_shape=[
            jax.ShapeDtypeStruct((CIRC, ROWS, LANES), jnp.float32),
            jax.ShapeDtypeStruct((LAY, SEC, LANES), jnp.float32),
        ],
        in_specs=[pl.BlockSpec(memory_space=pl.ANY)],
        out_specs=[pl.BlockSpec(memory_space=pltpu.VMEM)] * 2,
        scratch_shapes=[
            pltpu.VMEM((LAY, SEC, COMP, LANES), jnp.bfloat16),
            pltpu.VMEM((240, SEC * COMP), jnp.bfloat16),
            pltpu.SemaphoreType.DMA((LAY,)),
        ],
        compiler_params=pltpu.CompilerParams(vmem_limit_bytes=50 * 2**20),
    )(strain)


def owner_kernel(
    recv_ref, w_ref, region_ref, prior_ref, temp_ref, cond_ref, loss_ref, mullins_ref, own_ref, msg_ref
):
    c = lax.axis_index("circ")
    u = c // 2
    h = c % 2
    is_left = h == 0
    lane = lane_of((1, LANES))
    sub = row_of((8, LANES))
    p = recv_ref[...]
    hi = p.astype(jnp.bfloat16)
    lo = (p - hi.astype(jnp.float32)).astype(jnp.bfloat16)
    o = jnp.dot(
        w_ref[...], jnp.concatenate([hi, lo], axis=1), preferred_element_type=jnp.float32
    )
    coeffs = o[:128, :LANES] + o[128:, :LANES] + o[:128, LANES:]
    squared = coeffs[:64] * coeffs[:64]
    powers = [
        squared[32 * a : 32 * a + 8]
        + squared[32 * a + 8 : 32 * a + 16]
        + squared[32 * a + 16 : 32 * a + 24]
        + squared[32 * a + 24 : 32 * a + 32]
        for a in range(2)
    ]
    last = [coeffs[64 + 16 * b : 80 + 16 * b] for b in range(4)]
    comp0 = last[0] + pltpu.roll(last[1], 96, 1)
    comp1 = pltpu.roll(last[2], 64, 1) + pltpu.roll(last[3], 32, 1)
    comp0, comp1 = comp0 * comp0, comp1 * comp1
    powers.append(comp0[:8] + comp0[8:] + comp1[:8] + comp1[8:])

    quarter = jnp.where(u % 2 == 0, 3 * h, 1 + h)
    back = (LANES - 32 * quarter) % LANES

    def natural(ref):
        rows = [ref[pl.ds(4 * u + j, 1), :] for j in range(4)]
        rows.append(ref[pl.ds(32 + u // 2, 1), :])
        return rows

    def packed(rows):
        out = []
        for a in range(2):
            left, right = halves(rows[2 * a], rows[2 * a + 1])
            out.append(jnp.where(is_left, left, right))
        out.append(pltpu.roll(rows[4], back, 1))
        return out

    region = packed(natural(region_ref))
    prior = packed(natural(prior_ref))
    temp_rows = natural(temp_ref)
    temp = packed(temp_rows)
    cond_rows = natural(cond_ref)
    heats, peaks = [], []
    for i in range(3):
        q = loss_ref[:, 0:1] * powers[i][0:1]
        for k in range(1, HARM):
            q = q + loss_ref[:, k : k + 1] * powers[i][k : k + 1]
        picked = jnp.sum(jnp.where(region[i] == sub, q, 0.0), axis=0, keepdims=True)
        share = jnp.zeros((1, LANES), jnp.float32)
        for r in range(NREG):
            share = jnp.where(region[i] == r, mullins_ref[0:1, r : r + 1], share)
        top = jnp.max(recv_ref[pl.ds(45 + i, CIRC, stride=ROWS), :], axis=0, keepdims=True)
        peak = jnp.maximum(prior[i], top)
        heats.append(jnp.exp(-0.5 * temp[i]) * picked + share * (peak - prior[i]))
        peaks.append(peak)

    third = (lane >= 32) & (lane < 64)
    own = jnp.where(sub == 0, heats[0], 0.0)
    own = jnp.where(sub == 1, heats[1], own)
    own = jnp.where(sub == 2, peaks[0], own)
    own = jnp.where(sub == 3, peaks[1], own)
    own = jnp.where((sub == 4) & third, pltpu.roll(heats[2], 32, 1), own)
    own_ref[...] = jnp.where((sub == 5) & third, pltpu.roll(peaks[2], 32, 1), own)

    edge_heat = []
    for a in range(2):
        turned = pltpu.roll(heats[a], 64, 1)
        edge_heat.append(jnp.where(is_left, heats[a], turned))
        edge_heat.append(jnp.where(is_left, turned, heats[a]))
    edge_heat.append(jnp.where(is_left, heats[2], pltpu.roll(heats[2], 96, 1)))
    edge = jnp.where(is_left, lane, LANES - 1 - lane) < EDGE
    step = jnp.where(is_left, EDGE, LANES - EDGE)
    msg = jnp.zeros((8, LANES), jnp.float32)
    for j in range(5):
        row = jnp.where(edge, edge_heat[j], 0.0)
        row = row + pltpu.roll(jnp.where(edge, cond_rows[j], 0.0), step, 1)
        row = row + pltpu.roll(jnp.where(edge, temp_rows[j], 0.0), (2 * step) % LANES, 1)
        if j < 4:
            msg = msg + jnp.where(sub == 4 + j, row, 0.0)
        else:
            row = pltpu.roll(row, jnp.where(is_left, 32, 96), 1)
            msg = msg + jnp.where(sub == 6, row, 0.0)
    msg_ref[...] = msg


def owner(recv, w, region, prior, temp, cond, loss, mullins):
    vmem = pl.BlockSpec(memory_space=pltpu.VMEM)
    return pl.pallas_call(
        owner_kernel,
        name="owner",
        out_shape=[jax.ShapeDtypeStruct((8, LANES), jnp.float32)] * 2,
        in_specs=[vmem] * 8,
        out_specs=[vmem] * 2,
        compiler_params=pltpu.CompilerParams(vmem_limit_bytes=32 * 2**20),
    )(recv, w, region, prior, temp, cond, loss, mullins)


GROUPS = 6


def modulus_kernel(
    all_ref, energy_ref, region_ref, temp_ref, cond_ref, stiff_ref,
    field_hbm, peak_hbm, out_hbm,
    heat_s, peak_s, halo_s, cond_s, temp_s, region_s, field_s, out_s, sem,
):
    low = lane_of((8, LANES)) < 64
    lane = lane_of((FIELD_ROWS, LANES))
    for scratch in (heat_s, peak_s, halo_s, cond_s, temp_s):
        scratch[32:FIELD_ROWS] = jnp.zeros((8, LANES), jnp.float32)
    region_s[32:FIELD_ROWS] = jnp.zeros((8, LANES), jnp.int32)
    cond_s[0:LAY] = cond_ref[...]
    temp_s[0:LAY] = temp_ref[...]
    region_s[0:LAY] = region_ref[...]
    for a in range(2):
        for base, target in ((0, heat_s), (2, peak_s)):
            left = all_ref[pl.ds(base + a, 8, stride=16), :]
            right = all_ref[pl.ds(8 + base + a, 8, stride=16), :]
            target[pl.ds(2 * a, 8, stride=4), :] = jnp.where(low, left, pltpu.roll(right, 64, 1))
            target[pl.ds(2 * a + 1, 8, stride=4), :] = jnp.where(low, pltpu.roll(left, 64, 1), right)
    small = lane_of((4, LANES))
    for base, target in ((4, heat_s), (5, peak_s)):
        row = jnp.zeros((4, LANES), jnp.float32)
        for odd, h, g in ((0, 0, 0), (1, 0, 1), (1, 1, 2), (0, 1, 3)):
            part = all_ref[pl.ds(16 * odd + 8 * h + base, 4, stride=32), :]
            if g != 1:
                part = pltpu.roll(part, (32 * g - 32) % LANES, 1)
            row = jnp.where(small // 32 == g, part, row)
        target[32:LAY] = row
    wide = lane_of((8, LANES))
    outer = (wide < 3 * EDGE) | (wide >= LANES - 3 * EDGE)
    for j in range(4):
        both = all_ref[pl.ds(4 + j, 8, stride=16), :] + all_ref[pl.ds(12 + j, 8, stride=16), :]
        halo_s[pl.ds(j, 8, stride=4), :] = jnp.where(outer, both, 0.0)
    from_left = pltpu.roll(all_ref[pl.ds(6, 4, stride=32), :], 32, 1)
    from_right = pltpu.roll(all_ref[pl.ds(14, 4, stride=32), :], 96, 1)
    halo_s[32:LAY] = jnp.where(
        small >= LANES - 3 * EDGE, from_left, jnp.where(small < 3 * EDGE, from_right, 0.0)
    )

    halo = halo_s[...]

    def unpack(n):
        low_part = pltpu.roll(halo, (LANES - EDGE * n) % LANES, 1) if n else halo
        high_part = pltpu.roll(halo, EDGE * n, 1) if n else halo
        return jnp.where(
            lane < EDGE, low_part, jnp.where(lane >= LANES - EDGE, high_part, 0.0)
        )

    peak = peak_s[...]
    heat = (heat_s[...], unpack(0))
    cond = (cond_s[...], unpack(1))
    field = (temp_s[...], unpack(2))
    scale = [1.0 / (4.0 * k + SINK) for k in cond]
    heat = [x * y for x, y in zip(heat, scale)]
    cond = [x * y for x, y in zip(cond, scale)]
    rows = row_of((FIELD_ROWS, LANES))
    valid = rows < LAY
    first, final = lane == 0, lane == LANES - 1
    for _ in range(SWEEPS):
        right = [pltpu.roll(x, 1, 1) for x in field]
        left = [pltpu.roll(x, LANES - 1, 1) for x in field]
        new = []
        for i in range(2):
            beside = jnp.where(first, right[1 - i], right[i]) + jnp.where(final, left[1 - i], left[i])
            beside = beside + pltpu.roll(field[i], 1, 0) + pltpu.roll(field[i], FIELD_ROWS - 1, 0)
            new.append(jnp.where(valid, heat[i] + cond[i] * beside, 0.0))
        field = new
    field_s[...] = field[0]
    copies = [
        pltpu.make_async_copy(field_s.at[0:LAY], field_hbm, sem.at[0]),
        pltpu.make_async_copy(peak_s.at[0:LAY], peak_hbm, sem.at[1]),
    ]
    for copy in copies:
        copy.start()
    region = region_s[...]
    stiff = jnp.zeros((FIELD_ROWS, LANES), jnp.float32)
    for r in range(NREG):
        stiff = jnp.where(region == r, stiff_ref[0:1, r : r + 1], stiff)
    factor = stiff * jnp.exp(-0.5 * field[0])
    size = LAY // GROUPS
    for group in range(GROUPS):
        for l in range(group * size, (group + 1) * size):
            soft = jnp.tanh((peak[l : l + 1] - energy_ref[l]) * 0.25)
            out_s[l] = (factor[l : l + 1] * (1.0 - 0.5 * soft)).astype(jnp.bfloat16)
        where = pl.ds(group * size, size)
        copy = pltpu.make_async_copy(out_s.at[where], out_hbm.at[where], sem.at[2 + group])
        copy.start()
        copies.append(copy)
    for copy in copies:
        copy.wait()


def soften(everything, energy, region, temp, cond, stiff):
    vmem = pl.BlockSpec(memory_space=pltpu.VMEM)
    plane = pltpu.VMEM((FIELD_ROWS, LANES), jnp.float32)
    return pl.pallas_call(
        modulus_kernel,
        name="modulus",
        out_shape=[
            jax.ShapeDtypeStruct((LAY, LANES), jnp.float32),
            jax.ShapeDtypeStruct((LAY, LANES), jnp.float32),
            jax.ShapeDtypeStruct((LAY, SEC, LANES), jnp.bfloat16),
        ],
        in_specs=[vmem] * 6,
        out_specs=[pl.BlockSpec(memory_space=pl.ANY)] * 3,
        scratch_shapes=[
            plane, plane, plane, plane, plane,
            pltpu.VMEM((FIELD_ROWS, LANES), jnp.int32),
            plane,
            pltpu.VMEM((LAY, SEC, LANES), jnp.bfloat16),
            pltpu.SemaphoreType.DMA((2 + GROUPS,)),
        ],
        compiler_params=pltpu.CompilerParams(vmem_limit_bytes=32 * 2**20),
    )(everything, energy, region, temp, cond, stiff)


def per_device(sects, w, strain, region, prior, temp, cond, loss, mullins, stiff):
    send, energy = project(strain.transpose(0, 2, 1, 3))
    recv = lax.all_to_all(send, "circ", 0, 0, tiled=True)
    own, msg = owner(
        recv.reshape(CIRC * ROWS, LANES), w, region, prior, temp, cond, loss, mullins.reshape(1, NREG)
    )
    pairs = []
    for s in range(1, sects):
        for u in range(CIRC // 2):
            left, right = 2 * u * sects + s, (2 * u + 1) * sects + s - 1
            pairs += [(left, right), (right, left)]
    halo = lax.ppermute(msg, ("circ", "sect"), pairs)
    block = jnp.broadcast_to((own + halo)[None], (CIRC, 8, LANES))
    everything = lax.all_to_all(block, "circ", 0, 0, tiled=True)
    field, peak, modulus = soften(
        everything.reshape(CIRC * 8, LANES), energy, region, temp, cond, stiff.reshape(1, NREG)
    )
    return field, peak, modulus.transpose(1, 0, 2)


def solution(mesh):
    w = combine_matrix()
    maps = P(None, "sect")

    def whole(*args):
        return jax.shard_map(
            functools.partial(per_device, mesh.shape["sect"], jnp.asarray(w)),
            mesh=mesh,
            in_specs=(P("circ", None, None, "sect"), maps, maps, maps, maps, P(), P(), P()),
            out_specs=(maps, maps, P("circ", None, "sect")),
            check_vma=False,
        )(*args)

    return whole
```

```python
import functools
import math

import jax
import jax.numpy as jnp
import ml_dtypes
import numpy as np
from jax import lax
from jax.experimental import pallas as pl
from jax.experimental.pallas import tpu as pltpu
from jax.sharding import PartitionSpec as P

COMP = 2
HARM = 8
SWEEPS = 4
SINK = 0.1
SEC = 128
LAY = 36
LANES = 128
NREG = 8
CIRC = 16
NSEC = SEC * CIRC
RANK = 10
ROWS = 48
EDGE = 4
FIELD_ROWS = 40


def combine_matrix():
    half = 0.5 * (SEC - 1) * 2.0 * math.pi / NSEC
    nodes = 64
    n = (np.arange(nodes) + 0.5) * math.pi / nodes
    even = np.zeros((HARM, RANK))
    odd = np.zeros((HARM, RANK))
    for k in range(1, HARM + 1):
        for m in range(RANK):
            weight = (1.0 if m == 0 else 2.0) / nodes
            f = np.cos(k * half * np.cos(n)) if m % 2 == 0 else np.sin(k * half * np.cos(n))
            (even if m % 2 == 0 else odd)[k - 1, m] = weight * np.sum(f * np.cos(m * n))
    u = np.zeros((2 * HARM, CIRC, RANK))
    for d in range(CIRC):
        centre = 2.0 * math.pi * (SEC * d + 0.5 * (SEC - 1)) / NSEC
        for k in range(1, HARM + 1):
            c, s = math.cos(k * centre), math.sin(k * centre)
            u[k - 1, d] = c * even[k - 1] - s * odd[k - 1]
            u[HARM + k - 1, d] = s * even[k - 1] + c * odd[k - 1]
    u = u / math.sqrt(NSEC)
    w = np.zeros((128, CIRC, ROWS))
    for a in range(2):
        for comp in range(COMP):
            at = 20 * a + RANK * comp
            w[32 * a + 16 * comp : 32 * a + 16 * comp + 16, :, at : at + RANK] = u
    for b in range(4):
        first = 5 * (b % 2)
        w[64 + 16 * b : 64 + 16 * b + 16, :, 40:45] = u[:, :, first : first + 5]
    w = w.reshape(128, CIRC * ROWS)
    hi = w.astype(ml_dtypes.bfloat16)
    lo = (w - hi.astype(np.float64)).astype(ml_dtypes.bfloat16)
    return np.concatenate([hi, lo])


def lane_of(shape):
    return lax.broadcasted_iota(jnp.int32, shape, len(shape) - 1)


def row_of(shape):
    return lax.broadcasted_iota(jnp.int32, shape, 0)


def halves(first, second):
    low = lane_of(first.shape) < 64
    return (
        jnp.where(low, first, pltpu.roll(second, 64, 1)),
        jnp.where(low, pltpu.roll(first, 64, 1), second),
    )


def quarter_of(u, h):
    return 3 * h if u % 2 == 0 else 1 + h


def window_matrix():
    wide = (1, SEC * COMP)
    lane = lane_of(wide)
    t = ((lane % SEC).astype(jnp.float32) - 0.5 * (SEC - 1)) * (2.0 / (SEC - 1))
    basis = [jnp.ones(wide, jnp.float32), t]
    for _ in range(RANK - 2):
        basis.append(2.0 * t * basis[-1] - basis[-2])
    rows = [
        jnp.where(lane // SEC == comp, values, 0.0) for comp in range(COMP) for values in basis
    ]
    sub = row_of((8, SEC * COMP))
    parts = []
    for places in (
        range(20),
        range(4, 24),
        [8 * b + i for b in range(4) for i in range(5)],
    ):
        tiles = {}
        for place, row in zip(places, rows):
            tile = tiles.get(place // 8, jnp.zeros((8, SEC * COMP), jnp.float32))
            tiles[place // 8] = jnp.where(sub == place % 8, row, tile)
        rest = jnp.concatenate([tiles[i] for i in sorted(tiles)])
        for _ in range(3):
            part = rest.astype(jnp.bfloat16).astype(jnp.float32)
            parts.append(part)
            rest = rest - part
    return jnp.concatenate(parts).astype(jnp.bfloat16)


TAIL = 8
ORDER = ((TAIL, 0, 1), (2, 3, 4), (5, 6, 7))


def project_kernel(strain_hbm, send_ref, energy_ref, buf, a_ref, sem):
    copies = {}
    for group in ORDER:
        for u in group:
            for l in range(4 * u, 4 * u + 4):
                copies[l] = pltpu.make_async_copy(strain_hbm.at[:, l], buf.at[l], sem.at[l])
                copies[l].start()
    rows = buf.reshape(LAY, SEC * COMP, LANES)
    parity = lax.axis_index("sect") % 2
    tops = {}
    sums = {}
    tails = {}
    sub = row_of((8, LANES))
    block = lane_of((8, LANES)) // 32

    def pair(t):
        kind = 2 if t >= 16 else t % 2
        size = 32 if kind == 2 else 24
        base = 72 * kind
        x = [[rows[2 * t + i, pl.ds(c, SEC, stride=COMP), :] for i in range(2)] for c in range(COMP)]
        wide = jnp.concatenate([jnp.concatenate(both, axis=1) for both in x])
        d = jnp.dot(a_ref[base : base + 3 * size], wide, preferred_element_type=jnp.float32)
        d = d[:size] + d[size : 2 * size] + d[2 * size :]
        for i in range(2):
            l = 2 * t + i
            c0 = x[0][i].astype(jnp.float32)
            c1 = x[1][i].astype(jnp.float32)
            e = c0 * c0 + c1 * c1
            energy_ref[l] = e
            tops[l] = jnp.max(e, axis=0, keepdims=True)
            sums[l] = d[:, LANES * i : LANES * (i + 1)]

    def pack_tail():
        for v in range(4):
            x = sums[32 + v]
            shifted = []
            for delta in range(4):
                w = jnp.zeros((8, LANES), jnp.float32)
                for b in range(4):
                    w = jnp.where(block == (b - delta) % 4, x[8 * b : 8 * b + 8], w)
                shifted.append(pltpu.roll(w, 32 * delta, 1) if delta else w)
            for g in range(4):
                y = shifted[0]
                for b in range(4):
                    y = jnp.where(block == b, shifted[(b - g) % 4], y)
                top = tops[32 + v]
                if g:
                    top = pltpu.roll(top, LANES - 32 * g, 1)
                tails[v, g] = jnp.where(sub == 7, top, y)

    def pack(u):
        first = halves(sums[4 * u], sums[4 * u + 1])
        second = halves(sums[4 * u + 2], sums[4 * u + 3])
        top0 = halves(tops[4 * u], tops[4 * u + 1])
        top1 = halves(tops[4 * u + 2], tops[4 * u + 3])
        for h in range(2):
            c = 2 * u + (h + parity) % 2
            send_ref[c, 0:16] = first[h][0:16]
            send_ref[c, 16:24] = first[h][16:24] + second[h][0:8]
            send_ref[c, 24:40] = second[h][8:24]
            tile = jnp.where(sub == 5, top0[h], tails[u // 2, quarter_of(u, h)])
            send_ref[c, 40:48] = jnp.where(sub == 6, top1[h], tile)

    a_ref[...] = window_matrix()
    waiting = []
    for group in ORDER:
        for u in group:
            for l in range(4 * u, 4 * u + 4):
                copies[l].wait()
        for u in group:
            pair(2 * u)
            pair(2 * u + 1)
        for u in waiting:
            pack_tail() if u == TAIL else pack(u)
        waiting = group
    for u in waiting:
        pack_tail() if u == TAIL else pack(u)


def project(strain):
    return pl.pallas_call(
        project_kernel,
        name="project",
        out_shape=[
            jax.ShapeDtypeStruct((CIRC, ROWS, LANES), jnp.float32),
            jax.ShapeDtypeStruct((LAY, SEC, LANES), jnp.float32),
        ],
        in_specs=[pl.BlockSpec(memory_space=pl.ANY)],
        out_specs=[pl.BlockSpec(memory_space=pltpu.VMEM)] * 2,
        scratch_shapes=[
            pltpu.VMEM((LAY, SEC, COMP, LANES), jnp.bfloat16),
            pltpu.VMEM((240, SEC * COMP), jnp.bfloat16),
            pltpu.SemaphoreType.DMA((LAY,)),
        ],
        compiler_params=pltpu.CompilerParams(vmem_limit_bytes=50 * 2**20),
    )(strain)


def owner_kernel(
    recv_ref, w_ref, region_ref, prior_ref, temp_ref, cond_ref, loss_ref, mullins_ref, own_ref, msg_ref
):
    c = lax.axis_index("circ")
    u = c // 2
    h = (c + lax.axis_index("sect")) % 2
    is_left = h == 0
    lane = lane_of((1, LANES))
    sub = row_of((8, LANES))
    p = recv_ref[...]
    hi = p.astype(jnp.bfloat16)
    lo = (p - hi.astype(jnp.float32)).astype(jnp.bfloat16)
    o = jnp.dot(
        w_ref[...], jnp.concatenate([hi, lo], axis=1), preferred_element_type=jnp.float32
    )
    coeffs = o[:128, :LANES] + o[128:, :LANES] + o[:128, LANES:]
    squared = coeffs[:64] * coeffs[:64]
    powers = [
        squared[32 * a : 32 * a + 8]
        + squared[32 * a + 8 : 32 * a + 16]
        + squared[32 * a + 16 : 32 * a + 24]
        + squared[32 * a + 24 : 32 * a + 32]
        for a in range(2)
    ]
    last = [coeffs[64 + 16 * b : 80 + 16 * b] for b in range(4)]
    comp0 = last[0] + pltpu.roll(last[1], 96, 1)
    comp1 = pltpu.roll(last[2], 64, 1) + pltpu.roll(last[3], 32, 1)
    comp0, comp1 = comp0 * comp0, comp1 * comp1
    powers.append(comp0[:8] + comp0[8:] + comp1[:8] + comp1[8:])

    quarter = jnp.where(u % 2 == 0, 3 * h, 1 + h)
    back = (LANES - 32 * quarter) % LANES

    def natural(ref):
        rows = [ref[pl.ds(4 * u + j, 1), :] for j in range(4)]
        rows.append(ref[pl.ds(32 + u // 2, 1), :])
        return rows

    def packed(rows):
        out = []
        for a in range(2):
            left, right = halves(rows[2 * a], rows[2 * a + 1])
            out.append(jnp.where(is_left, left, right))
        out.append(pltpu.roll(rows[4], back, 1))
        return out

    region = packed(natural(region_ref))
    prior = packed(natural(prior_ref))
    temp_rows = natural(temp_ref)
    temp = packed(temp_rows)
    cond_rows = natural(cond_ref)
    heats, peaks = [], []
    for i in range(3):
        q = loss_ref[:, 0:1] * powers[i][0:1]
        for k in range(1, HARM):
            q = q + loss_ref[:, k : k + 1] * powers[i][k : k + 1]
        picked = jnp.sum(jnp.where(region[i] == sub, q, 0.0), axis=0, keepdims=True)
        share = jnp.zeros((1, LANES), jnp.float32)
        for r in range(NREG):
            share = jnp.where(region[i] == r, mullins_ref[0:1, r : r + 1], share)
        top = jnp.max(recv_ref[pl.ds(45 + i, CIRC, stride=ROWS), :], axis=0, keepdims=True)
        peak = jnp.maximum(prior[i], top)
        heats.append(jnp.exp(-0.5 * temp[i]) * picked + share * (peak - prior[i]))
        peaks.append(peak)

    third = (lane >= 32) & (lane < 64)
    own = jnp.where(sub == 0, heats[0], 0.0)
    own = jnp.where(sub == 1, heats[1], own)
    own = jnp.where(sub == 2, peaks[0], own)
    own = jnp.where(sub == 3, peaks[1], own)
    own = jnp.where((sub == 4) & third, pltpu.roll(heats[2], 32, 1), own)
    own_ref[...] = jnp.where((sub == 5) & third, pltpu.roll(peaks[2], 32, 1), own)

    edge_heat = []
    for a in range(2):
        turned = pltpu.roll(heats[a], 64, 1)
        edge_heat.append(jnp.where(is_left, heats[a], turned))
        edge_heat.append(jnp.where(is_left, turned, heats[a]))
    edge_heat.append(jnp.where(is_left, heats[2], pltpu.roll(heats[2], 96, 1)))
    edge = jnp.where(is_left, lane, LANES - 1 - lane) < EDGE
    step = jnp.where(is_left, EDGE, LANES - EDGE)
    msg = jnp.zeros((8, LANES), jnp.float32)
    for j in range(5):
        row = jnp.where(edge, edge_heat[j], 0.0)
        row = row + pltpu.roll(jnp.where(edge, cond_rows[j], 0.0), step, 1)
        row = row + pltpu.roll(jnp.where(edge, temp_rows[j], 0.0), (2 * step) % LANES, 1)
        if j < 4:
            msg = msg + jnp.where(sub == 4 + j, row, 0.0)
        else:
            row = pltpu.roll(row, jnp.where(is_left, 32, 96), 1)
            msg = msg + jnp.where(sub == 6, row, 0.0)
    msg_ref[...] = msg


def owner(recv, w, region, prior, temp, cond, loss, mullins):
    vmem = pl.BlockSpec(memory_space=pltpu.VMEM)
    return pl.pallas_call(
        owner_kernel,
        name="owner",
        out_shape=[jax.ShapeDtypeStruct((8, LANES), jnp.float32)] * 2,
        in_specs=[vmem] * 8,
        out_specs=[vmem] * 2,
        compiler_params=pltpu.CompilerParams(vmem_limit_bytes=32 * 2**20),
    )(recv, w, region, prior, temp, cond, loss, mullins)


GROUPS = 6


def modulus_kernel(
    all_ref, energy_ref, region_ref, temp_ref, cond_ref, stiff_ref,
    field_hbm, peak_hbm, out_hbm,
    heat_s, peak_s, halo_s, cond_s, temp_s, region_s, field_s, out_s, sem,
):
    low = lane_of((8, LANES)) < 64
    lane = lane_of((FIELD_ROWS, LANES))
    parity = lax.axis_index("sect") % 2
    at = [8 * parity, 8 * (1 - parity)]
    for scratch in (heat_s, peak_s, halo_s, cond_s, temp_s):
        scratch[32:FIELD_ROWS] = jnp.zeros((8, LANES), jnp.float32)
    region_s[32:FIELD_ROWS] = jnp.zeros((8, LANES), jnp.int32)
    cond_s[0:LAY] = cond_ref[...]
    temp_s[0:LAY] = temp_ref[...]
    region_s[0:LAY] = region_ref[...]
    for a in range(2):
        for base, target in ((0, heat_s), (2, peak_s)):
            left = all_ref[pl.ds(at[0] + base + a, 8, stride=16), :]
            right = all_ref[pl.ds(at[1] + base + a, 8, stride=16), :]
            target[pl.ds(2 * a, 8, stride=4), :] = jnp.where(low, left, pltpu.roll(right, 64, 1))
            target[pl.ds(2 * a + 1, 8, stride=4), :] = jnp.where(low, pltpu.roll(left, 64, 1), right)
    small = lane_of((4, LANES))
    for base, target in ((4, heat_s), (5, peak_s)):
        row = jnp.zeros((4, LANES), jnp.float32)
        for odd, h, g in ((0, 0, 0), (1, 0, 1), (1, 1, 2), (0, 1, 3)):
            part = all_ref[pl.ds(at[h] + 16 * odd + base, 4, stride=32), :]
            if g != 1:
                part = pltpu.roll(part, (32 * g - 32) % LANES, 1)
            row = jnp.where(small // 32 == g, part, row)
        target[32:LAY] = row
    wide = lane_of((8, LANES))
    outer = (wide < 3 * EDGE) | (wide >= LANES - 3 * EDGE)
    for j in range(4):
        both = all_ref[pl.ds(4 + j, 8, stride=16), :] + all_ref[pl.ds(12 + j, 8, stride=16), :]
        halo_s[pl.ds(j, 8, stride=4), :] = jnp.where(outer, both, 0.0)
    from_left = all_ref[pl.ds(at[0] + 6, 4, stride=32), :]
    from_right = all_ref[pl.ds(at[1] + 6, 4, stride=32), :]
    from_left = pltpu.roll(from_left, 32, 1)
    from_right = pltpu.roll(from_right, 96, 1)
    halo_s[32:LAY] = jnp.where(
        small >= LANES - 3 * EDGE, from_left, jnp.where(small < 3 * EDGE, from_right, 0.0)
    )

    halo = halo_s[...]

    def unpack(n):
        low_part = pltpu.roll(halo, (LANES - EDGE * n) % LANES, 1) if n else halo
        high_part = pltpu.roll(halo, EDGE * n, 1) if n else halo
        return jnp.where(
            lane < EDGE, low_part, jnp.where(lane >= LANES - EDGE, high_part, 0.0)
        )

    peak = peak_s[...]
    heat = (heat_s[...], unpack(0))
    cond = (cond_s[...], unpack(1))
    field = (temp_s[...], unpack(2))
    scale = [1.0 / (4.0 * k + SINK) for k in cond]
    heat = [x * y for x, y in zip(heat, scale)]
    cond = [x * y for x, y in zip(cond, scale)]
    rows = row_of((FIELD_ROWS, LANES))
    valid = rows < LAY
    first, final = lane == 0, lane == LANES - 1
    for _ in range(SWEEPS):
        right = [pltpu.roll(x, 1, 1) for x in field]
        left = [pltpu.roll(x, LANES - 1, 1) for x in field]
        new = []
        for i in range(2):
            beside = jnp.where(first, right[1 - i], right[i]) + jnp.where(final, left[1 - i], left[i])
            beside = beside + pltpu.roll(field[i], 1, 0) + pltpu.roll(field[i], FIELD_ROWS - 1, 0)
            new.append(jnp.where(valid, heat[i] + cond[i] * beside, 0.0))
        field = new
    field_s[...] = field[0]
    copies = [
        pltpu.make_async_copy(field_s.at[0:LAY], field_hbm, sem.at[0]),
        pltpu.make_async_copy(peak_s.at[0:LAY], peak_hbm, sem.at[1]),
    ]
    for copy in copies:
        copy.start()
    region = region_s[...]
    stiff = jnp.zeros((FIELD_ROWS, LANES), jnp.float32)
    for r in range(NREG):
        stiff = jnp.where(region == r, stiff_ref[0:1, r : r + 1], stiff)
    factor = stiff * jnp.exp(-0.5 * field[0])
    size = LAY // GROUPS
    for group in range(GROUPS):
        for l in range(group * size, (group + 1) * size):
            soft = jnp.tanh((peak[l : l + 1] - energy_ref[l]) * 0.25)
            out_s[l] = (factor[l : l + 1] * (1.0 - 0.5 * soft)).astype(jnp.bfloat16)
        where = pl.ds(group * size, size)
        copy = pltpu.make_async_copy(out_s.at[where], out_hbm.at[where], sem.at[2 + group])
        copy.start()
        copies.append(copy)
    for copy in copies:
        copy.wait()


def soften(everything, energy, region, temp, cond, stiff):
    vmem = pl.BlockSpec(memory_space=pltpu.VMEM)
    plane = pltpu.VMEM((FIELD_ROWS, LANES), jnp.float32)
    return pl.pallas_call(
        modulus_kernel,
        name="modulus",
        out_shape=[
            jax.ShapeDtypeStruct((LAY, LANES), jnp.float32),
            jax.ShapeDtypeStruct((LAY, LANES), jnp.float32),
            jax.ShapeDtypeStruct((LAY, SEC, LANES), jnp.bfloat16),
        ],
        in_specs=[vmem] * 6,
        out_specs=[pl.BlockSpec(memory_space=pl.ANY)] * 3,
        scratch_shapes=[
            plane, plane, plane, plane, plane,
            pltpu.VMEM((FIELD_ROWS, LANES), jnp.int32),
            plane,
            pltpu.VMEM((LAY, SEC, LANES), jnp.bfloat16),
            pltpu.SemaphoreType.DMA((2 + GROUPS,)),
        ],
        compiler_params=pltpu.CompilerParams(vmem_limit_bytes=32 * 2**20),
    )(everything, energy, region, temp, cond, stiff)


def per_device(sects, w, strain, region, prior, temp, cond, loss, mullins, stiff):
    send, energy = project(strain.transpose(0, 2, 1, 3))
    recv = lax.all_to_all(send, "circ", 0, 0, tiled=True)
    own, msg = owner(
        recv.reshape(CIRC * ROWS, LANES), w, region, prior, temp, cond, loss, mullins.reshape(1, NREG)
    )
    pairs = []
    for s in range(1, sects):
        for c in range(s % 2, CIRC, 2):
            here = c * sects + s
            pairs += [(here, here - 1), (here - 1, here)]
    halo = lax.ppermute(msg, ("circ", "sect"), pairs)
    block = jnp.broadcast_to((own + halo)[None], (CIRC, 8, LANES))
    everything = lax.all_to_all(block, "circ", 0, 0, tiled=True)
    field, peak, modulus = soften(
        everything.reshape(CIRC * 8, LANES), energy, region, temp, cond, stiff.reshape(1, NREG)
    )
    return field, peak, modulus.transpose(1, 0, 2)


def solution(mesh):
    w = combine_matrix()
    maps = P(None, "sect")

    def whole(*args):
        return jax.shard_map(
            functools.partial(per_device, mesh.shape["sect"], jnp.asarray(w)),
            mesh=mesh,
            in_specs=(P("circ", None, None, "sect"), maps, maps, maps, maps, P(), P(), P()),
            out_specs=(maps, maps, P("circ", None, "sect")),
            check_vma=False,
        )(*args)

    return whole
```

```python
import functools
import math

import jax
import jax.numpy as jnp
import ml_dtypes
import numpy as np
from jax import lax
from jax.experimental import pallas as pl
from jax.experimental.pallas import tpu as pltpu
from jax.sharding import PartitionSpec as P

COMP = 2
HARM = 8
SWEEPS = 4
SINK = 0.1
SEC = 128
LAY = 36
LANES = 128
NREG = 8
CIRC = 16
NSEC = SEC * CIRC
RANK = 10
ROWS = 48
EDGE = 4
FIELD_ROWS = 40


def combine_matrix():
    half = 0.5 * (SEC - 1) * 2.0 * math.pi / NSEC
    nodes = 64
    n = (np.arange(nodes) + 0.5) * math.pi / nodes
    even = np.zeros((HARM, RANK))
    odd = np.zeros((HARM, RANK))
    for k in range(1, HARM + 1):
        for m in range(RANK):
            weight = (1.0 if m == 0 else 2.0) / nodes
            f = np.cos(k * half * np.cos(n)) if m % 2 == 0 else np.sin(k * half * np.cos(n))
            (even if m % 2 == 0 else odd)[k - 1, m] = weight * np.sum(f * np.cos(m * n))
    u = np.zeros((2 * HARM, CIRC, RANK))
    for d in range(CIRC):
        centre = 2.0 * math.pi * (SEC * d + 0.5 * (SEC - 1)) / NSEC
        for k in range(1, HARM + 1):
            c, s = math.cos(k * centre), math.sin(k * centre)
            u[k - 1, d] = c * even[k - 1] - s * odd[k - 1]
            u[HARM + k - 1, d] = s * even[k - 1] + c * odd[k - 1]
    u = u / math.sqrt(NSEC)
    w = np.zeros((128, CIRC, ROWS))
    for a in range(2):
        for comp in range(COMP):
            at = 20 * a + RANK * comp
            w[32 * a + 16 * comp : 32 * a + 16 * comp + 16, :, at : at + RANK] = u
    for b in range(4):
        first = 5 * (b % 2)
        w[64 + 16 * b : 64 + 16 * b + 16, :, 40:45] = u[:, :, first : first + 5]
    w = w.reshape(128, CIRC * ROWS)
    hi = w.astype(ml_dtypes.bfloat16)
    lo = (w - hi.astype(np.float64)).astype(ml_dtypes.bfloat16)
    return np.concatenate([hi, lo])


def lane_of(shape):
    return lax.broadcasted_iota(jnp.int32, shape, len(shape) - 1)


def row_of(shape):
    return lax.broadcasted_iota(jnp.int32, shape, 0)


def halves(first, second):
    low = lane_of(first.shape) < 64
    return (
        jnp.where(low, first, pltpu.roll(second, 64, 1)),
        jnp.where(low, pltpu.roll(first, 64, 1), second),
    )


def quarter_of(u, h):
    return 3 * h if u % 2 == 0 else 1 + h


def window_matrix():
    wide = (1, SEC * COMP)
    lane = lane_of(wide)
    t = ((lane % SEC).astype(jnp.float32) - 0.5 * (SEC - 1)) * (2.0 / (SEC - 1))
    basis = [jnp.ones(wide, jnp.float32), t]
    for _ in range(RANK - 2):
        basis.append(2.0 * t * basis[-1] - basis[-2])
    rows = [
        jnp.where(lane // SEC == comp, values, 0.0) for comp in range(COMP) for values in basis
    ]
    sub = row_of((8, SEC * COMP))
    parts = []
    for places in (
        range(20),
        range(4, 24),
        [8 * b + i for b in range(4) for i in range(5)],
    ):
        tiles = {}
        for place, row in zip(places, rows):
            tile = tiles.get(place // 8, jnp.zeros((8, SEC * COMP), jnp.float32))
            tiles[place // 8] = jnp.where(sub == place % 8, row, tile)
        rest = jnp.concatenate([tiles[i] for i in sorted(tiles)])
        for _ in range(3):
            part = rest.astype(jnp.bfloat16).astype(jnp.float32)
            parts.append(part)
            rest = rest - part
    return jnp.concatenate(parts).astype(jnp.bfloat16)


TAIL = 8
ORDER = ((TAIL, 0, 1), (2, 3, 4), (5, 6, 7))


def project_kernel(strain_hbm, send_ref, energy_ref, buf, a_ref, sem):
    copies = {}
    for group in ORDER:
        for u in group:
            copies[u] = pltpu.make_async_copy(
                strain_hbm.at[:, pl.ds(4 * u, 4)], buf.at[u], sem.at[u]
            )
            copies[u].start()
    rows = buf.reshape(LAY // 4, SEC * 4 * COMP, LANES)
    parity = lax.axis_index("sect") % 2
    tops = {}
    sums = {}
    tails = {}
    sub = row_of((8, LANES))
    block = lane_of((8, LANES)) // 32

    def pair(t):
        kind = 2 if t >= 16 else t % 2
        size = 32 if kind == 2 else 24
        base = 72 * kind
        first = 4 * (t % 2)
        x = [
            [rows[t // 2, pl.ds(first + COMP * i + c, SEC, stride=4 * COMP), :] for i in range(2)]
            for c in range(COMP)
        ]
        wide = jnp.concatenate([jnp.concatenate(both, axis=1) for both in x])
        d = jnp.dot(a_ref[base : base + 3 * size], wide, preferred_element_type=jnp.float32)
        d = d[:size] + d[size : 2 * size] + d[2 * size :]
        for i in range(2):
            l = 2 * t + i
            c0 = x[0][i].astype(jnp.float32)
            c1 = x[1][i].astype(jnp.float32)
            e = c0 * c0 + c1 * c1
            energy_ref[l] = e
            tops[l] = jnp.max(e, axis=0, keepdims=True)
            sums[l] = d[:, LANES * i : LANES * (i + 1)]

    def pack_tail():
        for v in range(4):
            x = sums[32 + v]
            shifted = []
            for delta in range(4):
                w = jnp.zeros((8, LANES), jnp.float32)
                for b in range(4):
                    w = jnp.where(block == (b - delta) % 4, x[8 * b : 8 * b + 8], w)
                shifted.append(pltpu.roll(w, 32 * delta, 1) if delta else w)
            for g in range(4):
                y = shifted[0]
                for b in range(4):
                    y = jnp.where(block == b, shifted[(b - g) % 4], y)
                top = tops[32 + v]
                if g:
                    top = pltpu.roll(top, LANES - 32 * g, 1)
                tails[v, g] = jnp.where(sub == 7, top, y)

    def pack(u):
        first = halves(sums[4 * u], sums[4 * u + 1])
        second = halves(sums[4 * u + 2], sums[4 * u + 3])
        top0 = halves(tops[4 * u], tops[4 * u + 1])
        top1 = halves(tops[4 * u + 2], tops[4 * u + 3])
        for h in range(2):
            c = 2 * u + (h + parity) % 2
            send_ref[c, 0:16] = first[h][0:16]
            send_ref[c, 16:24] = first[h][16:24] + second[h][0:8]
            send_ref[c, 24:40] = second[h][8:24]
            tile = jnp.where(sub == 5, top0[h], tails[u // 2, quarter_of(u, h)])
            send_ref[c, 40:48] = jnp.where(sub == 6, top1[h], tile)

    a_ref[...] = window_matrix()
    waiting = []
    for group in ORDER:
        for u in group:
            copies[u].wait()
        for u in group:
            pair(2 * u)
            pair(2 * u + 1)
        for u in waiting:
            pack_tail() if u == TAIL else pack(u)
        waiting = group
    for u in waiting:
        pack_tail() if u == TAIL else pack(u)


def project(strain):
    return pl.pallas_call(
        project_kernel,
        name="project",
        out_shape=[
            jax.ShapeDtypeStruct((CIRC, ROWS, LANES), jnp.float32),
            jax.ShapeDtypeStruct((LAY, SEC, LANES), jnp.float32),
        ],
        in_specs=[pl.BlockSpec(memory_space=pl.ANY)],
        out_specs=[pl.BlockSpec(memory_space=pltpu.VMEM)] * 2,
        scratch_shapes=[
            pltpu.VMEM((LAY // 4, SEC, 4, COMP, LANES), jnp.bfloat16),
            pltpu.VMEM((240, SEC * COMP), jnp.bfloat16),
            pltpu.SemaphoreType.DMA((LAY // 4,)),
        ],
        compiler_params=pltpu.CompilerParams(vmem_limit_bytes=50 * 2**20),
    )(strain)


def owner_kernel(
    recv_ref, w_ref, region_ref, prior_ref, temp_ref, cond_ref, loss_ref, mullins_ref, own_ref, msg_ref
):
    c = lax.axis_index("circ")
    u = c // 2
    h = (c + lax.axis_index("sect")) % 2
    is_left = h == 0
    lane = lane_of((1, LANES))
    sub = row_of((8, LANES))
    p = recv_ref[...]
    hi = p.astype(jnp.bfloat16)
    lo = (p - hi.astype(jnp.float32)).astype(jnp.bfloat16)
    o = jnp.dot(
        w_ref[...], jnp.concatenate([hi, lo], axis=1), preferred_element_type=jnp.float32
    )
    coeffs = o[:128, :LANES] + o[128:, :LANES] + o[:128, LANES:]
    squared = coeffs[:64] * coeffs[:64]
    powers = [
        squared[32 * a : 32 * a + 8]
        + squared[32 * a + 8 : 32 * a + 16]
        + squared[32 * a + 16 : 32 * a + 24]
        + squared[32 * a + 24 : 32 * a + 32]
        for a in range(2)
    ]
    last = [coeffs[64 + 16 * b : 80 + 16 * b] for b in range(4)]
    comp0 = last[0] + pltpu.roll(last[1], 96, 1)
    comp1 = pltpu.roll(last[2], 64, 1) + pltpu.roll(last[3], 32, 1)
    comp0, comp1 = comp0 * comp0, comp1 * comp1
    powers.append(comp0[:8] + comp0[8:] + comp1[:8] + comp1[8:])

    quarter = jnp.where(u % 2 == 0, 3 * h, 1 + h)
    back = (LANES - 32 * quarter) % LANES

    def natural(ref):
        rows = [ref[pl.ds(4 * u + j, 1), :] for j in range(4)]
        rows.append(ref[pl.ds(32 + u // 2, 1), :])
        return rows

    def packed(rows):
        out = []
        for a in range(2):
            left, right = halves(rows[2 * a], rows[2 * a + 1])
            out.append(jnp.where(is_left, left, right))
        out.append(pltpu.roll(rows[4], back, 1))
        return out

    region = packed(natural(region_ref))
    prior = packed(natural(prior_ref))
    temp_rows = natural(temp_ref)
    temp = packed(temp_rows)
    cond_rows = natural(cond_ref)
    heats, peaks = [], []
    for i in range(3):
        q = loss_ref[:, 0:1] * powers[i][0:1]
        for k in range(1, HARM):
            q = q + loss_ref[:, k : k + 1] * powers[i][k : k + 1]
        picked = jnp.sum(jnp.where(region[i] == sub, q, 0.0), axis=0, keepdims=True)
        share = jnp.zeros((1, LANES), jnp.float32)
        for r in range(NREG):
            share = jnp.where(region[i] == r, mullins_ref[0:1, r : r + 1], share)
        top = jnp.max(recv_ref[pl.ds(45 + i, CIRC, stride=ROWS), :], axis=0, keepdims=True)
        peak = jnp.maximum(prior[i], top)
        heats.append(jnp.exp(-0.5 * temp[i]) * picked + share * (peak - prior[i]))
        peaks.append(peak)

    third = (lane >= 32) & (lane < 64)
    own = jnp.where(sub == 0, heats[0], 0.0)
    own = jnp.where(sub == 1, heats[1], own)
    own = jnp.where(sub == 2, peaks[0], own)
    own = jnp.where(sub == 3, peaks[1], own)
    own = jnp.where((sub == 4) & third, pltpu.roll(heats[2], 32, 1), own)
    own_ref[...] = jnp.where((sub == 5) & third, pltpu.roll(peaks[2], 32, 1), own)

    edge_heat = []
    for a in range(2):
        turned = pltpu.roll(heats[a], 64, 1)
        edge_heat.append(jnp.where(is_left, heats[a], turned))
        edge_heat.append(jnp.where(is_left, turned, heats[a]))
    edge_heat.append(jnp.where(is_left, heats[2], pltpu.roll(heats[2], 96, 1)))
    edge = jnp.where(is_left, lane, LANES - 1 - lane) < EDGE
    step = jnp.where(is_left, EDGE, LANES - EDGE)
    msg = jnp.zeros((8, LANES), jnp.float32)
    for j in range(5):
        row = jnp.where(edge, edge_heat[j], 0.0)
        row = row + pltpu.roll(jnp.where(edge, cond_rows[j], 0.0), step, 1)
        row = row + pltpu.roll(jnp.where(edge, temp_rows[j], 0.0), (2 * step) % LANES, 1)
        if j < 4:
            msg = msg + jnp.where(sub == 4 + j, row, 0.0)
        else:
            row = pltpu.roll(row, jnp.where(is_left, 32, 96), 1)
            msg = msg + jnp.where(sub == 6, row, 0.0)
    msg_ref[...] = msg


def owner(recv, w, region, prior, temp, cond, loss, mullins):
    vmem = pl.BlockSpec(memory_space=pltpu.VMEM)
    return pl.pallas_call(
        owner_kernel,
        name="owner",
        out_shape=[jax.ShapeDtypeStruct((8, LANES), jnp.float32)] * 2,
        in_specs=[vmem] * 8,
        out_specs=[vmem] * 2,
        compiler_params=pltpu.CompilerParams(vmem_limit_bytes=32 * 2**20),
    )(recv, w, region, prior, temp, cond, loss, mullins)


GROUPS = 6
EARLY = 12


def modulus_kernel(
    all_ref, energy_ref, region_ref, temp_ref, cond_ref, stiff_ref,
    field_hbm, peak_hbm, out_hbm,
    heat_s, peak_s, halo_s, cond_s, temp_s, region_s, field_s, soft_s, out_s, sem,
):
    low = lane_of((8, LANES)) < 64
    lane = lane_of((FIELD_ROWS, LANES))
    parity = lax.axis_index("sect") % 2
    at = [8 * parity, 8 * (1 - parity)]
    for scratch in (heat_s, peak_s, halo_s, cond_s, temp_s):
        scratch[32:FIELD_ROWS] = jnp.zeros((8, LANES), jnp.float32)
    region_s[32:FIELD_ROWS] = jnp.zeros((8, LANES), jnp.int32)
    cond_s[0:LAY] = cond_ref[...]
    temp_s[0:LAY] = temp_ref[...]
    region_s[0:LAY] = region_ref[...]
    for a in range(2):
        for base, target in ((0, heat_s), (2, peak_s)):
            left = all_ref[pl.ds(at[0] + base + a, 8, stride=16), :]
            right = all_ref[pl.ds(at[1] + base + a, 8, stride=16), :]
            target[pl.ds(2 * a, 8, stride=4), :] = jnp.where(low, left, pltpu.roll(right, 64, 1))
            target[pl.ds(2 * a + 1, 8, stride=4), :] = jnp.where(low, pltpu.roll(left, 64, 1), right)
    small = lane_of((4, LANES))
    for base, target in ((4, heat_s), (5, peak_s)):
        row = jnp.zeros((4, LANES), jnp.float32)
        for odd, h, g in ((0, 0, 0), (1, 0, 1), (1, 1, 2), (0, 1, 3)):
            part = all_ref[pl.ds(at[h] + 16 * odd + base, 4, stride=32), :]
            if g != 1:
                part = pltpu.roll(part, (32 * g - 32) % LANES, 1)
            row = jnp.where(small // 32 == g, part, row)
        target[32:LAY] = row
    wide = lane_of((8, LANES))
    outer = (wide < 3 * EDGE) | (wide >= LANES - 3 * EDGE)
    for j in range(4):
        both = all_ref[pl.ds(4 + j, 8, stride=16), :] + all_ref[pl.ds(12 + j, 8, stride=16), :]
        halo_s[pl.ds(j, 8, stride=4), :] = jnp.where(outer, both, 0.0)
    from_left = all_ref[pl.ds(at[0] + 6, 4, stride=32), :]
    from_right = all_ref[pl.ds(at[1] + 6, 4, stride=32), :]
    from_left = pltpu.roll(from_left, 32, 1)
    from_right = pltpu.roll(from_right, 96, 1)
    halo_s[32:LAY] = jnp.where(
        small >= LANES - 3 * EDGE, from_left, jnp.where(small < 3 * EDGE, from_right, 0.0)
    )

    peak = peak_s[...]
    halo = halo_s[...]

    def unpack(n):
        low_part = pltpu.roll(halo, (LANES - EDGE * n) % LANES, 1) if n else halo
        high_part = pltpu.roll(halo, EDGE * n, 1) if n else halo
        return jnp.where(
            lane < EDGE, low_part, jnp.where(lane >= LANES - EDGE, high_part, 0.0)
        )

    heat = (heat_s[...], unpack(0))
    cond = (cond_s[...], unpack(1))
    field = (temp_s[...], unpack(2))
    scale = [1.0 / (4.0 * k + SINK) for k in cond]
    heat = [x * y for x, y in zip(heat, scale)]
    cond = [x * y for x, y in zip(cond, scale)]
    rows = row_of((FIELD_ROWS, LANES))
    valid = rows < LAY
    first, final = lane == 0, lane == LANES - 1
    for _ in range(SWEEPS):
        right = [pltpu.roll(x, 1, 1) for x in field]
        left = [pltpu.roll(x, LANES - 1, 1) for x in field]
        new = []
        for i in range(2):
            beside = jnp.where(first, right[1 - i], right[i]) + jnp.where(final, left[1 - i], left[i])
            beside = beside + pltpu.roll(field[i], 1, 0) + pltpu.roll(field[i], FIELD_ROWS - 1, 0)
            new.append(jnp.where(valid, heat[i] + cond[i] * beside, 0.0))
        field = new
    for l in range(EARLY):
        soft_s[l] = 1.0 - 0.5 * jnp.tanh((peak[l : l + 1] - energy_ref[l]) * 0.25)
    field_s[...] = field[0]
    copies = [
        pltpu.make_async_copy(field_s.at[0:LAY], field_hbm, sem.at[0]),
        pltpu.make_async_copy(peak_s.at[0:LAY], peak_hbm, sem.at[1]),
    ]
    for copy in copies:
        copy.start()
    region = region_s[...]
    stiff = jnp.zeros((FIELD_ROWS, LANES), jnp.float32)
    for r in range(NREG):
        stiff = jnp.where(region == r, stiff_ref[0:1, r : r + 1], stiff)
    factor = stiff * jnp.exp(-0.5 * field[0])
    size = LAY // GROUPS
    for group in range(GROUPS):
        for l in range(group * size, (group + 1) * size):
            if l < EARLY:
                soft = soft_s[l]
            else:
                soft = 1.0 - 0.5 * jnp.tanh((peak[l : l + 1] - energy_ref[l]) * 0.25)
            out_s[l] = (factor[l : l + 1] * soft).astype(jnp.bfloat16)
        where = pl.ds(group * size, size)
        copy = pltpu.make_async_copy(out_s.at[where], out_hbm.at[where], sem.at[2 + group])
        copy.start()
        copies.append(copy)
    for copy in copies:
        copy.wait()


def soften(everything, energy, region, temp, cond, stiff):
    vmem = pl.BlockSpec(memory_space=pltpu.VMEM)
    plane = pltpu.VMEM((FIELD_ROWS, LANES), jnp.float32)
    return pl.pallas_call(
        modulus_kernel,
        name="modulus",
        out_shape=[
            jax.ShapeDtypeStruct((LAY, LANES), jnp.float32),
            jax.ShapeDtypeStruct((LAY, LANES), jnp.float32),
            jax.ShapeDtypeStruct((LAY, SEC, LANES), jnp.bfloat16),
        ],
        in_specs=[vmem] * 6,
        out_specs=[pl.BlockSpec(memory_space=pl.ANY)] * 3,
        scratch_shapes=[
            plane, plane, plane, plane, plane,
            pltpu.VMEM((FIELD_ROWS, LANES), jnp.int32),
            plane,
            pltpu.VMEM((EARLY, SEC, LANES), jnp.float32),
            pltpu.VMEM((LAY, SEC, LANES), jnp.bfloat16),
            pltpu.SemaphoreType.DMA((2 + GROUPS,)),
        ],
        compiler_params=pltpu.CompilerParams(vmem_limit_bytes=32 * 2**20),
    )(everything, energy, region, temp, cond, stiff)


def per_device(sects, w, strain, region, prior, temp, cond, loss, mullins, stiff):
    send, energy = project(strain.transpose(0, 2, 1, 3))
    recv = lax.all_to_all(send, "circ", 0, 0, tiled=True)
    own, msg = owner(
        recv.reshape(CIRC * ROWS, LANES), w, region, prior, temp, cond, loss, mullins.reshape(1, NREG)
    )
    pairs = []
    for s in range(1, sects):
        for c in range(s % 2, CIRC, 2):
            here = c * sects + s
            pairs += [(here, here - 1), (here - 1, here)]
    halo = lax.ppermute(msg, ("circ", "sect"), pairs)
    block = jnp.broadcast_to((own + halo)[None], (CIRC, 8, LANES))
    everything = lax.all_to_all(block, "circ", 0, 0, tiled=True)
    field, peak, modulus = soften(
        everything.reshape(CIRC * 8, LANES), energy, region, temp, cond, stiff.reshape(1, NREG)
    )
    return field, peak, modulus.transpose(1, 0, 2)


def solution(mesh):
    w = combine_matrix()
    maps = P(None, "sect")

    def whole(*args):
        return jax.shard_map(
            functools.partial(per_device, mesh.shape["sect"], jnp.asarray(w)),
            mesh=mesh,
            in_specs=(P("circ", None, None, "sect"), maps, maps, maps, maps, P(), P(), P()),
            out_specs=(maps, maps, P("circ", None, "sect")),
            check_vma=False,
        )(*args)

    return whole
```

```python
import functools
import math

import jax
import jax.numpy as jnp
import ml_dtypes
import numpy as np
from jax import lax
from jax.experimental import pallas as pl
from jax.experimental.pallas import tpu as pltpu
from jax.sharding import PartitionSpec as P

COMP = 2
HARM = 8
SWEEPS = 4
SINK = 0.1
SEC = 128
LAY = 36
LANES = 128
NREG = 8
CIRC = 16
NSEC = SEC * CIRC
RANK = 9
ROWS = 44
QUAD = 4
PADDED = 768
EDGE = 4
FIELD_ROWS = 40


def combine_matrix():
    half = 0.5 * (SEC - 1) * 2.0 * math.pi / NSEC
    nodes = 64
    n = (np.arange(nodes) + 0.5) * math.pi / nodes
    even = np.zeros((HARM, RANK))
    odd = np.zeros((HARM, RANK))
    for k in range(1, HARM + 1):
        for m in range(RANK):
            weight = (1.0 if m == 0 else 2.0) / nodes
            f = np.cos(k * half * np.cos(n)) if m % 2 == 0 else np.sin(k * half * np.cos(n))
            (even if m % 2 == 0 else odd)[k - 1, m] = weight * np.sum(f * np.cos(m * n))
    u = np.zeros((2 * HARM, CIRC, RANK))
    for d in range(CIRC):
        centre = 2.0 * math.pi * (SEC * d + 0.5 * (SEC - 1)) / NSEC
        for k in range(1, HARM + 1):
            c, s = math.cos(k * centre), math.sin(k * centre)
            u[k - 1, d] = c * even[k - 1] - s * odd[k - 1]
            u[HARM + k - 1, d] = s * even[k - 1] + c * odd[k - 1]
    u = u / math.sqrt(NSEC)
    w = np.zeros((128, CIRC, ROWS))
    for a in range(2):
        for comp in range(COMP):
            at = RANK * (COMP * a + comp)
            w[32 * a + 16 * comp : 32 * a + 16 * comp + 16, :, at : at + RANK] = u
    for b in range(4):
        part = u[:, :, 5 * (b % 2) : 5 * (b % 2) + 5]
        w[64 + 16 * b : 64 + 16 * b + 16, :, 36 : 36 + part.shape[2]] = part
    w = np.pad(w.reshape(128, CIRC * ROWS), ((0, 0), (0, PADDED - CIRC * ROWS)))
    hi = w.astype(ml_dtypes.bfloat16)
    lo = (w - hi.astype(np.float64)).astype(ml_dtypes.bfloat16)
    return np.concatenate([hi, lo])


def lane_of(shape):
    return lax.broadcasted_iota(jnp.int32, shape, len(shape) - 1)


def row_of(shape):
    return lax.broadcasted_iota(jnp.int32, shape, 0)


def halves(first, second):
    low = lane_of(first.shape) < 64
    return (
        jnp.where(low, first, pltpu.roll(second, 64, 1)),
        jnp.where(low, pltpu.roll(first, 64, 1), second),
    )


def quarter_of(u, h):
    return 3 * h if u % 2 == 0 else 1 + h


def window_matrix():
    wide = (1, SEC * COMP)
    lane = lane_of(wide)
    t = ((lane % SEC).astype(jnp.float32) - 0.5 * (SEC - 1)) * (2.0 / (SEC - 1))
    basis = [jnp.ones(wide, jnp.float32), t]
    for _ in range(RANK - 2):
        basis.append(2.0 * t * basis[-1] - basis[-2])
    rows = [
        jnp.where(lane // SEC == comp, values, 0.0) for comp in range(COMP) for values in basis
    ]
    sub = row_of((8, SEC * COMP))
    parts = []
    for places in (
        range(18),
        range(2, 20),
        [8 * b + (i + 4) % 8 for b in range(4) for i in range(5 - b % 2)],
    ):
        tiles = {}
        for place, row in zip(places, rows):
            tile = tiles.get(place // 8, jnp.zeros((8, SEC * COMP), jnp.float32))
            tiles[place // 8] = jnp.where(sub == place % 8, row, tile)
        rest = jnp.concatenate([tiles[i] for i in sorted(tiles)])
        for _ in range(3):
            part = rest.astype(jnp.bfloat16).astype(jnp.float32)
            parts.append(part)
            rest = rest - part
    return jnp.concatenate(parts).astype(jnp.bfloat16)


TAIL = 8
ORDER = ((TAIL, 0, 1), (2, 3, 4), (5, 6, 7))


def project_kernel(strain_hbm, send_ref, energy_ref, buf, a_ref, sem):
    copies = {}
    for group in ORDER:
        for u in group:
            copies[u] = pltpu.make_async_copy(
                strain_hbm.at[:, pl.ds(4 * u, 4)], buf.at[u], sem.at[u]
            )
            copies[u].start()
    rows = buf.reshape(LAY // 4, SEC * 4 * COMP, LANES)
    send = send_ref.reshape(CIRC, ROWS, LANES)
    parity = lax.axis_index("sect") % 2
    tops = {}
    sums = {}
    tails = {}
    sub = row_of((8, LANES))
    block = lane_of((8, LANES)) // 32

    def pair(t):
        kind = 2 if t >= 16 else t % 2
        size = 32 if kind == 2 else 24
        base = 72 * kind
        first = 4 * (t % 2)
        x = [
            [rows[t // 2, pl.ds(first + COMP * i + c, SEC, stride=4 * COMP), :] for i in range(2)]
            for c in range(COMP)
        ]
        wide = jnp.concatenate([jnp.concatenate(both, axis=1) for both in x])
        d = jnp.dot(a_ref[base : base + 3 * size], wide, preferred_element_type=jnp.float32)
        d = d[:size] + d[size : 2 * size] + d[2 * size :]
        for i in range(2):
            l = 2 * t + i
            c0 = x[0][i].astype(jnp.float32)
            c1 = x[1][i].astype(jnp.float32)
            e = c0 * c0 + c1 * c1
            energy_ref[l] = e
            tops[l] = jnp.max(e, axis=0, keepdims=True)
            sums[l] = d[:, LANES * i : LANES * (i + 1)]

    def pack_tail():
        for v in range(4):
            x = sums[32 + v]
            shifted = []
            for delta in range(4):
                w = jnp.zeros((8, LANES), jnp.float32)
                for b in range(4):
                    w = jnp.where(block == (b - delta) % 4, x[8 * b : 8 * b + 8], w)
                shifted.append(pltpu.roll(w, 32 * delta, 1) if delta else w)
            for g in range(4):
                y = shifted[0]
                for b in range(4):
                    y = jnp.where(block == b, shifted[(b - g) % 4], y)
                top = tops[32 + v]
                if g:
                    top = pltpu.roll(top, LANES - 32 * g, 1)
                tails[v, g] = jnp.where(sub == 3, top, y)

    def pack(u):
        first = halves(sums[4 * u], sums[4 * u + 1])
        second = halves(sums[4 * u + 2], sums[4 * u + 3])
        top0 = halves(tops[4 * u], tops[4 * u + 1])
        top1 = halves(tops[4 * u + 2], tops[4 * u + 3])
        for h in range(2):
            c = 2 * u + (h + parity) % 2
            tail = tails[u // 2, quarter_of(u, h)]
            send[c, 0:16] = first[h][0:16]
            send[c, 16:24] = first[h][16:24] + second[h][0:8]
            send[c, 24:32] = second[h][8:16]
            send[c, 32:40] = jnp.where(sub < 4, second[h][16:24], tail)
            tile = jnp.where(sub == 1, top0[h], tail)
            send[c, 40:44] = jnp.where(sub == 2, top1[h], tile)[0:4]

    a_ref[...] = window_matrix()
    waiting = []
    for group in ORDER:
        for u in group:
            copies[u].wait()
        for u in group:
            pair(2 * u)
            pair(2 * u + 1)
        for u in waiting:
            pack_tail() if u == TAIL else pack(u)
        waiting = group
    for u in waiting:
        pack_tail() if u == TAIL else pack(u)


def project(strain):
    return pl.pallas_call(
        project_kernel,
        name="project",
        out_shape=[
            jax.ShapeDtypeStruct((CIRC, ROWS // QUAD, QUAD, LANES), jnp.float32),
            jax.ShapeDtypeStruct((LAY, SEC, LANES), jnp.float32),
        ],
        in_specs=[pl.BlockSpec(memory_space=pl.ANY)],
        out_specs=[pl.BlockSpec(memory_space=pltpu.VMEM)] * 2,
        scratch_shapes=[
            pltpu.VMEM((LAY // 4, SEC, 4, COMP, LANES), jnp.bfloat16),
            pltpu.VMEM((240, SEC * COMP), jnp.bfloat16),
            pltpu.SemaphoreType.DMA((LAY // 4,)),
        ],
        compiler_params=pltpu.CompilerParams(vmem_limit_bytes=50 * 2**20),
    )(strain)


def owner_kernel(
    recv_ref, w_ref, region_ref, prior_ref, temp_ref, cond_ref, loss_ref, mullins_ref, own_ref, msg_ref
):
    c = lax.axis_index("circ")
    u = c // 2
    h = (c + lax.axis_index("sect")) % 2
    is_left = h == 0
    lane = lane_of((1, LANES))
    sub = row_of((8, LANES))
    recv = recv_ref.reshape(CIRC * ROWS, LANES)
    p = jnp.concatenate([recv[...], jnp.zeros((PADDED - CIRC * ROWS, LANES), jnp.float32)])
    hi = p.astype(jnp.bfloat16)
    lo = (p - hi.astype(jnp.float32)).astype(jnp.bfloat16)
    o = jnp.dot(
        w_ref[...], jnp.concatenate([hi, lo], axis=1), preferred_element_type=jnp.float32
    )
    coeffs = o[:128, :LANES] + o[128:, :LANES] + o[:128, LANES:]
    squared = coeffs[:64] * coeffs[:64]
    powers = [
        squared[32 * a : 32 * a + 8]
        + squared[32 * a + 8 : 32 * a + 16]
        + squared[32 * a + 16 : 32 * a + 24]
        + squared[32 * a + 24 : 32 * a + 32]
        for a in range(2)
    ]
    last = [coeffs[64 + 16 * b : 80 + 16 * b] for b in range(4)]
    comp0 = last[0] + pltpu.roll(last[1], 96, 1)
    comp1 = pltpu.roll(last[2], 64, 1) + pltpu.roll(last[3], 32, 1)
    comp0, comp1 = comp0 * comp0, comp1 * comp1
    powers.append(comp0[:8] + comp0[8:] + comp1[:8] + comp1[8:])

    quarter = jnp.where(u % 2 == 0, 3 * h, 1 + h)
    back = (LANES - 32 * quarter) % LANES

    def natural(ref):
        rows = [ref[pl.ds(4 * u + j, 1), :] for j in range(4)]
        rows.append(ref[pl.ds(32 + u // 2, 1), :])
        return rows

    def packed(rows):
        out = []
        for a in range(2):
            left, right = halves(rows[2 * a], rows[2 * a + 1])
            out.append(jnp.where(is_left, left, right))
        out.append(pltpu.roll(rows[4], back, 1))
        return out

    region = packed(natural(region_ref))
    prior = packed(natural(prior_ref))
    temp_rows = natural(temp_ref)
    temp = packed(temp_rows)
    cond_rows = natural(cond_ref)
    heats, peaks = [], []
    for i in range(3):
        q = loss_ref[:, 0:1] * powers[i][0:1]
        for k in range(1, HARM):
            q = q + loss_ref[:, k : k + 1] * powers[i][k : k + 1]
        picked = jnp.sum(jnp.where(region[i] == sub, q, 0.0), axis=0, keepdims=True)
        share = jnp.zeros((1, LANES), jnp.float32)
        for r in range(NREG):
            share = jnp.where(region[i] == r, mullins_ref[0:1, r : r + 1], share)
        top = jnp.max(recv[pl.ds(41 + i, CIRC, stride=ROWS), :], axis=0, keepdims=True)
        peak = jnp.maximum(prior[i], top)
        heats.append(jnp.exp(-0.5 * temp[i]) * picked + share * (peak - prior[i]))
        peaks.append(peak)

    third = (lane >= 32) & (lane < 64)
    own = jnp.where(sub == 0, heats[0], 0.0)
    own = jnp.where(sub == 1, heats[1], own)
    own = jnp.where(sub == 2, peaks[0], own)
    own = jnp.where(sub == 3, peaks[1], own)
    own = jnp.where((sub == 4) & third, pltpu.roll(heats[2], 32, 1), own)
    own_ref[...] = jnp.where((sub == 5) & third, pltpu.roll(peaks[2], 32, 1), own)

    edge_heat = []
    for a in range(2):
        turned = pltpu.roll(heats[a], 64, 1)
        edge_heat.append(jnp.where(is_left, heats[a], turned))
        edge_heat.append(jnp.where(is_left, turned, heats[a]))
    edge_heat.append(jnp.where(is_left, heats[2], pltpu.roll(heats[2], 96, 1)))
    edge = jnp.where(is_left, lane, LANES - 1 - lane) < EDGE
    step = jnp.where(is_left, EDGE, LANES - EDGE)
    msg = jnp.zeros((8, LANES), jnp.float32)
    for j in range(5):
        row = jnp.where(edge, edge_heat[j], 0.0)
        row = row + pltpu.roll(jnp.where(edge, cond_rows[j], 0.0), step, 1)
        row = row + pltpu.roll(jnp.where(edge, temp_rows[j], 0.0), (2 * step) % LANES, 1)
        if j < 4:
            msg = msg + jnp.where(sub == 4 + j, row, 0.0)
        else:
            row = pltpu.roll(row, jnp.where(is_left, 32, 96), 1)
            msg = msg + jnp.where(sub == 6, row, 0.0)
    msg_ref[...] = msg


def owner(recv, w, region, prior, temp, cond, loss, mullins):
    vmem = pl.BlockSpec(memory_space=pltpu.VMEM)
    return pl.pallas_call(
        owner_kernel,
        name="owner",
        out_shape=[jax.ShapeDtypeStruct((8, LANES), jnp.float32)] * 2,
        in_specs=[vmem] * 8,
        out_specs=[vmem] * 2,
        compiler_params=pltpu.CompilerParams(vmem_limit_bytes=32 * 2**20),
    )(recv, w, region, prior, temp, cond, loss, mullins)


GROUPS = 6
EARLY = 12


def modulus_kernel(
    all_ref, energy_ref, region_ref, temp_ref, cond_ref, stiff_ref,
    field_hbm, peak_hbm, out_hbm,
    heat_s, peak_s, halo_s, cond_s, temp_s, region_s, field_s, soft_s, out_s, sem,
):
    low = lane_of((8, LANES)) < 64
    lane = lane_of((FIELD_ROWS, LANES))
    parity = lax.axis_index("sect") % 2
    at = [8 * parity, 8 * (1 - parity)]
    for scratch in (heat_s, peak_s, halo_s, cond_s, temp_s):
        scratch[32:FIELD_ROWS] = jnp.zeros((8, LANES), jnp.float32)
    region_s[32:FIELD_ROWS] = jnp.zeros((8, LANES), jnp.int32)
    cond_s[0:LAY] = cond_ref[...]
    temp_s[0:LAY] = temp_ref[...]
    region_s[0:LAY] = region_ref[...]
    for a in range(2):
        for base, target in ((0, heat_s), (2, peak_s)):
            left = all_ref[pl.ds(at[0] + base + a, 8, stride=16), :]
            right = all_ref[pl.ds(at[1] + base + a, 8, stride=16), :]
            target[pl.ds(2 * a, 8, stride=4), :] = jnp.where(low, left, pltpu.roll(right, 64, 1))
            target[pl.ds(2 * a + 1, 8, stride=4), :] = jnp.where(low, pltpu.roll(left, 64, 1), right)
    small = lane_of((4, LANES))
    for base, target in ((4, heat_s), (5, peak_s)):
        row = jnp.zeros((4, LANES), jnp.float32)
        for odd, h, g in ((0, 0, 0), (1, 0, 1), (1, 1, 2), (0, 1, 3)):
            part = all_ref[pl.ds(at[h] + 16 * odd + base, 4, stride=32), :]
            if g != 1:
                part = pltpu.roll(part, (32 * g - 32) % LANES, 1)
            row = jnp.where(small // 32 == g, part, row)
        target[32:LAY] = row
    wide = lane_of((8, LANES))
    outer = (wide < 3 * EDGE) | (wide >= LANES - 3 * EDGE)
    for j in range(4):
        both = all_ref[pl.ds(4 + j, 8, stride=16), :] + all_ref[pl.ds(12 + j, 8, stride=16), :]
        halo_s[pl.ds(j, 8, stride=4), :] = jnp.where(outer, both, 0.0)
    from_left = all_ref[pl.ds(at[0] + 6, 4, stride=32), :]
    from_right = all_ref[pl.ds(at[1] + 6, 4, stride=32), :]
    from_left = pltpu.roll(from_left, 32, 1)
    from_right = pltpu.roll(from_right, 96, 1)
    halo_s[32:LAY] = jnp.where(
        small >= LANES - 3 * EDGE, from_left, jnp.where(small < 3 * EDGE, from_right, 0.0)
    )

    peak = peak_s[...]
    halo = halo_s[...]

    def unpack(n):
        low_part = pltpu.roll(halo, (LANES - EDGE * n) % LANES, 1) if n else halo
        high_part = pltpu.roll(halo, EDGE * n, 1) if n else halo
        return jnp.where(
            lane < EDGE, low_part, jnp.where(lane >= LANES - EDGE, high_part, 0.0)
        )

    heat = (heat_s[...], unpack(0))
    cond = (cond_s[...], unpack(1))
    field = (temp_s[...], unpack(2))
    scale = [1.0 / (4.0 * k + SINK) for k in cond]
    heat = [x * y for x, y in zip(heat, scale)]
    cond = [x * y for x, y in zip(cond, scale)]
    rows = row_of((FIELD_ROWS, LANES))
    valid = rows < LAY
    first, final = lane == 0, lane == LANES - 1
    for _ in range(SWEEPS):
        right = [pltpu.roll(x, 1, 1) for x in field]
        left = [pltpu.roll(x, LANES - 1, 1) for x in field]
        new = []
        for i in range(2):
            beside = jnp.where(first, right[1 - i], right[i]) + jnp.where(final, left[1 - i], left[i])
            beside = beside + pltpu.roll(field[i], 1, 0) + pltpu.roll(field[i], FIELD_ROWS - 1, 0)
            new.append(jnp.where(valid, heat[i] + cond[i] * beside, 0.0))
        field = new
    for l in range(EARLY):
        soft_s[l] = 1.0 - 0.5 * jnp.tanh((peak[l : l + 1] - energy_ref[l]) * 0.25)
    field_s[...] = field[0]
    copies = [
        pltpu.make_async_copy(field_s.at[0:LAY], field_hbm, sem.at[0]),
        pltpu.make_async_copy(peak_s.at[0:LAY], peak_hbm, sem.at[1]),
    ]
    for copy in copies:
        copy.start()
    region = region_s[...]
    stiff = jnp.zeros((FIELD_ROWS, LANES), jnp.float32)
    for r in range(NREG):
        stiff = jnp.where(region == r, stiff_ref[0:1, r : r + 1], stiff)
    factor = stiff * jnp.exp(-0.5 * field[0])
    size = LAY // GROUPS
    for group in range(GROUPS):
        for l in range(group * size, (group + 1) * size):
            if l < EARLY:
                soft = soft_s[l]
            else:
                soft = 1.0 - 0.5 * jnp.tanh((peak[l : l + 1] - energy_ref[l]) * 0.25)
            out_s[l] = (factor[l : l + 1] * soft).astype(jnp.bfloat16)
        where = pl.ds(group * size, size)
        copy = pltpu.make_async_copy(out_s.at[where], out_hbm.at[where], sem.at[2 + group])
        copy.start()
        copies.append(copy)
    for copy in copies:
        copy.wait()


def soften(everything, energy, region, temp, cond, stiff):
    vmem = pl.BlockSpec(memory_space=pltpu.VMEM)
    plane = pltpu.VMEM((FIELD_ROWS, LANES), jnp.float32)
    return pl.pallas_call(
        modulus_kernel,
        name="modulus",
        out_shape=[
            jax.ShapeDtypeStruct((LAY, LANES), jnp.float32),
            jax.ShapeDtypeStruct((LAY, LANES), jnp.float32),
            jax.ShapeDtypeStruct((LAY, SEC, LANES), jnp.bfloat16),
        ],
        in_specs=[vmem] * 6,
        out_specs=[pl.BlockSpec(memory_space=pl.ANY)] * 3,
        scratch_shapes=[
            plane, plane, plane, plane, plane,
            pltpu.VMEM((FIELD_ROWS, LANES), jnp.int32),
            plane,
            pltpu.VMEM((EARLY, SEC, LANES), jnp.float32),
            pltpu.VMEM((LAY, SEC, LANES), jnp.bfloat16),
            pltpu.SemaphoreType.DMA((2 + GROUPS,)),
        ],
        compiler_params=pltpu.CompilerParams(vmem_limit_bytes=32 * 2**20),
    )(everything, energy, region, temp, cond, stiff)


def per_device(sects, w, strain, region, prior, temp, cond, loss, mullins, stiff):
    send, energy = project(strain.transpose(0, 2, 1, 3))
    recv = lax.all_to_all(send, "circ", 0, 0, tiled=True)
    own, msg = owner(
        recv, w, region, prior, temp, cond, loss, mullins.reshape(1, NREG)
    )
    pairs = []
    for s in range(1, sects):
        for c in range(s % 2, CIRC, 2):
            here = c * sects + s
            pairs += [(here, here - 1), (here - 1, here)]
    halo = lax.ppermute(msg, ("circ", "sect"), pairs)
    block = jnp.broadcast_to((own + halo)[None], (CIRC, 8, LANES))
    everything = lax.all_to_all(block, "circ", 0, 0, tiled=True)
    field, peak, modulus = soften(
        everything.reshape(CIRC * 8, LANES), energy, region, temp, cond, stiff.reshape(1, NREG)
    )
    return field, peak, modulus.transpose(1, 0, 2)


def solution(mesh):
    w = combine_matrix()
    maps = P(None, "sect")

    def whole(*args):
        return jax.shard_map(
            functools.partial(per_device, mesh.shape["sect"], jnp.asarray(w)),
            mesh=mesh,
            in_specs=(P("circ", None, None, "sect"), maps, maps, maps, maps, P(), P(), P()),
            out_specs=(maps, maps, P("circ", None, "sect")),
            check_vma=False,
        )(*args)

    return whole
```

```python
import functools
import math

import jax
import jax.numpy as jnp
import ml_dtypes
import numpy as np
from jax import lax
from jax.experimental import pallas as pl
from jax.experimental.pallas import tpu as pltpu
from jax.sharding import PartitionSpec as P

COMP = 2
HARM = 8
SWEEPS = 4
SINK = 0.1
SEC = 128
LAY = 36
LANES = 128
NREG = 8
CIRC = 16
NSEC = SEC * CIRC
RANK = 9
ROWS = 44
QUAD = 4
PADDED = 768
EDGE = 4
FIELD_ROWS = 40


def combine_matrix():
    half = 0.5 * (SEC - 1) * 2.0 * math.pi / NSEC
    nodes = 64
    n = (np.arange(nodes) + 0.5) * math.pi / nodes
    even = np.zeros((HARM, RANK))
    odd = np.zeros((HARM, RANK))
    for k in range(1, HARM + 1):
        for m in range(RANK):
            weight = (1.0 if m == 0 else 2.0) / nodes
            f = np.cos(k * half * np.cos(n)) if m % 2 == 0 else np.sin(k * half * np.cos(n))
            (even if m % 2 == 0 else odd)[k - 1, m] = weight * np.sum(f * np.cos(m * n))
    u = np.zeros((2 * HARM, CIRC, RANK))
    for d in range(CIRC):
        centre = 2.0 * math.pi * (SEC * d + 0.5 * (SEC - 1)) / NSEC
        for k in range(1, HARM + 1):
            c, s = math.cos(k * centre), math.sin(k * centre)
            u[k - 1, d] = c * even[k - 1] - s * odd[k - 1]
            u[HARM + k - 1, d] = s * even[k - 1] + c * odd[k - 1]
    u = u / math.sqrt(NSEC)
    w = np.zeros((128, CIRC, ROWS))
    for a in range(2):
        for comp in range(COMP):
            at = RANK * (COMP * a + comp)
            w[32 * a + 16 * comp : 32 * a + 16 * comp + 16, :, at : at + RANK] = u
    for b in range(4):
        part = u[:, :, 5 * (b % 2) : 5 * (b % 2) + 5]
        w[64 + 16 * b : 64 + 16 * b + 16, :, 36 : 36 + part.shape[2]] = part
    w = np.pad(w.reshape(128, CIRC * ROWS), ((0, 0), (0, PADDED - CIRC * ROWS)))
    hi = w.astype(ml_dtypes.bfloat16)
    lo = (w - hi.astype(np.float64)).astype(ml_dtypes.bfloat16)
    return np.concatenate([hi, lo])


def lane_of(shape):
    return lax.broadcasted_iota(jnp.int32, shape, len(shape) - 1)


def row_of(shape):
    return lax.broadcasted_iota(jnp.int32, shape, 0)


def halves(first, second):
    low = lane_of(first.shape) < 64
    return (
        jnp.where(low, first, pltpu.roll(second, 64, 1)),
        jnp.where(low, pltpu.roll(first, 64, 1), second),
    )


def across(u):
    return u if u < 4 else u + 8


def within(u):
    return u + 4


def quarter_of(u, h):
    return 3 * h if u % 2 == 0 else 1 + h


def window_matrix():
    wide = (1, SEC * COMP)
    lane = lane_of(wide)
    t = ((lane % SEC).astype(jnp.float32) - 0.5 * (SEC - 1)) * (2.0 / (SEC - 1))
    basis = [jnp.ones(wide, jnp.float32), t]
    for _ in range(RANK - 2):
        basis.append(2.0 * t * basis[-1] - basis[-2])
    rows = [
        jnp.where(lane // SEC == comp, values, 0.0) for comp in range(COMP) for values in basis
    ]
    sub = row_of((8, SEC * COMP))
    parts = []
    for places in (
        range(18),
        range(2, 20),
        [8 * b + (i + 4) % 8 for b in range(4) for i in range(5 - b % 2)],
    ):
        tiles = {}
        for place, row in zip(places, rows):
            tile = tiles.get(place // 8, jnp.zeros((8, SEC * COMP), jnp.float32))
            tiles[place // 8] = jnp.where(sub == place % 8, row, tile)
        rest = jnp.concatenate([tiles[i] for i in sorted(tiles)])
        for _ in range(3):
            part = rest.astype(jnp.bfloat16).astype(jnp.float32)
            parts.append(part)
            rest = rest - part
    return jnp.concatenate(parts).astype(jnp.bfloat16)


TAIL = 8
ORDER = ((TAIL, 0), (1, 2, 3, 4), (5, 6, 7))


def project_kernel(strain_hbm, send_ref, energy_ref, buf, a_ref, sem):
    copies = {}
    for group in ORDER:
        for u in group:
            copies[u] = pltpu.make_async_copy(
                strain_hbm.at[:, pl.ds(4 * u, 4)], buf.at[u], sem.at[u]
            )
            copies[u].start()
    rows = buf.reshape(LAY // 4, SEC * 4 * COMP, LANES)
    send = send_ref.reshape(CIRC, ROWS, LANES)
    parity = lax.axis_index("sect") % 2
    tops = {}
    sums = {}
    tails = {}
    sub = row_of((8, LANES))
    block = lane_of((8, LANES)) // 32

    def pair(t):
        kind = 2 if t >= 16 else t % 2
        size = 32 if kind == 2 else 24
        base = 72 * kind
        first = 4 * (t % 2)
        x = [
            [rows[t // 2, pl.ds(first + COMP * i + c, SEC, stride=4 * COMP), :] for i in range(2)]
            for c in range(COMP)
        ]
        wide = jnp.concatenate([jnp.concatenate(both, axis=1) for both in x])
        d = jnp.dot(a_ref[base : base + 3 * size], wide, preferred_element_type=jnp.float32)
        d = d[:size] + d[size : 2 * size] + d[2 * size :]
        for i in range(2):
            l = 2 * t + i
            c0 = x[0][i].astype(jnp.float32)
            c1 = x[1][i].astype(jnp.float32)
            e = c0 * c0 + c1 * c1
            energy_ref[l] = e
            tops[l] = jnp.max(e, axis=0, keepdims=True)
            sums[l] = d[:, LANES * i : LANES * (i + 1)]

    def pack_tail():
        for v in range(4):
            x = sums[32 + v]
            shifted = []
            for delta in range(4):
                w = jnp.zeros((8, LANES), jnp.float32)
                for b in range(4):
                    w = jnp.where(block == (b - delta) % 4, x[8 * b : 8 * b + 8], w)
                shifted.append(pltpu.roll(w, 32 * delta, 1) if delta else w)
            for g in range(4):
                y = shifted[0]
                for b in range(4):
                    y = jnp.where(block == b, shifted[(b - g) % 4], y)
                top = tops[32 + v]
                if g:
                    top = pltpu.roll(top, LANES - 32 * g, 1)
                tails[v, g] = jnp.where(sub == 3, top, y)

    def pack(u):
        first = halves(sums[4 * u], sums[4 * u + 1])
        second = halves(sums[4 * u + 2], sums[4 * u + 3])
        top0 = halves(tops[4 * u], tops[4 * u + 1])
        top1 = halves(tops[4 * u + 2], tops[4 * u + 3])
        for h in range(2):
            c = across(u) + (within(u) - across(u)) * ((h + parity) % 2)
            tail = tails[u // 2, quarter_of(u, h)]
            send[c, 0:16] = first[h][0:16]
            send[c, 16:24] = first[h][16:24] + second[h][0:8]
            send[c, 24:32] = second[h][8:16]
            send[c, 32:40] = jnp.where(sub < 4, second[h][16:24], tail)
            tile = jnp.where(sub == 1, top0[h], tail)
            send[c, 40:44] = jnp.where(sub == 2, top1[h], tile)[0:4]

    a_ref[...] = window_matrix()
    waiting = []
    for group in ORDER:
        for u in group:
            copies[u].wait()
        for u in group:
            pair(2 * u)
            pair(2 * u + 1)
        for u in waiting:
            pack_tail() if u == TAIL else pack(u)
        waiting = group
    for u in waiting:
        pack_tail() if u == TAIL else pack(u)


def project(strain):
    return pl.pallas_call(
        project_kernel,
        name="project",
        out_shape=[
            jax.ShapeDtypeStruct((CIRC, ROWS // QUAD, QUAD, LANES), jnp.float32),
            jax.ShapeDtypeStruct((LAY, SEC, LANES), jnp.float32),
        ],
        in_specs=[pl.BlockSpec(memory_space=pl.ANY)],
        out_specs=[pl.BlockSpec(memory_space=pltpu.VMEM)] * 2,
        scratch_shapes=[
            pltpu.VMEM((LAY // 4, SEC, 4, COMP, LANES), jnp.bfloat16),
            pltpu.VMEM((240, SEC * COMP), jnp.bfloat16),
            pltpu.SemaphoreType.DMA((LAY // 4,)),
        ],
        compiler_params=pltpu.CompilerParams(vmem_limit_bytes=50 * 2**20),
    )(strain)


def owner_kernel(
    recv_ref, w_ref, region_ref, prior_ref, temp_ref, cond_ref, loss_ref, mullins_ref, own_ref, msg_ref
):
    c = lax.axis_index("circ")
    u = c % 4 + 4 * (c // 8)
    h = (lax.axis_index("sect") + (c // 4 + 1) // 2) % 2
    is_left = h == 0
    lane = lane_of((1, LANES))
    sub = row_of((8, LANES))
    recv = recv_ref.reshape(CIRC * ROWS, LANES)
    p = jnp.concatenate([recv[...], jnp.zeros((PADDED - CIRC * ROWS, LANES), jnp.float32)])
    hi = p.astype(jnp.bfloat16)
    lo = (p - hi.astype(jnp.float32)).astype(jnp.bfloat16)
    o = jnp.dot(
        w_ref[...], jnp.concatenate([hi, lo], axis=1), preferred_element_type=jnp.float32
    )
    coeffs = o[:128, :LANES] + o[128:, :LANES] + o[:128, LANES:]
    squared = coeffs[:64] * coeffs[:64]
    powers = [
        squared[32 * a : 32 * a + 8]
        + squared[32 * a + 8 : 32 * a + 16]
        + squared[32 * a + 16 : 32 * a + 24]
        + squared[32 * a + 24 : 32 * a + 32]
        for a in range(2)
    ]
    last = [coeffs[64 + 16 * b : 80 + 16 * b] for b in range(4)]
    comp0 = last[0] + pltpu.roll(last[1], 96, 1)
    comp1 = pltpu.roll(last[2], 64, 1) + pltpu.roll(last[3], 32, 1)
    comp0, comp1 = comp0 * comp0, comp1 * comp1
    powers.append(comp0[:8] + comp0[8:] + comp1[:8] + comp1[8:])

    quarter = jnp.where(u % 2 == 0, 3 * h, 1 + h)
    back = (LANES - 32 * quarter) % LANES

    def natural(ref):
        rows = [ref[pl.ds(4 * u + j, 1), :] for j in range(4)]
        rows.append(ref[pl.ds(32 + u // 2, 1), :])
        return rows

    def packed(rows):
        out = []
        for a in range(2):
            left, right = halves(rows[2 * a], rows[2 * a + 1])
            out.append(jnp.where(is_left, left, right))
        out.append(pltpu.roll(rows[4], back, 1))
        return out

    region = packed(natural(region_ref))
    prior = packed(natural(prior_ref))
    temp_rows = natural(temp_ref)
    temp = packed(temp_rows)
    cond_rows = natural(cond_ref)
    heats, peaks = [], []
    for i in range(3):
        q = loss_ref[:, 0:1] * powers[i][0:1]
        for k in range(1, HARM):
            q = q + loss_ref[:, k : k + 1] * powers[i][k : k + 1]
        picked = jnp.sum(jnp.where(region[i] == sub, q, 0.0), axis=0, keepdims=True)
        share = jnp.zeros((1, LANES), jnp.float32)
        for r in range(NREG):
            share = jnp.where(region[i] == r, mullins_ref[0:1, r : r + 1], share)
        top = jnp.max(recv[pl.ds(41 + i, CIRC, stride=ROWS), :], axis=0, keepdims=True)
        peak = jnp.maximum(prior[i], top)
        heats.append(jnp.exp(-0.5 * temp[i]) * picked + share * (peak - prior[i]))
        peaks.append(peak)

    third = (lane >= 32) & (lane < 64)
    own = jnp.where(sub == 0, heats[0], 0.0)
    own = jnp.where(sub == 1, heats[1], own)
    own = jnp.where(sub == 2, peaks[0], own)
    own = jnp.where(sub == 3, peaks[1], own)
    own = jnp.where((sub == 4) & third, pltpu.roll(heats[2], 32, 1), own)
    own_ref[...] = jnp.where((sub == 5) & third, pltpu.roll(peaks[2], 32, 1), own)

    edge_heat = []
    for a in range(2):
        turned = pltpu.roll(heats[a], 64, 1)
        edge_heat.append(jnp.where(is_left, heats[a], turned))
        edge_heat.append(jnp.where(is_left, turned, heats[a]))
    edge_heat.append(jnp.where(is_left, heats[2], pltpu.roll(heats[2], 96, 1)))
    edge = jnp.where(is_left, lane, LANES - 1 - lane) < EDGE
    step = jnp.where(is_left, EDGE, LANES - EDGE)
    msg = jnp.zeros((8, LANES), jnp.float32)
    for j in range(5):
        row = jnp.where(edge, edge_heat[j], 0.0)
        row = row + pltpu.roll(jnp.where(edge, cond_rows[j], 0.0), step, 1)
        row = row + pltpu.roll(jnp.where(edge, temp_rows[j], 0.0), (2 * step) % LANES, 1)
        if j < 4:
            msg = msg + jnp.where(sub == 4 + j, row, 0.0)
        else:
            row = pltpu.roll(row, jnp.where(is_left, 32, 96), 1)
            msg = msg + jnp.where(sub == 6, row, 0.0)
    msg_ref[...] = msg


def owner(recv, w, region, prior, temp, cond, loss, mullins):
    vmem = pl.BlockSpec(memory_space=pltpu.VMEM)
    return pl.pallas_call(
        owner_kernel,
        name="owner",
        out_shape=[jax.ShapeDtypeStruct((8, LANES), jnp.float32)] * 2,
        in_specs=[vmem] * 8,
        out_specs=[vmem] * 2,
        compiler_params=pltpu.CompilerParams(vmem_limit_bytes=32 * 2**20),
    )(recv, w, region, prior, temp, cond, loss, mullins)


GROUPS = 6
EARLY = 12


def modulus_kernel(
    all_ref, energy_ref, region_ref, temp_ref, cond_ref, stiff_ref,
    field_hbm, peak_hbm, out_hbm,
    heat_s, peak_s, halo_s, cond_s, temp_s, region_s, field_s, soft_s, out_s, sem,
):
    low = lane_of((8, LANES)) < 64
    lane = lane_of((FIELD_ROWS, LANES))
    even = lax.axis_index("sect") % 2 == 0

    def sides(k):
        far = jnp.concatenate(
            [all_ref[pl.ds(k, 4, stride=8), :], all_ref[pl.ds(96 + k, 4, stride=8), :]]
        )
        near = all_ref[pl.ds(32 + k, 8, stride=8), :]
        return jnp.where(even, far, near), jnp.where(even, near, far)

    def tail_sides(k, odd):
        k = k + 8 * odd
        far = jnp.concatenate(
            [all_ref[pl.ds(k, 2, stride=16), :], all_ref[pl.ds(96 + k, 2, stride=16), :]]
        )
        near = all_ref[pl.ds(32 + k, 4, stride=16), :]
        return jnp.where(even, far, near), jnp.where(even, near, far)

    for scratch in (heat_s, peak_s, halo_s, cond_s, temp_s):
        scratch[32:FIELD_ROWS] = jnp.zeros((8, LANES), jnp.float32)
    region_s[32:FIELD_ROWS] = jnp.zeros((8, LANES), jnp.int32)
    cond_s[0:LAY] = cond_ref[...]
    temp_s[0:LAY] = temp_ref[...]
    region_s[0:LAY] = region_ref[...]
    for a in range(2):
        for base, target in ((0, heat_s), (2, peak_s)):
            left, right = sides(base + a)
            target[pl.ds(2 * a, 8, stride=4), :] = jnp.where(low, left, pltpu.roll(right, 64, 1))
            target[pl.ds(2 * a + 1, 8, stride=4), :] = jnp.where(low, pltpu.roll(left, 64, 1), right)
    small = lane_of((4, LANES))
    for base, target in ((4, heat_s), (5, peak_s)):
        row = jnp.zeros((4, LANES), jnp.float32)
        parts = [tail_sides(base, odd) for odd in range(2)]
        for odd, h, g in ((0, 0, 0), (1, 0, 1), (1, 1, 2), (0, 1, 3)):
            part = parts[odd][h]
            if g != 1:
                part = pltpu.roll(part, (32 * g - 32) % LANES, 1)
            row = jnp.where(small // 32 == g, part, row)
        target[32:LAY] = row
    wide = lane_of((8, LANES))
    outer = (wide < 3 * EDGE) | (wide >= LANES - 3 * EDGE)
    for j in range(4):
        left, right = sides(4 + j)
        halo_s[pl.ds(j, 8, stride=4), :] = jnp.where(outer, left + right, 0.0)
    from_left, from_right = tail_sides(6, 0)
    from_left = pltpu.roll(from_left, 32, 1)
    from_right = pltpu.roll(from_right, 96, 1)
    halo_s[32:LAY] = jnp.where(
        small >= LANES - 3 * EDGE, from_left, jnp.where(small < 3 * EDGE, from_right, 0.0)
    )

    peak = peak_s[...]
    halo = halo_s[...]

    def unpack(n):
        low_part = pltpu.roll(halo, (LANES - EDGE * n) % LANES, 1) if n else halo
        high_part = pltpu.roll(halo, EDGE * n, 1) if n else halo
        return jnp.where(
            lane < EDGE, low_part, jnp.where(lane >= LANES - EDGE, high_part, 0.0)
        )

    heat = (heat_s[...], unpack(0))
    cond = (cond_s[...], unpack(1))
    field = (temp_s[...], unpack(2))
    scale = [1.0 / (4.0 * k + SINK) for k in cond]
    heat = [x * y for x, y in zip(heat, scale)]
    cond = [x * y for x, y in zip(cond, scale)]
    rows = row_of((FIELD_ROWS, LANES))
    valid = rows < LAY
    first, final = lane == 0, lane == LANES - 1
    for _ in range(SWEEPS):
        right = [pltpu.roll(x, 1, 1) for x in field]
        left = [pltpu.roll(x, LANES - 1, 1) for x in field]
        new = []
        for i in range(2):
            beside = jnp.where(first, right[1 - i], right[i]) + jnp.where(final, left[1 - i], left[i])
            beside = beside + pltpu.roll(field[i], 1, 0) + pltpu.roll(field[i], FIELD_ROWS - 1, 0)
            new.append(jnp.where(valid, heat[i] + cond[i] * beside, 0.0))
        field = new
    for l in range(EARLY):
        soft_s[l] = 1.0 - 0.5 * jnp.tanh((peak[l : l + 1] - energy_ref[l]) * 0.25)
    field_s[...] = field[0]
    copies = [
        pltpu.make_async_copy(field_s.at[0:LAY], field_hbm, sem.at[0]),
        pltpu.make_async_copy(peak_s.at[0:LAY], peak_hbm, sem.at[1]),
    ]
    for copy in copies:
        copy.start()
    region = region_s[...]
    stiff = jnp.zeros((FIELD_ROWS, LANES), jnp.float32)
    for r in range(NREG):
        stiff = jnp.where(region == r, stiff_ref[0:1, r : r + 1], stiff)
    factor = stiff * jnp.exp(-0.5 * field[0])
    size = LAY // GROUPS
    for group in range(GROUPS):
        for l in range(group * size, (group + 1) * size):
            if l < EARLY:
                soft = soft_s[l]
            else:
                soft = 1.0 - 0.5 * jnp.tanh((peak[l : l + 1] - energy_ref[l]) * 0.25)
            out_s[l] = (factor[l : l + 1] * soft).astype(jnp.bfloat16)
        where = pl.ds(group * size, size)
        copy = pltpu.make_async_copy(out_s.at[where], out_hbm.at[where], sem.at[2 + group])
        copy.start()
        copies.append(copy)
    for copy in copies:
        copy.wait()


def soften(everything, energy, region, temp, cond, stiff):
    vmem = pl.BlockSpec(memory_space=pltpu.VMEM)
    plane = pltpu.VMEM((FIELD_ROWS, LANES), jnp.float32)
    return pl.pallas_call(
        modulus_kernel,
        name="modulus",
        out_shape=[
            jax.ShapeDtypeStruct((LAY, LANES), jnp.float32),
            jax.ShapeDtypeStruct((LAY, LANES), jnp.float32),
            jax.ShapeDtypeStruct((LAY, SEC, LANES), jnp.bfloat16),
        ],
        in_specs=[vmem] * 6,
        out_specs=[pl.BlockSpec(memory_space=pl.ANY)] * 3,
        scratch_shapes=[
            plane, plane, plane, plane, plane,
            pltpu.VMEM((FIELD_ROWS, LANES), jnp.int32),
            plane,
            pltpu.VMEM((EARLY, SEC, LANES), jnp.float32),
            pltpu.VMEM((LAY, SEC, LANES), jnp.bfloat16),
            pltpu.SemaphoreType.DMA((2 + GROUPS,)),
        ],
        compiler_params=pltpu.CompilerParams(vmem_limit_bytes=32 * 2**20),
    )(everything, energy, region, temp, cond, stiff)


def per_device(sects, w, strain, region, prior, temp, cond, loss, mullins, stiff):
    send, energy = project(strain.transpose(0, 2, 1, 3))
    recv = lax.all_to_all(send, "circ", 0, 0, tiled=True)
    own, msg = owner(
        recv, w, region, prior, temp, cond, loss, mullins.reshape(1, NREG)
    )
    pairs = []
    for s in range(1, sects):
        for u in range(CIRC // 2):
            here = (within(u) if s % 2 else across(u)) * sects + s
            pairs += [(here, here - 1), (here - 1, here)]
    halo = lax.ppermute(msg, ("circ", "sect"), pairs)
    block = jnp.broadcast_to((own + halo)[None], (CIRC, 8, LANES))
    everything = lax.all_to_all(block, "circ", 0, 0, tiled=True)
    field, peak, modulus = soften(
        everything.reshape(CIRC * 8, LANES), energy, region, temp, cond, stiff.reshape(1, NREG)
    )
    return field, peak, modulus.transpose(1, 0, 2)


def solution(mesh):
    w = combine_matrix()
    maps = P(None, "sect")

    def whole(*args):
        return jax.shard_map(
            functools.partial(per_device, mesh.shape["sect"], jnp.asarray(w)),
            mesh=mesh,
            in_specs=(P("circ", None, None, "sect"), maps, maps, maps, maps, P(), P(), P()),
            out_specs=(maps, maps, P("circ", None, "sect")),
            check_vma=False,
        )(*args)

    return whole
```

```python
import functools
import math

import jax
import jax.numpy as jnp
import ml_dtypes
import numpy as np
from jax import lax
from jax.experimental import pallas as pl
from jax.experimental.pallas import tpu as pltpu
from jax.sharding import PartitionSpec as P

COMP = 2
HARM = 8
SWEEPS = 4
SINK = 0.1
SEC = 128
LAY = 36
LANES = 128
NREG = 8
CIRC = 16
NSEC = SEC * CIRC
RANK = 9
ROWS = 44
QUAD = 4
PADDED = 768
EDGE = 4
FIELD_ROWS = 40


def combine_matrix():
    half = 0.5 * (SEC - 1) * 2.0 * math.pi / NSEC
    nodes = 64
    n = (np.arange(nodes) + 0.5) * math.pi / nodes
    even = np.zeros((HARM, RANK))
    odd = np.zeros((HARM, RANK))
    for k in range(1, HARM + 1):
        for m in range(RANK):
            weight = (1.0 if m == 0 else 2.0) / nodes
            f = np.cos(k * half * np.cos(n)) if m % 2 == 0 else np.sin(k * half * np.cos(n))
            (even if m % 2 == 0 else odd)[k - 1, m] = weight * np.sum(f * np.cos(m * n))
    u = np.zeros((2 * HARM, CIRC, RANK))
    for d in range(CIRC):
        centre = 2.0 * math.pi * (SEC * d + 0.5 * (SEC - 1)) / NSEC
        for k in range(1, HARM + 1):
            c, s = math.cos(k * centre), math.sin(k * centre)
            u[k - 1, d] = c * even[k - 1] - s * odd[k - 1]
            u[HARM + k - 1, d] = s * even[k - 1] + c * odd[k - 1]
    u = u / math.sqrt(NSEC)
    w = np.zeros((128, CIRC, ROWS))
    for a in range(2):
        for comp in range(COMP):
            at = RANK * (COMP * a + comp)
            w[32 * a + 16 * comp : 32 * a + 16 * comp + 16, :, at : at + RANK] = u
    for b in range(4):
        part = u[:, :, 5 * (b % 2) : 5 * (b % 2) + 5]
        w[64 + 16 * b : 64 + 16 * b + 16, :, 36 : 36 + part.shape[2]] = part
    w = np.pad(w.reshape(128, CIRC * ROWS), ((0, 0), (0, PADDED - CIRC * ROWS)))
    hi = w.astype(ml_dtypes.bfloat16)
    lo = (w - hi.astype(np.float64)).astype(ml_dtypes.bfloat16)
    return np.concatenate([hi, lo])


def lane_of(shape):
    return lax.broadcasted_iota(jnp.int32, shape, len(shape) - 1)


def row_of(shape):
    return lax.broadcasted_iota(jnp.int32, shape, 0)


def halves(first, second):
    low = lane_of(first.shape) < 64
    return (
        jnp.where(low, first, pltpu.roll(second, 64, 1)),
        jnp.where(low, pltpu.roll(first, 64, 1), second),
    )


def across(u):
    return u if u < 4 else u + 8


def within(u):
    return u + 4


def quarter_of(u, h):
    return 3 * h if u % 2 == 0 else 1 + h


def window_matrix():
    wide = (1, SEC * COMP)
    lane = lane_of(wide)
    t = ((lane % SEC).astype(jnp.float32) - 0.5 * (SEC - 1)) * (2.0 / (SEC - 1))
    basis = [jnp.ones(wide, jnp.float32), t]
    for _ in range(RANK - 2):
        basis.append(2.0 * t * basis[-1] - basis[-2])
    rows = [
        jnp.where(lane // SEC == comp, values, 0.0) for comp in range(COMP) for values in basis
    ]
    sub = row_of((8, SEC * COMP))
    parts = []
    for places in (
        range(18),
        range(2, 20),
        [8 * b + (i + 4) % 8 for b in range(4) for i in range(5 - b % 2)],
    ):
        tiles = {}
        for place, row in zip(places, rows):
            tile = tiles.get(place // 8, jnp.zeros((8, SEC * COMP), jnp.float32))
            tiles[place // 8] = jnp.where(sub == place % 8, row, tile)
        rest = jnp.concatenate([tiles[i] for i in sorted(tiles)])
        for _ in range(3):
            part = rest.astype(jnp.bfloat16).astype(jnp.float32)
            parts.append(part)
            rest = rest - part
    return jnp.concatenate(parts).astype(jnp.bfloat16)


TAIL = 8
ORDER = ((TAIL, 0), (1, 2, 3, 4), (5, 6, 7))


def project_kernel(strain_hbm, send_ref, energy_ref, buf, a_ref, sem):
    copies = {}
    for group in ORDER:
        for u in group:
            copies[u] = pltpu.make_async_copy(
                strain_hbm.at[:, pl.ds(4 * u, 4)], buf.at[u], sem.at[u]
            )
            copies[u].start()
    rows = buf.reshape(LAY // 4, SEC * 4 * COMP, LANES)
    send = send_ref.reshape(CIRC, ROWS, LANES)
    parity = lax.axis_index("sect") % 2
    tops = {}
    sums = {}
    tails = {}
    sub = row_of((8, LANES))
    block = lane_of((8, LANES)) // 32

    def pair(t):
        kind = 2 if t >= 16 else t % 2
        size = 32 if kind == 2 else 24
        base = 72 * kind
        first = 4 * (t % 2)
        x = [
            [rows[t // 2, pl.ds(first + COMP * i + c, SEC, stride=4 * COMP), :] for i in range(2)]
            for c in range(COMP)
        ]
        wide = jnp.concatenate([jnp.concatenate(both, axis=1) for both in x])
        d = jnp.dot(a_ref[base : base + 3 * size], wide, preferred_element_type=jnp.float32)
        d = d[:size] + d[size : 2 * size] + d[2 * size :]
        for i in range(2):
            l = 2 * t + i
            c0 = x[0][i].astype(jnp.float32)
            c1 = x[1][i].astype(jnp.float32)
            e = c0 * c0 + c1 * c1
            energy_ref[l] = e
            tops[l] = jnp.max(e, axis=0, keepdims=True)
            sums[l] = d[:, LANES * i : LANES * (i + 1)]

    def pack_tail():
        for v in range(4):
            x = sums[32 + v]
            shifted = []
            for delta in range(4):
                w = jnp.zeros((8, LANES), jnp.float32)
                for b in range(4):
                    w = jnp.where(block == (b - delta) % 4, x[8 * b : 8 * b + 8], w)
                shifted.append(pltpu.roll(w, 32 * delta, 1) if delta else w)
            for g in range(4):
                y = shifted[0]
                for b in range(4):
                    y = jnp.where(block == b, shifted[(b - g) % 4], y)
                top = tops[32 + v]
                if g:
                    top = pltpu.roll(top, LANES - 32 * g, 1)
                tails[v, g] = jnp.where(sub == 3, top, y)

    def pack(u):
        first = halves(sums[4 * u], sums[4 * u + 1])
        second = halves(sums[4 * u + 2], sums[4 * u + 3])
        top0 = halves(tops[4 * u], tops[4 * u + 1])
        top1 = halves(tops[4 * u + 2], tops[4 * u + 3])
        for h in range(2):
            c = across(u) + (within(u) - across(u)) * ((h + parity) % 2)
            tail = tails[u // 2, quarter_of(u, h)]
            send[c, 0:16] = first[h][0:16]
            send[c, 16:24] = first[h][16:24] + second[h][0:8]
            send[c, 24:32] = second[h][8:16]
            send[c, 32:40] = jnp.where(sub < 4, second[h][16:24], tail)
            tile = jnp.where(sub == 1, top0[h], tail)
            send[c, 40:44] = jnp.where(sub == 2, top1[h], tile)[0:4]

    a_ref[...] = window_matrix()
    waiting = []
    for group in ORDER:
        for u in group:
            copies[u].wait()
        for u in group:
            pair(2 * u)
            pair(2 * u + 1)
        for u in waiting:
            pack_tail() if u == TAIL else pack(u)
        waiting = group
    for u in waiting:
        pack_tail() if u == TAIL else pack(u)


def project(strain):
    return pl.pallas_call(
        project_kernel,
        name="project",
        out_shape=[
            jax.ShapeDtypeStruct((CIRC, ROWS // QUAD, QUAD, LANES), jnp.float32),
            jax.ShapeDtypeStruct((LAY, SEC, LANES), jnp.float32),
        ],
        in_specs=[pl.BlockSpec(memory_space=pl.ANY)],
        out_specs=[pl.BlockSpec(memory_space=pltpu.VMEM)] * 2,
        scratch_shapes=[
            pltpu.VMEM((LAY // 4, SEC, 4, COMP, LANES), jnp.bfloat16),
            pltpu.VMEM((240, SEC * COMP), jnp.bfloat16),
            pltpu.SemaphoreType.DMA((LAY // 4,)),
        ],
        compiler_params=pltpu.CompilerParams(vmem_limit_bytes=50 * 2**20),
    )(strain)


def owner_kernel(
    recv_ref, w_ref, region_ref, prior_ref, temp_ref, cond_ref, loss_ref, mullins_ref, own_ref, msg_ref
):
    c = lax.axis_index("circ")
    u = c % 4 + 4 * (c // 8)
    h = (lax.axis_index("sect") + (c // 4 + 1) // 2) % 2
    is_left = h == 0
    lane = lane_of((1, LANES))
    sub = row_of((8, LANES))
    recv = recv_ref.reshape(CIRC * ROWS, LANES)
    p = jnp.concatenate([recv[...], jnp.zeros((PADDED - CIRC * ROWS, LANES), jnp.float32)])
    hi = p.astype(jnp.bfloat16)
    lo = (p - hi.astype(jnp.float32)).astype(jnp.bfloat16)
    o = jnp.dot(
        w_ref[...], jnp.concatenate([hi, lo], axis=1), preferred_element_type=jnp.float32
    )
    coeffs = o[:128, :LANES] + o[128:, :LANES] + o[:128, LANES:]
    squared = coeffs[:64] * coeffs[:64]
    powers = [
        squared[32 * a : 32 * a + 8]
        + squared[32 * a + 8 : 32 * a + 16]
        + squared[32 * a + 16 : 32 * a + 24]
        + squared[32 * a + 24 : 32 * a + 32]
        for a in range(2)
    ]
    last = [coeffs[64 + 16 * b : 80 + 16 * b] for b in range(4)]
    comp0 = last[0] + pltpu.roll(last[1], 96, 1)
    comp1 = pltpu.roll(last[2], 64, 1) + pltpu.roll(last[3], 32, 1)
    comp0, comp1 = comp0 * comp0, comp1 * comp1
    powers.append(comp0[:8] + comp0[8:] + comp1[:8] + comp1[8:])

    quarter = jnp.where(u % 2 == 0, 3 * h, 1 + h)
    back = (LANES - 32 * quarter) % LANES

    low = lane_of((4, LANES)) < 64

    def stacked(vectors):
        out = jnp.where(sub == 0, vectors[0], vectors[1])
        return jnp.where(sub == 2, vectors[2], out)

    def own_cells(ref):
        rows = ref[pl.ds(4 * u, 4), :]
        last = ref[pl.ds(32 + u // 2, 1), :]
        turned = pltpu.roll(rows, 64, 1)
        evens = jnp.where(is_left, rows, turned)
        odds = jnp.where(is_left, turned, rows)
        odds = pltpu.roll(jnp.concatenate([odds, odds]), 7, 0)[0:4]
        mixed = jnp.where(low, evens, odds)
        return stacked([mixed[0:1], mixed[2:3], pltpu.roll(last, back, 1)]), rows, last

    region, _, _ = own_cells(region_ref)
    prior, _, _ = own_cells(prior_ref)
    temp, temp_rows, temp_last = own_cells(temp_ref)
    cond_rows = cond_ref[pl.ds(4 * u, 4), :]
    cond_last = cond_ref[pl.ds(32 + u // 2, 1), :]
    picked = []
    for i in range(3):
        q = loss_ref[:, 0:1] * powers[i][0:1]
        for k in range(1, HARM):
            q = q + loss_ref[:, k : k + 1] * powers[i][k : k + 1]
        picked.append(
            jnp.sum(jnp.where(region[i : i + 1] == sub, q, 0.0), axis=0, keepdims=True)
        )
    share = jnp.zeros((8, LANES), jnp.float32)
    for r in range(NREG):
        share = jnp.where(region == r, mullins_ref[0:1, r : r + 1], share)
    top = stacked(
        [
            jnp.max(recv[pl.ds(41 + i, CIRC, stride=ROWS), :], axis=0, keepdims=True)
            for i in range(3)
        ]
    )
    peak = jnp.maximum(prior, top)
    heat = jnp.exp(-0.5 * temp) * stacked(picked) + share * (peak - prior)
    heats = [heat[i : i + 1] for i in range(3)]
    peaks = [peak[i : i + 1] for i in range(3)]

    third = (lane >= 32) & (lane < 64)
    own = jnp.where(sub == 0, heats[0], 0.0)
    own = jnp.where(sub == 1, heats[1], own)
    own = jnp.where(sub == 2, peaks[0], own)
    own = jnp.where(sub == 3, peaks[1], own)
    own = jnp.where((sub == 4) & third, pltpu.roll(heats[2], 32, 1), own)
    own_ref[...] = jnp.where((sub == 5) & third, pltpu.roll(peaks[2], 32, 1), own)

    edge = jnp.where(is_left, lane, LANES - 1 - lane) < EDGE
    step = jnp.where(is_left, EDGE, LANES - EDGE)

    def message(heat_rows, cond_part, temp_part):
        row = jnp.where(edge, heat_rows, 0.0)
        row = row + pltpu.roll(jnp.where(edge, cond_part, 0.0), step, 1)
        return row + pltpu.roll(jnp.where(edge, temp_part, 0.0), (2 * step) % LANES, 1)

    turned = pltpu.roll(heat, 64, 1)
    evens = jnp.where(is_left, heat, turned)
    odds = jnp.where(is_left, turned, heat)
    four = jnp.concatenate([evens[0:1], odds[0:1], evens[1:2], odds[1:2]])
    main = message(four, cond_rows, temp_rows)
    final = jnp.where(is_left, heats[2], pltpu.roll(heats[2], 96, 1))
    final = pltpu.roll(message(final, cond_last, temp_last), jnp.where(is_left, 32, 96), 1)
    msg = jnp.concatenate([jnp.zeros((4, LANES), jnp.float32), main])
    msg = msg + jnp.where(sub == 6, final, 0.0)
    msg_ref[...] = msg


def owner(recv, w, region, prior, temp, cond, loss, mullins):
    vmem = pl.BlockSpec(memory_space=pltpu.VMEM)
    return pl.pallas_call(
        owner_kernel,
        name="owner",
        out_shape=[jax.ShapeDtypeStruct((8, LANES), jnp.float32)] * 2,
        in_specs=[vmem] * 8,
        out_specs=[vmem] * 2,
        compiler_params=pltpu.CompilerParams(vmem_limit_bytes=32 * 2**20),
    )(recv, w, region, prior, temp, cond, loss, mullins)


GROUPS = 6
EARLY = 12


def modulus_kernel(
    all_ref, energy_ref, region_ref, temp_ref, cond_ref, stiff_ref,
    field_hbm, peak_hbm, out_hbm,
    heat_s, peak_s, halo_s, cond_s, temp_s, region_s, field_s, soft_s, out_s, sem,
):
    low = lane_of((8, LANES)) < 64
    lane = lane_of((FIELD_ROWS, LANES))
    even = lax.axis_index("sect") % 2 == 0

    def sides(k):
        far = jnp.concatenate(
            [all_ref[pl.ds(k, 4, stride=8), :], all_ref[pl.ds(96 + k, 4, stride=8), :]]
        )
        near = all_ref[pl.ds(32 + k, 8, stride=8), :]
        return jnp.where(even, far, near), jnp.where(even, near, far)

    def tail_sides(k, odd):
        k = k + 8 * odd
        far = jnp.concatenate(
            [all_ref[pl.ds(k, 2, stride=16), :], all_ref[pl.ds(96 + k, 2, stride=16), :]]
        )
        near = all_ref[pl.ds(32 + k, 4, stride=16), :]
        return jnp.where(even, far, near), jnp.where(even, near, far)

    for scratch in (heat_s, peak_s, halo_s, cond_s, temp_s):
        scratch[32:FIELD_ROWS] = jnp.zeros((8, LANES), jnp.float32)
    region_s[32:FIELD_ROWS] = jnp.zeros((8, LANES), jnp.int32)
    cond_s[0:LAY] = cond_ref[...]
    temp_s[0:LAY] = temp_ref[...]
    region_s[0:LAY] = region_ref[...]
    for a in range(2):
        for base, target in ((0, heat_s), (2, peak_s)):
            left, right = sides(base + a)
            target[pl.ds(2 * a, 8, stride=4), :] = jnp.where(low, left, pltpu.roll(right, 64, 1))
            target[pl.ds(2 * a + 1, 8, stride=4), :] = jnp.where(low, pltpu.roll(left, 64, 1), right)
    small = lane_of((4, LANES))
    for base, target in ((4, heat_s), (5, peak_s)):
        row = jnp.zeros((4, LANES), jnp.float32)
        parts = [tail_sides(base, odd) for odd in range(2)]
        for odd, h, g in ((0, 0, 0), (1, 0, 1), (1, 1, 2), (0, 1, 3)):
            part = parts[odd][h]
            if g != 1:
                part = pltpu.roll(part, (32 * g - 32) % LANES, 1)
            row = jnp.where(small // 32 == g, part, row)
        target[32:LAY] = row
    wide = lane_of((8, LANES))
    outer = (wide < 3 * EDGE) | (wide >= LANES - 3 * EDGE)
    for j in range(4):
        left, right = sides(4 + j)
        halo_s[pl.ds(j, 8, stride=4), :] = jnp.where(outer, left + right, 0.0)
    from_left, from_right = tail_sides(6, 0)
    from_left = pltpu.roll(from_left, 32, 1)
    from_right = pltpu.roll(from_right, 96, 1)
    halo_s[32:LAY] = jnp.where(
        small >= LANES - 3 * EDGE, from_left, jnp.where(small < 3 * EDGE, from_right, 0.0)
    )

    peak = peak_s[...]
    halo = halo_s[...]

    def unpack(n):
        low_part = pltpu.roll(halo, (LANES - EDGE * n) % LANES, 1) if n else halo
        high_part = pltpu.roll(halo, EDGE * n, 1) if n else halo
        return jnp.where(
            lane < EDGE, low_part, jnp.where(lane >= LANES - EDGE, high_part, 0.0)
        )

    heat = (heat_s[...], unpack(0))
    cond = (cond_s[...], unpack(1))
    field = (temp_s[...], unpack(2))
    scale = [1.0 / (4.0 * k + SINK) for k in cond]
    heat = [x * y for x, y in zip(heat, scale)]
    cond = [x * y for x, y in zip(cond, scale)]
    rows = row_of((FIELD_ROWS, LANES))
    valid = rows < LAY
    first, final = lane == 0, lane == LANES - 1
    for _ in range(SWEEPS):
        right = [pltpu.roll(x, 1, 1) for x in field]
        left = [pltpu.roll(x, LANES - 1, 1) for x in field]
        new = []
        for i in range(2):
            beside = jnp.where(first, right[1 - i], right[i]) + jnp.where(final, left[1 - i], left[i])
            beside = beside + pltpu.roll(field[i], 1, 0) + pltpu.roll(field[i], FIELD_ROWS - 1, 0)
            new.append(jnp.where(valid, heat[i] + cond[i] * beside, 0.0))
        field = new
    for l in range(EARLY):
        soft_s[l] = 1.0 - 0.5 * jnp.tanh((peak[l : l + 1] - energy_ref[l]) * 0.25)
    field_s[...] = field[0]
    copies = [
        pltpu.make_async_copy(field_s.at[0:LAY], field_hbm, sem.at[0]),
        pltpu.make_async_copy(peak_s.at[0:LAY], peak_hbm, sem.at[1]),
    ]
    for copy in copies:
        copy.start()
    region = region_s[...]
    stiff = jnp.zeros((FIELD_ROWS, LANES), jnp.float32)
    for r in range(NREG):
        stiff = jnp.where(region == r, stiff_ref[0:1, r : r + 1], stiff)
    factor = stiff * jnp.exp(-0.5 * field[0])
    size = LAY // GROUPS
    for group in range(GROUPS):
        for l in range(group * size, (group + 1) * size):
            if l < EARLY:
                soft = soft_s[l]
            else:
                soft = 1.0 - 0.5 * jnp.tanh((peak[l : l + 1] - energy_ref[l]) * 0.25)
            out_s[l] = (factor[l : l + 1] * soft).astype(jnp.bfloat16)
        where = pl.ds(group * size, size)
        copy = pltpu.make_async_copy(out_s.at[where], out_hbm.at[where], sem.at[2 + group])
        copy.start()
        copies.append(copy)
    for copy in copies:
        copy.wait()


def soften(everything, energy, region, temp, cond, stiff):
    vmem = pl.BlockSpec(memory_space=pltpu.VMEM)
    plane = pltpu.VMEM((FIELD_ROWS, LANES), jnp.float32)
    return pl.pallas_call(
        modulus_kernel,
        name="modulus",
        out_shape=[
            jax.ShapeDtypeStruct((LAY, LANES), jnp.float32),
            jax.ShapeDtypeStruct((LAY, LANES), jnp.float32),
            jax.ShapeDtypeStruct((LAY, SEC, LANES), jnp.bfloat16),
        ],
        in_specs=[vmem] * 6,
        out_specs=[pl.BlockSpec(memory_space=pl.ANY)] * 3,
        scratch_shapes=[
            plane, plane, plane, plane, plane,
            pltpu.VMEM((FIELD_ROWS, LANES), jnp.int32),
            plane,
            pltpu.VMEM((EARLY, SEC, LANES), jnp.float32),
            pltpu.VMEM((LAY, SEC, LANES), jnp.bfloat16),
            pltpu.SemaphoreType.DMA((2 + GROUPS,)),
        ],
        compiler_params=pltpu.CompilerParams(vmem_limit_bytes=32 * 2**20),
    )(everything, energy, region, temp, cond, stiff)


def per_device(sects, w, strain, region, prior, temp, cond, loss, mullins, stiff):
    send, energy = project(strain.transpose(0, 2, 1, 3))
    recv = lax.all_to_all(send, "circ", 0, 0, tiled=True)
    own, msg = owner(
        recv, w, region, prior, temp, cond, loss, mullins.reshape(1, NREG)
    )
    pairs = []
    for s in range(1, sects):
        for u in range(CIRC // 2):
            here = (within(u) if s % 2 else across(u)) * sects + s
            pairs += [(here, here - 1), (here - 1, here)]
    halo = lax.ppermute(msg, ("circ", "sect"), pairs)
    block = jnp.broadcast_to((own + halo)[None], (CIRC, 8, LANES))
    everything = lax.all_to_all(block, "circ", 0, 0, tiled=True)
    field, peak, modulus = soften(
        everything.reshape(CIRC * 8, LANES), energy, region, temp, cond, stiff.reshape(1, NREG)
    )
    return field, peak, modulus.transpose(1, 0, 2)


def solution(mesh):
    w = combine_matrix()
    maps = P(None, "sect")

    def whole(*args):
        return jax.shard_map(
            functools.partial(per_device, mesh.shape["sect"], jnp.asarray(w)),
            mesh=mesh,
            in_specs=(P("circ", None, None, "sect"), maps, maps, maps, maps, P(), P(), P()),
            out_specs=(maps, maps, P("circ", None, "sect")),
            check_vma=False,
        )(*args)

    return whole
```

```python
import functools
import math

import jax
import jax.numpy as jnp
import ml_dtypes
import numpy as np
from jax import lax
from jax.experimental import pallas as pl
from jax.experimental.pallas import tpu as pltpu
from jax.sharding import PartitionSpec as P

COMP = 2
HARM = 8
SWEEPS = 4
SINK = 0.1
SEC = 128
LAY = 36
LANES = 128
NREG = 8
CIRC = 16
NSEC = SEC * CIRC
RANK = 9
ROWS = 44
QUAD = 4
PADDED = 768
EDGE = 4
FIELD_ROWS = 40


def combine_matrix():
    half = 0.5 * (SEC - 1) * 2.0 * math.pi / NSEC
    nodes = 64
    n = (np.arange(nodes) + 0.5) * math.pi / nodes
    even = np.zeros((HARM, RANK))
    odd = np.zeros((HARM, RANK))
    for k in range(1, HARM + 1):
        for m in range(RANK):
            weight = (1.0 if m == 0 else 2.0) / nodes
            f = np.cos(k * half * np.cos(n)) if m % 2 == 0 else np.sin(k * half * np.cos(n))
            (even if m % 2 == 0 else odd)[k - 1, m] = weight * np.sum(f * np.cos(m * n))
    u = np.zeros((2 * HARM, CIRC, RANK))
    for d in range(CIRC):
        centre = 2.0 * math.pi * (SEC * d + 0.5 * (SEC - 1)) / NSEC
        for k in range(1, HARM + 1):
            c, s = math.cos(k * centre), math.sin(k * centre)
            u[k - 1, d] = c * even[k - 1] - s * odd[k - 1]
            u[HARM + k - 1, d] = s * even[k - 1] + c * odd[k - 1]
    u = u / math.sqrt(NSEC)
    w = np.zeros((128, CIRC, ROWS))
    for a in range(2):
        for comp in range(COMP):
            at = RANK * (COMP * a + comp)
            w[32 * a + 16 * comp : 32 * a + 16 * comp + 16, :, at : at + RANK] = u
    for b in range(4):
        part = u[:, :, 5 * (b % 2) : 5 * (b % 2) + 5]
        w[64 + 16 * b : 64 + 16 * b + 16, :, 36 : 36 + part.shape[2]] = part
    w = np.pad(w.reshape(128, CIRC * ROWS), ((0, 0), (0, PADDED - CIRC * ROWS)))
    hi = w.astype(ml_dtypes.bfloat16)
    lo = (w - hi.astype(np.float64)).astype(ml_dtypes.bfloat16)
    return np.concatenate([hi, lo])


def lane_of(shape):
    return lax.broadcasted_iota(jnp.int32, shape, len(shape) - 1)


def row_of(shape):
    return lax.broadcasted_iota(jnp.int32, shape, 0)


def halves(first, second):
    low = lane_of(first.shape) < 64
    return (
        jnp.where(low, first, pltpu.roll(second, 64, 1)),
        jnp.where(low, pltpu.roll(first, 64, 1), second),
    )


def across(u):
    return u if u < 4 else u + 8


def within(u):
    return u + 4


def quarter_of(u, h):
    return 3 * h if u % 2 == 0 else 1 + h


def window_matrix():
    wide = (1, SEC * COMP)
    lane = lane_of(wide)
    t = ((lane % SEC).astype(jnp.float32) - 0.5 * (SEC - 1)) * (2.0 / (SEC - 1))
    basis = [jnp.ones(wide, jnp.float32), t]
    for _ in range(RANK - 2):
        basis.append(2.0 * t * basis[-1] - basis[-2])
    rows = [
        jnp.where(lane // SEC == comp, values, 0.0) for comp in range(COMP) for values in basis
    ]
    sub = row_of((8, SEC * COMP))
    parts = []
    for places in (
        range(18),
        range(2, 20),
        [8 * b + (i + 4) % 8 for b in range(4) for i in range(5 - b % 2)],
    ):
        tiles = {}
        for place, row in zip(places, rows):
            tile = tiles.get(place // 8, jnp.zeros((8, SEC * COMP), jnp.float32))
            tiles[place // 8] = jnp.where(sub == place % 8, row, tile)
        rest = jnp.concatenate([tiles[i] for i in sorted(tiles)])
        for _ in range(3):
            part = rest.astype(jnp.bfloat16).astype(jnp.float32)
            parts.append(part)
            rest = rest - part
    return jnp.concatenate(parts).astype(jnp.bfloat16)


TAIL = 8
ORDER = ((TAIL, 0), (1, 2, 3, 4), (5, 6, 7))


def project_kernel(strain_hbm, send_ref, energy_ref, buf, a_ref, sem):
    copies = {}
    for group in ORDER:
        for u in group:
            copies[u] = pltpu.make_async_copy(
                strain_hbm.at[:, pl.ds(4 * u, 4)], buf.at[u], sem.at[u]
            )
            copies[u].start(priority=1)
    rows = buf.reshape(LAY // 4, SEC * 4 * COMP, LANES)
    send = send_ref.reshape(CIRC, ROWS, LANES)
    parity = lax.axis_index("sect") % 2
    tops = {}
    sums = {}
    tails = {}
    sub = row_of((8, LANES))
    block = lane_of((8, LANES)) // 32

    def pair(t):
        kind = 2 if t >= 16 else t % 2
        size = 32 if kind == 2 else 24
        base = 72 * kind
        first = 4 * (t % 2)
        x = [
            [rows[t // 2, pl.ds(first + COMP * i + c, SEC, stride=4 * COMP), :] for i in range(2)]
            for c in range(COMP)
        ]
        wide = jnp.concatenate([jnp.concatenate(both, axis=1) for both in x])
        d = jnp.dot(a_ref[base : base + 3 * size], wide, preferred_element_type=jnp.float32)
        d = d[:size] + d[size : 2 * size] + d[2 * size :]
        for i in range(2):
            l = 2 * t + i
            c0 = x[0][i].astype(jnp.float32)
            c1 = x[1][i].astype(jnp.float32)
            e = c0 * c0 + c1 * c1
            energy_ref[l] = e
            tops[l] = jnp.max(e, axis=0, keepdims=True)
            sums[l] = d[:, LANES * i : LANES * (i + 1)]

    def pack_tail():
        for v in range(4):
            x = sums[32 + v]
            shifted = []
            for delta in range(4):
                w = jnp.zeros((8, LANES), jnp.float32)
                for b in range(4):
                    w = jnp.where(block == (b - delta) % 4, x[8 * b : 8 * b + 8], w)
                shifted.append(pltpu.roll(w, 32 * delta, 1) if delta else w)
            for g in range(4):
                y = shifted[0]
                for b in range(4):
                    y = jnp.where(block == b, shifted[(b - g) % 4], y)
                top = tops[32 + v]
                if g:
                    top = pltpu.roll(top, LANES - 32 * g, 1)
                tails[v, g] = jnp.where(sub == 3, top, y)

    def pack(u):
        first = halves(sums[4 * u], sums[4 * u + 1])
        second = halves(sums[4 * u + 2], sums[4 * u + 3])
        top0 = halves(tops[4 * u], tops[4 * u + 1])
        top1 = halves(tops[4 * u + 2], tops[4 * u + 3])
        for h in range(2):
            c = across(u) + (within(u) - across(u)) * ((h + parity) % 2)
            tail = tails[u // 2, quarter_of(u, h)]
            send[c, 0:16] = first[h][0:16]
            send[c, 16:24] = first[h][16:24] + second[h][0:8]
            send[c, 24:32] = second[h][8:16]
            send[c, 32:40] = jnp.where(sub < 4, second[h][16:24], tail)
            tile = jnp.where(sub == 1, top0[h], tail)
            send[c, 40:44] = jnp.where(sub == 2, top1[h], tile)[0:4]

    a_ref[...] = window_matrix()
    waiting = []
    for group in ORDER:
        for u in group:
            copies[u].wait()
        for u in group:
            pair(2 * u)
            pair(2 * u + 1)
        for u in waiting:
            pack_tail() if u == TAIL else pack(u)
        waiting = group
    for u in waiting:
        pack_tail() if u == TAIL else pack(u)


def project(strain):
    return pl.pallas_call(
        project_kernel,
        name="project",
        out_shape=[
            jax.ShapeDtypeStruct((CIRC, ROWS // QUAD, QUAD, LANES), jnp.float32),
            jax.ShapeDtypeStruct((LAY, SEC, LANES), jnp.float32),
        ],
        in_specs=[pl.BlockSpec(memory_space=pl.ANY)],
        out_specs=[pl.BlockSpec(memory_space=pltpu.VMEM)] * 2,
        scratch_shapes=[
            pltpu.VMEM((LAY // 4, SEC, 4, COMP, LANES), jnp.bfloat16),
            pltpu.VMEM((240, SEC * COMP), jnp.bfloat16),
            pltpu.SemaphoreType.DMA((LAY // 4,)),
        ],
        compiler_params=pltpu.CompilerParams(vmem_limit_bytes=50 * 2**20),
    )(strain)


def owner_kernel(
    recv_ref, w_ref, region_ref, prior_ref, temp_ref, cond_ref, loss_ref, mullins_ref, own_ref, msg_ref
):
    c = lax.axis_index("circ")
    u = c % 4 + 4 * (c // 8)
    h = (lax.axis_index("sect") + (c // 4 + 1) // 2) % 2
    is_left = h == 0
    lane = lane_of((1, LANES))
    sub = row_of((8, LANES))
    recv = recv_ref.reshape(CIRC * ROWS, LANES)
    p = jnp.concatenate([recv[...], jnp.zeros((PADDED - CIRC * ROWS, LANES), jnp.float32)])
    hi = p.astype(jnp.bfloat16)
    lo = (p - hi.astype(jnp.float32)).astype(jnp.bfloat16)
    o = jnp.dot(
        w_ref[...], jnp.concatenate([hi, lo], axis=1), preferred_element_type=jnp.float32
    )
    coeffs = o[:128, :LANES] + o[128:, :LANES] + o[:128, LANES:]
    squared = coeffs[:64] * coeffs[:64]
    powers = [
        squared[32 * a : 32 * a + 8]
        + squared[32 * a + 8 : 32 * a + 16]
        + squared[32 * a + 16 : 32 * a + 24]
        + squared[32 * a + 24 : 32 * a + 32]
        for a in range(2)
    ]
    last = [coeffs[64 + 16 * b : 80 + 16 * b] for b in range(4)]
    comp0 = last[0] + pltpu.roll(last[1], 96, 1)
    comp1 = pltpu.roll(last[2], 64, 1) + pltpu.roll(last[3], 32, 1)
    comp0, comp1 = comp0 * comp0, comp1 * comp1
    powers.append(comp0[:8] + comp0[8:] + comp1[:8] + comp1[8:])

    quarter = jnp.where(u % 2 == 0, 3 * h, 1 + h)
    back = (LANES - 32 * quarter) % LANES

    low = lane_of((4, LANES)) < 64

    def stacked(vectors):
        out = jnp.where(sub == 0, vectors[0], vectors[1])
        return jnp.where(sub == 2, vectors[2], out)

    def own_cells(ref):
        rows = ref[pl.ds(4 * u, 4), :]
        last = ref[pl.ds(32 + u // 2, 1), :]
        turned = pltpu.roll(rows, 64, 1)
        evens = jnp.where(is_left, rows, turned)
        odds = jnp.where(is_left, turned, rows)
        odds = pltpu.roll(jnp.concatenate([odds, odds]), 7, 0)[0:4]
        mixed = jnp.where(low, evens, odds)
        return stacked([mixed[0:1], mixed[2:3], pltpu.roll(last, back, 1)]), rows, last

    region, _, _ = own_cells(region_ref)
    prior, _, _ = own_cells(prior_ref)
    temp, temp_rows, temp_last = own_cells(temp_ref)
    cond_rows = cond_ref[pl.ds(4 * u, 4), :]
    cond_last = cond_ref[pl.ds(32 + u // 2, 1), :]
    picked = []
    for i in range(3):
        q = loss_ref[:, 0:1] * powers[i][0:1]
        for k in range(1, HARM):
            q = q + loss_ref[:, k : k + 1] * powers[i][k : k + 1]
        picked.append(
            jnp.sum(jnp.where(region[i : i + 1] == sub, q, 0.0), axis=0, keepdims=True)
        )
    share = jnp.zeros((8, LANES), jnp.float32)
    for r in range(NREG):
        share = jnp.where(region == r, mullins_ref[0:1, r : r + 1], share)
    top = stacked(
        [
            jnp.max(recv[pl.ds(41 + i, CIRC, stride=ROWS), :], axis=0, keepdims=True)
            for i in range(3)
        ]
    )
    peak = jnp.maximum(prior, top)
    heat = jnp.exp(-0.5 * temp) * stacked(picked) + share * (peak - prior)
    heats = [heat[i : i + 1] for i in range(3)]
    peaks = [peak[i : i + 1] for i in range(3)]

    third = (lane >= 32) & (lane < 64)
    own = jnp.where(sub == 0, heats[0], 0.0)
    own = jnp.where(sub == 1, heats[1], own)
    own = jnp.where(sub == 2, peaks[0], own)
    own = jnp.where(sub == 3, peaks[1], own)
    own = jnp.where((sub == 4) & third, pltpu.roll(heats[2], 32, 1), own)
    own_ref[...] = jnp.where((sub == 5) & third, pltpu.roll(peaks[2], 32, 1), own)

    edge = jnp.where(is_left, lane, LANES - 1 - lane) < EDGE
    step = jnp.where(is_left, EDGE, LANES - EDGE)

    def message(heat_rows, cond_part, temp_part):
        row = jnp.where(edge, heat_rows, 0.0)
        row = row + pltpu.roll(jnp.where(edge, cond_part, 0.0), step, 1)
        return row + pltpu.roll(jnp.where(edge, temp_part, 0.0), (2 * step) % LANES, 1)

    turned = pltpu.roll(heat, 64, 1)
    evens = jnp.where(is_left, heat, turned)
    odds = jnp.where(is_left, turned, heat)
    four = jnp.concatenate([evens[0:1], odds[0:1], evens[1:2], odds[1:2]])
    main = message(four, cond_rows, temp_rows)
    final = jnp.where(is_left, heats[2], pltpu.roll(heats[2], 96, 1))
    final = pltpu.roll(message(final, cond_last, temp_last), jnp.where(is_left, 32, 96), 1)
    msg = jnp.concatenate([jnp.zeros((4, LANES), jnp.float32), main])
    msg = msg + jnp.where(sub == 6, final, 0.0)
    msg_ref[...] = msg


def owner(recv, w, region, prior, temp, cond, loss, mullins):
    vmem = pl.BlockSpec(memory_space=pltpu.VMEM)
    return pl.pallas_call(
        owner_kernel,
        name="owner",
        out_shape=[jax.ShapeDtypeStruct((8, LANES), jnp.float32)] * 2,
        in_specs=[vmem] * 8,
        out_specs=[vmem] * 2,
        compiler_params=pltpu.CompilerParams(vmem_limit_bytes=32 * 2**20),
    )(recv, w, region, prior, temp, cond, loss, mullins)


GROUPS = 6
EARLY = 12


def modulus_kernel(
    all_ref, energy_ref, region_ref, temp_ref, cond_ref, stiff_ref,
    field_hbm, peak_hbm, out_hbm,
    heat_s, peak_s, halo_s, cond_s, temp_s, region_s, field_s, soft_s, out_s, sem,
):
    low = lane_of((8, LANES)) < 64
    lane = lane_of((FIELD_ROWS, LANES))
    even = lax.axis_index("sect") % 2 == 0

    def sides(k):
        far = jnp.concatenate(
            [all_ref[pl.ds(k, 4, stride=8), :], all_ref[pl.ds(96 + k, 4, stride=8), :]]
        )
        near = all_ref[pl.ds(32 + k, 8, stride=8), :]
        return jnp.where(even, far, near), jnp.where(even, near, far)

    def tail_sides(k, odd):
        k = k + 8 * odd
        far = jnp.concatenate(
            [all_ref[pl.ds(k, 2, stride=16), :], all_ref[pl.ds(96 + k, 2, stride=16), :]]
        )
        near = all_ref[pl.ds(32 + k, 4, stride=16), :]
        return jnp.where(even, far, near), jnp.where(even, near, far)

    for scratch in (heat_s, peak_s, halo_s, cond_s, temp_s):
        scratch[32:FIELD_ROWS] = jnp.zeros((8, LANES), jnp.float32)
    region_s[32:FIELD_ROWS] = jnp.zeros((8, LANES), jnp.int32)
    cond_s[0:LAY] = cond_ref[...]
    temp_s[0:LAY] = temp_ref[...]
    region_s[0:LAY] = region_ref[...]
    for a in range(2):
        for base, target in ((0, heat_s), (2, peak_s)):
            left, right = sides(base + a)
            target[pl.ds(2 * a, 8, stride=4), :] = jnp.where(low, left, pltpu.roll(right, 64, 1))
            target[pl.ds(2 * a + 1, 8, stride=4), :] = jnp.where(low, pltpu.roll(left, 64, 1), right)
    small = lane_of((4, LANES))
    for base, target in ((4, heat_s), (5, peak_s)):
        row = jnp.zeros((4, LANES), jnp.float32)
        parts = [tail_sides(base, odd) for odd in range(2)]
        for odd, h, g in ((0, 0, 0), (1, 0, 1), (1, 1, 2), (0, 1, 3)):
            part = parts[odd][h]
            if g != 1:
                part = pltpu.roll(part, (32 * g - 32) % LANES, 1)
            row = jnp.where(small // 32 == g, part, row)
        target[32:LAY] = row
    wide = lane_of((8, LANES))
    outer = (wide < 3 * EDGE) | (wide >= LANES - 3 * EDGE)
    for j in range(4):
        left, right = sides(4 + j)
        halo_s[pl.ds(j, 8, stride=4), :] = jnp.where(outer, left + right, 0.0)
    from_left, from_right = tail_sides(6, 0)
    from_left = pltpu.roll(from_left, 32, 1)
    from_right = pltpu.roll(from_right, 96, 1)
    halo_s[32:LAY] = jnp.where(
        small >= LANES - 3 * EDGE, from_left, jnp.where(small < 3 * EDGE, from_right, 0.0)
    )

    peak = peak_s[...]
    halo = halo_s[...]

    def unpack(n):
        low_part = pltpu.roll(halo, (LANES - EDGE * n) % LANES, 1) if n else halo
        high_part = pltpu.roll(halo, EDGE * n, 1) if n else halo
        return jnp.where(
            lane < EDGE, low_part, jnp.where(lane >= LANES - EDGE, high_part, 0.0)
        )

    heat = (heat_s[...], unpack(0))
    cond = (cond_s[...], unpack(1))
    field = (temp_s[...], unpack(2))
    scale = [1.0 / (4.0 * k + SINK) for k in cond]
    heat = [x * y for x, y in zip(heat, scale)]
    cond = [x * y for x, y in zip(cond, scale)]
    rows = row_of((FIELD_ROWS, LANES))
    valid = rows < LAY
    first, final = lane == 0, lane == LANES - 1
    for _ in range(SWEEPS):
        right = [pltpu.roll(x, 1, 1) for x in field]
        left = [pltpu.roll(x, LANES - 1, 1) for x in field]
        new = []
        for i in range(2):
            beside = jnp.where(first, right[1 - i], right[i]) + jnp.where(final, left[1 - i], left[i])
            beside = beside + pltpu.roll(field[i], 1, 0) + pltpu.roll(field[i], FIELD_ROWS - 1, 0)
            new.append(jnp.where(valid, heat[i] + cond[i] * beside, 0.0))
        field = new
    for l in range(EARLY):
        soft_s[l] = 1.0 - 0.5 * jnp.tanh((peak[l : l + 1] - energy_ref[l]) * 0.25)
    field_s[...] = field[0]
    copies = [
        pltpu.make_async_copy(field_s.at[0:LAY], field_hbm, sem.at[0]),
        pltpu.make_async_copy(peak_s.at[0:LAY], peak_hbm, sem.at[1]),
    ]
    for copy in copies:
        copy.start()
    region = region_s[...]
    stiff = jnp.zeros((FIELD_ROWS, LANES), jnp.float32)
    for r in range(NREG):
        stiff = jnp.where(region == r, stiff_ref[0:1, r : r + 1], stiff)
    factor = stiff * jnp.exp(-0.5 * field[0])
    size = LAY // GROUPS
    for group in range(GROUPS):
        for l in range(group * size, (group + 1) * size):
            if l < EARLY:
                soft = soft_s[l]
            else:
                soft = 1.0 - 0.5 * jnp.tanh((peak[l : l + 1] - energy_ref[l]) * 0.25)
            out_s[l] = (factor[l : l + 1] * soft).astype(jnp.bfloat16)
        where = pl.ds(group * size, size)
        copy = pltpu.make_async_copy(out_s.at[where], out_hbm.at[where], sem.at[2 + group])
        copy.start()
        copies.append(copy)
    for copy in copies:
        copy.wait()


def soften(everything, energy, region, temp, cond, stiff):
    vmem = pl.BlockSpec(memory_space=pltpu.VMEM)
    plane = pltpu.VMEM((FIELD_ROWS, LANES), jnp.float32)
    return pl.pallas_call(
        modulus_kernel,
        name="modulus",
        out_shape=[
            jax.ShapeDtypeStruct((LAY, LANES), jnp.float32),
            jax.ShapeDtypeStruct((LAY, LANES), jnp.float32),
            jax.ShapeDtypeStruct((LAY, SEC, LANES), jnp.bfloat16),
        ],
        in_specs=[vmem] * 6,
        out_specs=[pl.BlockSpec(memory_space=pl.ANY)] * 3,
        scratch_shapes=[
            plane, plane, plane, plane, plane,
            pltpu.VMEM((FIELD_ROWS, LANES), jnp.int32),
            plane,
            pltpu.VMEM((EARLY, SEC, LANES), jnp.float32),
            pltpu.VMEM((LAY, SEC, LANES), jnp.bfloat16),
            pltpu.SemaphoreType.DMA((2 + GROUPS,)),
        ],
        compiler_params=pltpu.CompilerParams(vmem_limit_bytes=32 * 2**20),
    )(everything, energy, region, temp, cond, stiff)


def per_device(sects, w, strain, region, prior, temp, cond, loss, mullins, stiff):
    send, energy = project(strain.transpose(0, 2, 1, 3))
    recv = lax.all_to_all(send, "circ", 0, 0, tiled=True)
    own, msg = owner(
        recv, w, region, prior, temp, cond, loss, mullins.reshape(1, NREG)
    )
    pairs = []
    for s in range(1, sects):
        for u in range(CIRC // 2):
            here = (within(u) if s % 2 else across(u)) * sects + s
            pairs += [(here, here - 1), (here - 1, here)]
    halo = lax.ppermute(msg, ("circ", "sect"), pairs)
    block = jnp.broadcast_to((own + halo)[None], (CIRC, 8, LANES))
    everything = lax.all_to_all(block, "circ", 0, 0, tiled=True)
    field, peak, modulus = soften(
        everything.reshape(CIRC * 8, LANES), energy, region, temp, cond, stiff.reshape(1, NREG)
    )
    return field, peak, modulus.transpose(1, 0, 2)


def solution(mesh):
    w = combine_matrix()
    maps = P(None, "sect")

    def whole(*args):
        return jax.shard_map(
            functools.partial(per_device, mesh.shape["sect"], jnp.asarray(w)),
            mesh=mesh,
            in_specs=(P("circ", None, None, "sect"), maps, maps, maps, maps, P(), P(), P()),
            out_specs=(maps, maps, P("circ", None, "sect")),
            check_vma=False,
        )(*args)

    return whole
```

```python
import functools
import math

import jax
import jax.numpy as jnp
import ml_dtypes
import numpy as np
from jax import lax
from jax.experimental import pallas as pl
from jax.experimental.pallas import tpu as pltpu
from jax.sharding import PartitionSpec as P

COMP = 2
HARM = 8
SWEEPS = 4
SINK = 0.1
SEC = 128
LAY = 36
LANES = 128
NREG = 8
CIRC = 16
NSEC = SEC * CIRC
RANK = 9
ROWS = 44
QUAD = 4
PADDED = 768
EDGE = 4
FIELD_ROWS = 40


def combine_matrix():
    half = 0.5 * (SEC - 1) * 2.0 * math.pi / NSEC
    nodes = 64
    n = (np.arange(nodes) + 0.5) * math.pi / nodes
    even = np.zeros((HARM, RANK))
    odd = np.zeros((HARM, RANK))
    for k in range(1, HARM + 1):
        for m in range(RANK):
            weight = (1.0 if m == 0 else 2.0) / nodes
            f = np.cos(k * half * np.cos(n)) if m % 2 == 0 else np.sin(k * half * np.cos(n))
            (even if m % 2 == 0 else odd)[k - 1, m] = weight * np.sum(f * np.cos(m * n))
    u = np.zeros((2 * HARM, CIRC, RANK))
    for d in range(CIRC):
        centre = 2.0 * math.pi * (SEC * d + 0.5 * (SEC - 1)) / NSEC
        for k in range(1, HARM + 1):
            c, s = math.cos(k * centre), math.sin(k * centre)
            u[k - 1, d] = c * even[k - 1] - s * odd[k - 1]
            u[HARM + k - 1, d] = s * even[k - 1] + c * odd[k - 1]
    u = u / math.sqrt(NSEC)
    w = np.zeros((128, CIRC, ROWS))
    for a in range(2):
        for comp in range(COMP):
            at = RANK * (COMP * a + comp)
            w[32 * a + 16 * comp : 32 * a + 16 * comp + 16, :, at : at + RANK] = u
    for b in range(4):
        part = u[:, :, 5 * (b % 2) : 5 * (b % 2) + 5]
        w[64 + 16 * b : 64 + 16 * b + 16, :, 36 : 36 + part.shape[2]] = part
    w = np.pad(w.reshape(128, CIRC * ROWS), ((0, 0), (0, PADDED - CIRC * ROWS)))
    hi = w.astype(ml_dtypes.bfloat16)
    lo = (w - hi.astype(np.float64)).astype(ml_dtypes.bfloat16)
    return np.concatenate([hi, lo])


def lane_of(shape):
    return lax.broadcasted_iota(jnp.int32, shape, len(shape) - 1)


def row_of(shape):
    return lax.broadcasted_iota(jnp.int32, shape, 0)


def halves(first, second):
    low = lane_of(first.shape) < 64
    return (
        jnp.where(low, first, pltpu.roll(second, 64, 1)),
        jnp.where(low, pltpu.roll(first, 64, 1), second),
    )


def across(u):
    return u if u < 4 else u + 8


def within(u):
    return u + 4


def quarter_of(u, h):
    return 3 * h if u % 2 == 0 else 1 + h


def window_matrix():
    wide = (1, SEC * COMP)
    lane = lane_of(wide)
    t = ((lane % SEC).astype(jnp.float32) - 0.5 * (SEC - 1)) * (2.0 / (SEC - 1))
    basis = [jnp.ones(wide, jnp.float32), t]
    for _ in range(RANK - 2):
        basis.append(2.0 * t * basis[-1] - basis[-2])
    rows = [
        jnp.where(lane // SEC == comp, values, 0.0) for comp in range(COMP) for values in basis
    ]
    sub = row_of((8, SEC * COMP))
    parts = []
    for places in (
        range(18),
        range(2, 20),
        [8 * b + (i + 4) % 8 for b in range(4) for i in range(5 - b % 2)],
    ):
        tiles = {}
        for place, row in zip(places, rows):
            tile = tiles.get(place // 8, jnp.zeros((8, SEC * COMP), jnp.float32))
            tiles[place // 8] = jnp.where(sub == place % 8, row, tile)
        rest = jnp.concatenate([tiles[i] for i in sorted(tiles)])
        for _ in range(3):
            part = rest.astype(jnp.bfloat16).astype(jnp.float32)
            parts.append(part)
            rest = rest - part
    return jnp.concatenate(parts).astype(jnp.bfloat16)


TAIL = 8
ORDER = ((TAIL, 0), (1, 2, 3, 4), (5, 6, 7))


def project_kernel(strain_hbm, send_ref, energy_ref, buf, a_ref, sem):
    copies = {}
    for group in ORDER:
        for u in group:
            copies[u] = pltpu.make_async_copy(
                strain_hbm.at[:, pl.ds(4 * u, 4)], buf.at[u], sem.at[u]
            )
            copies[u].start()
    rows = buf.reshape(LAY // 4, SEC * 4 * COMP, LANES)
    send = send_ref.reshape(CIRC, ROWS, LANES)
    parity = lax.axis_index("sect") % 2
    tops = {}
    sums = {}
    tails = {}
    sub = row_of((8, LANES))
    block = lane_of((8, LANES)) // 32

    def pair(t):
        kind = 2 if t >= 16 else t % 2
        size = 32 if kind == 2 else 24
        base = 72 * kind
        first = 4 * (t % 2)
        x = [
            [rows[t // 2, pl.ds(first + COMP * i + c, SEC, stride=4 * COMP), :] for i in range(2)]
            for c in range(COMP)
        ]
        wide = jnp.concatenate([jnp.concatenate(both, axis=1) for both in x])
        d = jnp.dot(a_ref[base : base + 3 * size], wide, preferred_element_type=jnp.float32)
        d = d[:size] + d[size : 2 * size] + d[2 * size :]
        for i in range(2):
            l = 2 * t + i
            c0 = x[0][i].astype(jnp.float32)
            c1 = x[1][i].astype(jnp.float32)
            e = c0 * c0 + c1 * c1
            energy_ref[l] = e
            tops[l] = jnp.max(e, axis=0, keepdims=True)
            sums[l] = d[:, LANES * i : LANES * (i + 1)]

    def pack_tail():
        for v in range(4):
            x = sums[32 + v]
            shifted = []
            for delta in range(4):
                w = jnp.zeros((8, LANES), jnp.float32)
                for b in range(4):
                    w = jnp.where(block == (b - delta) % 4, x[8 * b : 8 * b + 8], w)
                shifted.append(pltpu.roll(w, 32 * delta, 1) if delta else w)
            for g in range(4):
                y = shifted[0]
                for b in range(4):
                    y = jnp.where(block == b, shifted[(b - g) % 4], y)
                top = tops[32 + v]
                if g:
                    top = pltpu.roll(top, LANES - 32 * g, 1)
                tails[v, g] = jnp.where(sub == 3, top, y)

    def pack(u):
        first = halves(sums[4 * u], sums[4 * u + 1])
        second = halves(sums[4 * u + 2], sums[4 * u + 3])
        top0 = halves(tops[4 * u], tops[4 * u + 1])
        top1 = halves(tops[4 * u + 2], tops[4 * u + 3])
        for h in range(2):
            c = across(u) + (within(u) - across(u)) * ((h + parity) % 2)
            tail = tails[u // 2, quarter_of(u, h)]
            send[c, 0:16] = first[h][0:16]
            send[c, 16:24] = first[h][16:24] + second[h][0:8]
            send[c, 24:32] = second[h][8:16]
            send[c, 32:40] = jnp.where(sub < 4, second[h][16:24], tail)
            tile = jnp.where(sub == 1, top0[h], tail)
            send[c, 40:44] = jnp.where(sub == 2, top1[h], tile)[0:4]

    a_ref[...] = window_matrix()
    waiting = []
    for group in ORDER:
        for u in group:
            copies[u].wait()
        for u in group:
            pair(2 * u)
            pair(2 * u + 1)
        for u in waiting:
            pack_tail() if u == TAIL else pack(u)
        waiting = group
    for u in waiting:
        pack_tail() if u == TAIL else pack(u)


def project(strain):
    return pl.pallas_call(
        project_kernel,
        name="project",
        out_shape=[
            jax.ShapeDtypeStruct((CIRC, ROWS // QUAD, QUAD, LANES), jnp.float32),
            jax.ShapeDtypeStruct((LAY, SEC, LANES), jnp.float32),
        ],
        in_specs=[pl.BlockSpec(memory_space=pl.ANY)],
        out_specs=[pl.BlockSpec(memory_space=pltpu.VMEM)] * 2,
        scratch_shapes=[
            pltpu.VMEM((LAY // 4, SEC, 4, COMP, LANES), jnp.bfloat16),
            pltpu.VMEM((240, SEC * COMP), jnp.bfloat16),
            pltpu.SemaphoreType.DMA((LAY // 4,)),
        ],
        compiler_params=pltpu.CompilerParams(vmem_limit_bytes=50 * 2**20),
    )(strain)


def owner_kernel(
    recv_ref, w_ref, region_ref, prior_ref, temp_ref, cond_ref, loss_ref, mullins_ref, own_ref, msg_ref
):
    c = lax.axis_index("circ")
    u = c % 4 + 4 * (c // 8)
    h = (lax.axis_index("sect") + (c // 4 + 1) // 2) % 2
    is_left = h == 0
    lane = lane_of((1, LANES))
    sub = row_of((8, LANES))
    recv = recv_ref.reshape(CIRC * ROWS, LANES)
    p = jnp.concatenate([recv[...], jnp.zeros((PADDED - CIRC * ROWS, LANES), jnp.float32)])
    hi = p.astype(jnp.bfloat16)
    lo = (p - hi.astype(jnp.float32)).astype(jnp.bfloat16)
    o = jnp.dot(
        w_ref[...], jnp.concatenate([hi, lo], axis=1), preferred_element_type=jnp.float32
    )
    coeffs = o[:128, :LANES] + o[128:, :LANES] + o[:128, LANES:]
    squared = coeffs[:64] * coeffs[:64]
    powers = [
        squared[32 * a : 32 * a + 8]
        + squared[32 * a + 8 : 32 * a + 16]
        + squared[32 * a + 16 : 32 * a + 24]
        + squared[32 * a + 24 : 32 * a + 32]
        for a in range(2)
    ]
    last = [coeffs[64 + 16 * b : 80 + 16 * b] for b in range(4)]
    comp0 = last[0] + pltpu.roll(last[1], 96, 1)
    comp1 = pltpu.roll(last[2], 64, 1) + pltpu.roll(last[3], 32, 1)
    comp0, comp1 = comp0 * comp0, comp1 * comp1
    powers.append(comp0[:8] + comp0[8:] + comp1[:8] + comp1[8:])

    quarter = jnp.where(u % 2 == 0, 3 * h, 1 + h)
    back = (LANES - 32 * quarter) % LANES

    low = lane_of((4, LANES)) < 64

    def stacked(vectors):
        out = jnp.where(sub == 0, vectors[0], vectors[1])
        return jnp.where(sub == 2, vectors[2], out)

    def own_cells(ref):
        rows = ref[pl.ds(4 * u, 4), :]
        last = ref[pl.ds(32 + u // 2, 1), :]
        turned = pltpu.roll(rows, 64, 1)
        evens = jnp.where(is_left, rows, turned)
        odds = jnp.where(is_left, turned, rows)
        odds = pltpu.roll(jnp.concatenate([odds, odds]), 7, 0)[0:4]
        mixed = jnp.where(low, evens, odds)
        return stacked([mixed[0:1], mixed[2:3], pltpu.roll(last, back, 1)]), rows, last

    region, _, _ = own_cells(region_ref)
    prior, _, _ = own_cells(prior_ref)
    temp, temp_rows, temp_last = own_cells(temp_ref)
    cond_rows = cond_ref[pl.ds(4 * u, 4), :]
    cond_last = cond_ref[pl.ds(32 + u // 2, 1), :]
    picked = []
    for i in range(3):
        q = loss_ref[:, 0:1] * powers[i][0:1]
        for k in range(1, HARM):
            q = q + loss_ref[:, k : k + 1] * powers[i][k : k + 1]
        picked.append(
            jnp.sum(jnp.where(region[i : i + 1] == sub, q, 0.0), axis=0, keepdims=True)
        )
    share = jnp.zeros((8, LANES), jnp.float32)
    for r in range(NREG):
        share = jnp.where(region == r, mullins_ref[0:1, r : r + 1], share)
    top = stacked(
        [
            jnp.max(recv[pl.ds(41 + i, CIRC, stride=ROWS), :], axis=0, keepdims=True)
            for i in range(3)
        ]
    )
    peak = jnp.maximum(prior, top)
    heat = jnp.exp(-0.5 * temp) * stacked(picked) + share * (peak - prior)
    heats = [heat[i : i + 1] for i in range(3)]
    peaks = [peak[i : i + 1] for i in range(3)]

    third = (lane >= 32) & (lane < 64)
    own = jnp.where(sub == 0, heats[0], 0.0)
    own = jnp.where(sub == 1, heats[1], own)
    own = jnp.where(sub == 2, peaks[0], own)
    own = jnp.where(sub == 3, peaks[1], own)
    own = jnp.where((sub == 4) & third, pltpu.roll(heats[2], 32, 1), own)
    own_ref[...] = jnp.where((sub == 5) & third, pltpu.roll(peaks[2], 32, 1), own)

    edge = jnp.where(is_left, lane, LANES - 1 - lane) < EDGE
    step = jnp.where(is_left, EDGE, LANES - EDGE)

    def message(heat_rows, cond_part, temp_part):
        row = jnp.where(edge, heat_rows, 0.0)
        row = row + pltpu.roll(jnp.where(edge, cond_part, 0.0), step, 1)
        return row + pltpu.roll(jnp.where(edge, temp_part, 0.0), (2 * step) % LANES, 1)

    turned = pltpu.roll(heat, 64, 1)
    evens = jnp.where(is_left, heat, turned)
    odds = jnp.where(is_left, turned, heat)
    four = jnp.concatenate([evens[0:1], odds[0:1], evens[1:2], odds[1:2]])
    main = message(four, cond_rows, temp_rows)
    final = jnp.where(is_left, heats[2], pltpu.roll(heats[2], 96, 1))
    final = pltpu.roll(message(final, cond_last, temp_last), jnp.where(is_left, 32, 96), 1)
    msg = jnp.concatenate([jnp.zeros((4, LANES), jnp.float32), main])
    msg = msg + jnp.where(sub == 6, final, 0.0)
    msg_ref[...] = msg


def owner(recv, w, region, prior, temp, cond, loss, mullins):
    vmem = pl.BlockSpec(memory_space=pltpu.VMEM)
    return pl.pallas_call(
        owner_kernel,
        name="owner",
        out_shape=[jax.ShapeDtypeStruct((8, LANES), jnp.float32)] * 2,
        in_specs=[vmem] * 8,
        out_specs=[vmem] * 2,
        compiler_params=pltpu.CompilerParams(vmem_limit_bytes=32 * 2**20),
    )(recv, w, region, prior, temp, cond, loss, mullins)


GROUPS = 6
EARLY = 24


def modulus_kernel(
    all_ref, energy_ref, region_ref, temp_ref, cond_ref, stiff_ref,
    field_hbm, peak_hbm, out_hbm,
    heat_s, peak_s, halo_s, cond_s, temp_s, region_s, field_s, soft_s, out_s, sem,
):
    low = lane_of((8, LANES)) < 64
    lane = lane_of((FIELD_ROWS, LANES))
    even = lax.axis_index("sect") % 2 == 0

    def sides(k):
        far = jnp.concatenate(
            [all_ref[pl.ds(k, 4, stride=8), :], all_ref[pl.ds(96 + k, 4, stride=8), :]]
        )
        near = all_ref[pl.ds(32 + k, 8, stride=8), :]
        return jnp.where(even, far, near), jnp.where(even, near, far)

    def tail_sides(k, odd):
        k = k + 8 * odd
        far = jnp.concatenate(
            [all_ref[pl.ds(k, 2, stride=16), :], all_ref[pl.ds(96 + k, 2, stride=16), :]]
        )
        near = all_ref[pl.ds(32 + k, 4, stride=16), :]
        return jnp.where(even, far, near), jnp.where(even, near, far)

    for scratch in (heat_s, peak_s, halo_s, cond_s, temp_s):
        scratch[32:FIELD_ROWS] = jnp.zeros((8, LANES), jnp.float32)
    region_s[32:FIELD_ROWS] = jnp.zeros((8, LANES), jnp.int32)
    cond_s[0:LAY] = cond_ref[...]
    temp_s[0:LAY] = temp_ref[...]
    region_s[0:LAY] = region_ref[...]
    for a in range(2):
        for base, target in ((0, heat_s), (2, peak_s)):
            left, right = sides(base + a)
            target[pl.ds(2 * a, 8, stride=4), :] = jnp.where(low, left, pltpu.roll(right, 64, 1))
            target[pl.ds(2 * a + 1, 8, stride=4), :] = jnp.where(low, pltpu.roll(left, 64, 1), right)
    small = lane_of((4, LANES))
    for base, target in ((4, heat_s), (5, peak_s)):
        row = jnp.zeros((4, LANES), jnp.float32)
        parts = [tail_sides(base, odd) for odd in range(2)]
        for odd, h, g in ((0, 0, 0), (1, 0, 1), (1, 1, 2), (0, 1, 3)):
            part = parts[odd][h]
            if g != 1:
                part = pltpu.roll(part, (32 * g - 32) % LANES, 1)
            row = jnp.where(small // 32 == g, part, row)
        target[32:LAY] = row
    wide = lane_of((8, LANES))
    outer = (wide < 3 * EDGE) | (wide >= LANES - 3 * EDGE)
    for j in range(4):
        left, right = sides(4 + j)
        halo_s[pl.ds(j, 8, stride=4), :] = jnp.where(outer, left + right, 0.0)
    from_left, from_right = tail_sides(6, 0)
    from_left = pltpu.roll(from_left, 32, 1)
    from_right = pltpu.roll(from_right, 96, 1)
    halo_s[32:LAY] = jnp.where(
        small >= LANES - 3 * EDGE, from_left, jnp.where(small < 3 * EDGE, from_right, 0.0)
    )

    peak = peak_s[...]
    halo = halo_s[...]

    def unpack(n):
        low_part = pltpu.roll(halo, (LANES - EDGE * n) % LANES, 1) if n else halo
        high_part = pltpu.roll(halo, EDGE * n, 1) if n else halo
        return jnp.where(
            lane < EDGE, low_part, jnp.where(lane >= LANES - EDGE, high_part, 0.0)
        )

    heat = (heat_s[...], unpack(0))
    cond = (cond_s[...], unpack(1))
    field = (temp_s[...], unpack(2))
    scale = [1.0 / (4.0 * k + SINK) for k in cond]
    heat = [x * y for x, y in zip(heat, scale)]
    cond = [x * y for x, y in zip(cond, scale)]
    rows = row_of((FIELD_ROWS, LANES))
    valid = rows < LAY
    first, final = lane == 0, lane == LANES - 1
    for _ in range(SWEEPS):
        right = [pltpu.roll(x, 1, 1) for x in field]
        left = [pltpu.roll(x, LANES - 1, 1) for x in field]
        new = []
        for i in range(2):
            beside = jnp.where(first, right[1 - i], right[i]) + jnp.where(final, left[1 - i], left[i])
            beside = beside + pltpu.roll(field[i], 1, 0) + pltpu.roll(field[i], FIELD_ROWS - 1, 0)
            new.append(jnp.where(valid, heat[i] + cond[i] * beside, 0.0))
        field = new
    for l in range(EARLY):
        soft_s[l] = 1.0 - 0.5 * jnp.tanh((peak[l : l + 1] - energy_ref[l]) * 0.25)
    field_s[...] = field[0]
    copies = [
        pltpu.make_async_copy(field_s.at[0:LAY], field_hbm, sem.at[0]),
        pltpu.make_async_copy(peak_s.at[0:LAY], peak_hbm, sem.at[1]),
    ]
    for copy in copies:
        copy.start()
    region = region_s[...]
    stiff = jnp.zeros((FIELD_ROWS, LANES), jnp.float32)
    for r in range(NREG):
        stiff = jnp.where(region == r, stiff_ref[0:1, r : r + 1], stiff)
    factor = stiff * jnp.exp(-0.5 * field[0])
    size = LAY // GROUPS
    for group in range(GROUPS):
        for l in range(group * size, (group + 1) * size):
            if l < EARLY:
                soft = soft_s[l]
            else:
                soft = 1.0 - 0.5 * jnp.tanh((peak[l : l + 1] - energy_ref[l]) * 0.25)
            out_s[l] = (factor[l : l + 1] * soft).astype(jnp.bfloat16)
        where = pl.ds(group * size, size)
        copy = pltpu.make_async_copy(out_s.at[where], out_hbm.at[where], sem.at[2 + group])
        copy.start()
        copies.append(copy)
    for copy in copies:
        copy.wait()


def soften(everything, energy, region, temp, cond, stiff):
    vmem = pl.BlockSpec(memory_space=pltpu.VMEM)
    plane = pltpu.VMEM((FIELD_ROWS, LANES), jnp.float32)
    return pl.pallas_call(
        modulus_kernel,
        name="modulus",
        out_shape=[
            jax.ShapeDtypeStruct((LAY, LANES), jnp.float32),
            jax.ShapeDtypeStruct((LAY, LANES), jnp.float32),
            jax.ShapeDtypeStruct((LAY, SEC, LANES), jnp.bfloat16),
        ],
        in_specs=[vmem] * 6,
        out_specs=[pl.BlockSpec(memory_space=pl.ANY)] * 3,
        scratch_shapes=[
            plane, plane, plane, plane, plane,
            pltpu.VMEM((FIELD_ROWS, LANES), jnp.int32),
            plane,
            pltpu.VMEM((EARLY, SEC, LANES), jnp.float32),
            pltpu.VMEM((LAY, SEC, LANES), jnp.bfloat16),
            pltpu.SemaphoreType.DMA((2 + GROUPS,)),
        ],
        compiler_params=pltpu.CompilerParams(vmem_limit_bytes=32 * 2**20),
    )(everything, energy, region, temp, cond, stiff)


def per_device(sects, w, strain, region, prior, temp, cond, loss, mullins, stiff):
    send, energy = project(strain.transpose(0, 2, 1, 3))
    recv = lax.all_to_all(send, "circ", 0, 0, tiled=True)
    own, msg = owner(
        recv, w, region, prior, temp, cond, loss, mullins.reshape(1, NREG)
    )
    pairs = []
    for s in range(1, sects):
        for u in range(CIRC // 2):
            here = (within(u) if s % 2 else across(u)) * sects + s
            pairs += [(here, here - 1), (here - 1, here)]
    halo = lax.ppermute(msg, ("circ", "sect"), pairs)
    block = jnp.broadcast_to((own + halo)[None], (CIRC, 8, LANES))
    everything = lax.all_to_all(block, "circ", 0, 0, tiled=True)
    field, peak, modulus = soften(
        everything.reshape(CIRC * 8, LANES), energy, region, temp, cond, stiff.reshape(1, NREG)
    )
    return field, peak, modulus.transpose(1, 0, 2)


def solution(mesh):
    w = combine_matrix()
    maps = P(None, "sect")

    def whole(*args):
        return jax.shard_map(
            functools.partial(per_device, mesh.shape["sect"], jnp.asarray(w)),
            mesh=mesh,
            in_specs=(P("circ", None, None, "sect"), maps, maps, maps, maps, P(), P(), P()),
            out_specs=(maps, maps, P("circ", None, "sect")),
            check_vma=False,
        )(*args)

    return whole
```
